128 devices in a mesh: narrow: 2 (over z_hi), wide: 64 (over z_lo, x, y, core).
Axes of the slice: x: 4, y: 4, z: 4 (z_hi: 2, z_lo: 2; z = z_hi * 2 + z_lo), core: 2. Of those that a mesh axis runs over, the one named last changes fastest.
Arguments:
- inputs: bfloat16 [32768, 768], P('wide', 'narrow'), may hold values from -6 to 6
- block_ids: int32 [32768], replicated, may hold values from 0 to 255, never falling along the last dimension, each value on 1 to 256 neighbouring positions
- expert_ids: int32 [32768, 2], P('wide'), may hold values from 0 to 11, all different within a row; in each aligned block of 512 rows (0 to 511, 512 to 1023, ...) at most 128 rows name the same one
- prev_scores: float32 [32768, 12], P('wide'), may hold values from -6 to 6
- gain_one: bfloat16 [768], P('narrow'), may hold values from 0.5 to 1.5
- w_qkv: bfloat16 [768, 2304], P('narrow', 'wide'), may hold values from -0.21875 to 0.21875
- w_out: bfloat16 [768, 768], P('wide', 'narrow'), may hold values from -6 to 6
- gain_two: bfloat16 [768], P('narrow'), may hold values from 0.5 to 1.5
- w_router: bfloat16 [768, 12], P('narrow'), may hold values from -0.15625 to 0.15625
- w_residual: bfloat16 [12, 12], replicated, may hold values from -0.875 to 0.875
- w_const: bfloat16 [768, 4], P('narrow'), may hold values from -0.21875 to 0.21875
- const_vec: bfloat16 [2, 768], P(None, 'narrow'), may hold values from -6 to 6
- w_gate: bfloat16 [768, 16384], P('narrow', 'wide'), may hold values from -0.21875 to 0.21875
- w_up: bfloat16 [768, 16384], P('narrow', 'wide'), may hold values from -0.21875 to 0.21875
- w_down: bfloat16 [16384, 768], P('wide', 'narrow'), may hold values from -0.25 to 0.25
- cotangent: bfloat16 [32768, 768], P('wide', 'narrow'), may hold values from -6 to 6
Outputs:
- layer_out: bfloat16 [32768, 768], P('wide', 'narrow')
- grad_inputs: float32 [32768, 768], P('wide', 'narrow')
- grad_prev: float32 [32768, 12], P('wide')
- grad_gain_one: float32 [768], P('narrow')
- grad_w_qkv: float32 [768, 2304], P('narrow', 'wide')
- grad_w_out: float32 [768, 768], P('wide', 'narrow')
- grad_gain_two: float32 [768], P('narrow')
- grad_w_router: float32 [768, 12], P('narrow')
- grad_w_residual: float32 [12, 12], replicated
- grad_w_const: float32 [768, 4], P('narrow')
- grad_const_vec: float32 [2, 768], P(None, 'narrow')
- grad_w_gate: float32 [768, 16384], P('narrow', 'wide')
- grad_w_up: float32 [768, 16384], P('narrow', 'wide')
- grad_w_down: float32 [16384, 768], P('wide', 'narrow')
The draws below stay inside these ranges and needn't reach their ends.
Inputs may be any that keep to these rules, and one draw needn't show every extreme that they name: `expert_ids`: each row names two different experts: 0 to 7 are feed-forward experts, 8 the zero expert, 9 the copy expert, 10 and 11 the constant experts. In each aligned block of 512 rows no expert is named by more than 128 rows, a bound that some block reaches. `block_ids`: never falling along the tokens; each id covers 1 to 256 consecutive tokens, one exactly 256.
All inputs are finite; a program needn't handle non-finite values.
Results may differ from the reference program's by a relative error of at most 0.035.
Values may be sent and summed in bfloat16 or wider, within the bound.
A program may use at most 192 MiB of HBM per device.

```python
import math
import jax
import jax.numpy as jnp
import numpy as np
from jax import lax

D = 768
HEADS = 12
HEAD_DIM = 64
FF = 2048
EXPERTS = 8
ROUTES = 12
TOK_DEV = 512
SEQ = 4096
BLOCK = 256
CAP = 128
TOKENS = 32768
N_WIDE = 64


def steps_of(own_key, shape, pieces, low, largest):
    gain, own = 1.0, jax.random.fold_in(own_key, 6)
    for dim, shards_of in pieces:
        heights = jnp.exp(jax.random.uniform(jax.random.fold_in(own, dim), (shards_of,), jnp.float32, low / len(pieces), largest / len(pieces)))
        gain = gain * jnp.repeat(heights, shape[dim] // shards_of).reshape([-1 if axis == dim else 1 for axis in range(len(shape))])
    return gain


def split_up(number_of, total, reach, lean):
    portions = [(1 << 20) // math.isqrt(rank ** lean) + 1 for rank in range(2, number_of + 1)]
    spare, holding = total - reach - (number_of - 1), [1] * (number_of - 1)
    while spare > 0:
        free = [i for i in range(number_of - 1) if holding[i] < reach]
        pool, remaining = sum([portions[i] for i in free]), spare
        for i in free:
            extra = min(reach - holding[i], max(1, remaining * portions[i] // pool), spare)
            holding[i] = holding[i] + extra
            spare = spare - extra
    return np.array([reach] + holding)


def uneven_parts(key, count, total, bound, lean):
    if count == 2:
        one = jax.random.randint(key, (), max(1, total - bound), min(bound, total - 1) + 1)
        return jnp.stack([one, total - one])
    sizes = jnp.asarray(split_up(count, total, bound, lean), jnp.int32)
    twos = (count - 1) // 2
    source_of, taker = sizes[1:1 + 2 * twos:2], sizes[2:2 + 2 * twos:2]
    margin = jnp.minimum(source_of - 1, bound - taker)
    moved = jax.random.randint(jax.random.fold_in(key, 1), (twos,), 0, 1 << 20) % (margin + 1)
    sizes = sizes.at[1:1 + 2 * twos:2].set(source_of - moved).at[2:2 + 2 * twos:2].set(taker + moved)
    return sizes[jax.random.permutation(jax.random.fold_in(key, 2), count)]


def deal_out(rng, own, number, rows, number_of, top, bound, lean):
    order = jax.random.permutation(rng, number_of)
    crowded, ordinary = shares(number_of, rows * top, bound, lean, True), shares(number_of, rows * top, bound, lean, False)
    places = jnp.arange(number_of)

    def named(sizes, offset_by):
        used = int((sizes > 0).sum())
        fixed = max(1, used // 4)
        moved = fixed + (places - fixed + offset_by * (used - fixed)) % max(1, number_of - fixed)
        return jnp.zeros((number_of,), jnp.int32).at[order[jnp.where(places < fixed, places, moved)]].set(jnp.asarray(sizes, jnp.int32))

    sizes = jnp.where(number % 4 == 0, named(crowded, number // 4), named(ordinary, number - number // 4 - 1))
    mixed = jax.random.permutation(jax.random.fold_in(own, 3), number_of)
    giver, sink = mixed[0:number_of // 2 * 2:2], mixed[1:number_of // 2 * 2:2]
    room = jnp.minimum(sizes[giver] - 1, bound - sizes[sink]) // 2
    room = jnp.where((giver == order[0]) | (sink == order[0]) | (sizes[sink] == 0), 0, jnp.maximum(room, 0))
    moved = jax.random.randint(jax.random.fold_in(own, 4), (number_of // 2,), 0, 1 << 20) % (room + 1)
    sizes = sizes.at[giver].add(-moved).at[sink].add(moved)
    items = jnp.searchsorted(jnp.cumsum(sizes), jnp.arange(rows * top), side="right").astype(jnp.int32)
    grid = items.reshape(top, rows).T
    grid = grid[jax.random.permutation(jax.random.fold_in(own, 1), rows)]
    offset_by = jax.random.randint(jax.random.fold_in(own, 2), (rows, 1), 0, top)
    return jnp.take_along_axis(grid, (jnp.arange(top)[None, :] + offset_by) % top, axis=1)


def shares(count, total, most, slope, full):
    portions = [(1 << 20) // math.isqrt(rank ** slope) + 1 for rank in range(1, count + 1)]
    largest = most if full else min(most, max(-(-total // count), total * portions[0] // sum(portions)))
    least = 1 if total - largest >= count - 1 else 0
    holding, rest = [largest] + [least] * (count - 1), total - largest - least * (count - 1)
    while rest > 0:
        candidates = [i for i in range(1, count) if holding[i] < largest] or [i for i in range(1, count) if holding[i] < most]
        whole, left = sum([portions[i] for i in candidates]), rest
        for i in candidates:
            more = min(most - holding[i], max(1, left * portions[i] // whole), rest)
            holding[i] = holding[i] + more
            rest = rest - more
    return np.array(holding)


def gaussian(key, shape, scale, most, pieces=(), kind=jnp.bfloat16):
    entries = scale * jax.random.normal(key, shape, jnp.float32)
    if pieces:
        entries = entries * steps_of(key, shape, pieces, -0.22, 0.18)
    return jnp.clip(entries, -most, most).astype(kind)


def setup_inputs(seed: int = 0) -> dict:
    streams_of = jax.random.split(jax.random.key(seed), 17)
    inputs = gaussian(streams_of[0], (TOKENS, D), 1.0, 6.0, ((0, 64), (1, 2)))
    block_ids = jnp.searchsorted(jnp.cumsum(uneven_parts(streams_of[1], 2 * TOKENS // BLOCK, TOKENS, BLOCK, 1)), jnp.arange(TOKENS), side="right").astype(jnp.int32)
    expert_ids_keys = jax.random.split(jax.random.fold_in(streams_of[2], 1), TOKENS // TOK_DEV)
    expert_ids_turns = jax.random.permutation(jax.random.fold_in(streams_of[2], 3), TOKENS // TOK_DEV)
    expert_ids = jax.vmap(lambda own, number: deal_out(jax.random.fold_in(streams_of[2], 2), own, number, TOK_DEV, ROUTES, 2, CAP, 1))(expert_ids_keys, expert_ids_turns).reshape((TOKENS, 2))
    prev_scores = gaussian(streams_of[3], (TOKENS, ROUTES), 1.0, 6.0, ((0, 64),), jnp.float32)
    gain_one = jnp.clip(1.0 + 0.1 * jax.random.normal(streams_of[4], (D,), jnp.float32), 0.5, 1.5).astype(jnp.bfloat16)
    w_qkv = gaussian(streams_of[5], (D, 3 * D), D ** -0.5, 0.21875, ((0, 2), (1, 64)))
    w_out = gaussian(streams_of[6], (D, D), 1 ** -0.5, 6.0, ((0, 64), (1, 2)))
    gain_two = jnp.clip(1.0 + 0.1 * jax.random.normal(streams_of[7], (D,), jnp.float32), 0.5, 1.5).astype(jnp.bfloat16)
    w_router = gaussian(streams_of[8], (D, ROUTES), (2 * D) ** -0.5, 0.15625, ((0, 2),))
    w_residual = gaussian(streams_of[9], (ROUTES, ROUTES), (4 * ROUTES) ** -0.5, 0.875)
    w_const = gaussian(streams_of[10], (D, 4), D ** -0.5, 0.21875, ((0, 2),))
    const_vec = gaussian(streams_of[11], (2, D), 1.0, 6.0, ((1, 2),))
    w_gate = gaussian(streams_of[12], (D, EXPERTS * FF), D ** -0.5, 0.21875, ((0, 2), (1, 64)))
    w_up = gaussian(streams_of[13], (D, EXPERTS * FF), D ** -0.5, 0.21875, ((0, 2), (1, 64)))
    w_down = gaussian(streams_of[14], (EXPERTS * FF, D), (FF // 4) ** -0.5, 0.25, ((0, 64), (1, 2)))
    cotangent = gaussian(streams_of[15], (TOKENS, D), 1.0, 6.0, ((0, 64), (1, 2)))
    return dict(inputs=inputs, block_ids=block_ids, expert_ids=expert_ids, prev_scores=prev_scores, gain_one=gain_one, w_qkv=w_qkv, w_out=w_out, gain_two=gain_two, w_router=w_router, w_residual=w_residual, w_const=w_const, const_vec=const_vec, w_gate=w_gate, w_up=w_up, w_down=w_down, cotangent=cotangent)


@jax.custom_vjp
def low(v):
    return lax.optimization_barrier(v.astype(jnp.bfloat16)).astype(jnp.float32)

@jax.custom_vjp
def low_back(v):
    return v

def low_keep(v):
    return (low(v), None)

def low_pass(kept, grad):
    return (grad,)

def back_keep(v):
    return (v, None)

def back_low(kept, grad):
    return (low(grad),)
low.defvjp(low_keep, low_pass)
low_back.defvjp(back_keep, back_low)
epsilon = 1e-06
highest = lax.Precision.HIGHEST

def exact_dot(left_side, right_side):
    return jnp.dot(left_side, right_side, precision=highest, preferred_element_type=jnp.float32)

def pair_softmax(logit_pairs):
    pair_top = lax.optimization_barrier(jnp.max(logit_pairs, axis=-1, keepdims=True))
    pair_exp = jnp.exp(logit_pairs - pair_top)
    return pair_exp / lax.optimization_barrier(jnp.sum(pair_exp, axis=-1, keepdims=True))

def slot_tables(expert_ids):
    pair_ids = expert_ids.reshape(N_WIDE, TOK_DEV * 2).astype(jnp.int32)
    expert_range = jnp.arange(EXPERTS, dtype=jnp.int32)
    pair_hot = (pair_ids[:, :, None] == expert_range[None, None, :]).astype(jnp.int32)
    pair_rank = lax.optimization_barrier(jnp.sum((jnp.cumsum(pair_hot, axis=1) - 1) * pair_hot, axis=2)).astype(jnp.int32)
    pair_slot = jnp.where(pair_ids < EXPERTS, pair_ids * CAP + pair_rank, EXPERTS * CAP).astype(jnp.int32)
    pair_index = jnp.arange(TOK_DEV * 2, dtype=jnp.int32)
    source_rows = jnp.broadcast_to(jnp.arange(N_WIDE, dtype=jnp.int32)[:, None], pair_ids.shape)
    pair_token = (source_rows * TOK_DEV + pair_index[None, :] // 2).astype(jnp.int32)
    pair_pick = jnp.broadcast_to(pair_index[None, :] % 2, pair_ids.shape).astype(jnp.int32)
    slot_token = jnp.full((N_WIDE, EXPERTS * CAP + 1), N_WIDE * TOK_DEV, jnp.int32)
    slot_token = slot_token.at[source_rows, pair_slot].set(pair_token)
    slot_pick = jnp.zeros((N_WIDE, EXPERTS * CAP + 1), jnp.int32).at[source_rows, pair_slot].set(pair_pick)
    slot_token = slot_token[:, :EXPERTS * CAP].reshape(N_WIDE, EXPERTS, CAP).transpose(1, 0, 2)
    slot_pick = slot_pick[:, :EXPERTS * CAP].reshape(N_WIDE, EXPERTS, CAP).transpose(1, 0, 2)
    return (slot_token.reshape(EXPERTS, N_WIDE * CAP), slot_pick.reshape(EXPERTS, N_WIDE * CAP))

def attend_sequence(operands):
    seq_queries, seq_keys, seq_values, seq_blocks = operands
    query_rows = math.gcd(SEQ, 512)
    query_parts = seq_queries.reshape(SEQ // query_rows, query_rows, HEADS, HEAD_DIM)
    block_parts = seq_blocks.reshape(SEQ // query_rows, query_rows)

    def attend_part(part):
        part_queries, part_blocks = part
        scores = jnp.einsum('qhc,khc->hqk', part_queries, seq_keys, precision=highest)
        scores = low_back(scores * (1.0 / math.sqrt(HEAD_DIM)))
        allowed = seq_blocks[None, :] <= part_blocks[:, None]
        scores = jnp.where(allowed[None], scores, -1e+30)
        row_top = lax.optimization_barrier(jnp.max(scores, axis=2, keepdims=True))
        shifted = jnp.exp(scores - row_top)
        prob_rows = low(shifted / lax.optimization_barrier(jnp.sum(shifted, axis=2, keepdims=True)))
        return jnp.einsum('hqk,khc->qhc', prob_rows, seq_values, precision=highest)
    outputs = lax.map(jax.checkpoint(attend_part), (query_parts, block_parts))
    return outputs.reshape(SEQ, HEADS, HEAD_DIM)

def run_expert(operands):
    slot_rows, gate_weight, up_weight, down_weight = operands
    gate_pre = low_back(exact_dot(slot_rows, gate_weight))
    up_pre = low_back(exact_dot(slot_rows, up_weight))
    hidden_units = low(gate_pre * jax.nn.sigmoid(gate_pre) * up_pre)
    return low_back(exact_dot(hidden_units, down_weight))

def forward(inputs, gain_one, w_qkv, w_out, gain_two, w_router, w_residual, w_const, const_vec, w_gate, w_up, w_down, prev_scores, expert_ids, block_ids, slot_token, slot_pick):
    token_count = inputs.shape[0]
    inv_one = lax.rsqrt(lax.optimization_barrier(jnp.mean(inputs * inputs, axis=1)) + epsilon)
    scaled_one = low(inputs * gain_one)
    project = low_back(exact_dot(scaled_one, w_qkv))
    qkv_all = low(inv_one[:, None] * project).reshape(token_count // SEQ, SEQ, 3, HEADS, HEAD_DIM)
    seq_blocks = block_ids.reshape(token_count // SEQ, SEQ)
    attended = lax.map(jax.checkpoint(attend_sequence), (qkv_all[:, :, 0], qkv_all[:, :, 1], qkv_all[:, :, 2], seq_blocks))
    attended = low(low_back(attended.reshape(token_count, D)))
    attn_out = low_back(exact_dot(attended, w_out))
    hidden = inputs + attn_out
    inv_two = lax.rsqrt(lax.optimization_barrier(jnp.mean(hidden * hidden, axis=1)) + epsilon)
    normed = low(hidden * inv_two[:, None] * gain_two)
    weighted = hidden * gain_two
    logits = inv_two[:, None] * exact_dot(weighted, w_router) + exact_dot(prev_scores, w_residual)
    const_logit = inv_two[:, None] * exact_dot(weighted, w_const)
    gate_probs = pair_softmax(jnp.take_along_axis(logits, expert_ids, axis=1))
    const_alpha = pair_softmax(const_logit.reshape(token_count, 2, 2))
    padded = jnp.concatenate([normed, jnp.zeros((1, D), jnp.float32)], axis=0)
    gate_padded = jnp.concatenate([gate_probs, jnp.zeros((1, 2), jnp.float32)], axis=0)
    expert_rows = padded[slot_token]
    slot_gates = gate_padded[slot_token, slot_pick]
    gate_weights = w_gate.reshape(D, EXPERTS, FF).transpose(1, 0, 2)
    up_weights = w_up.reshape(D, EXPERTS, FF).transpose(1, 0, 2)
    down_weights = w_down.reshape(EXPERTS, FF, D)
    expert_out = lax.map(jax.checkpoint(run_expert), (expert_rows, gate_weights, up_weights, down_weights))
    contributions = (slot_gates[:, :, None] * expert_out).reshape(-1, D)
    ffn_mix = jax.ops.segment_sum(contributions, slot_token.reshape(-1), num_segments=token_count + 1)[:token_count]
    copy_weight = lax.optimization_barrier(jnp.sum(gate_probs * (expert_ids == EXPERTS + 1), axis=1))
    const_pick = (expert_ids[:, :, None] == EXPERTS + 2 + jnp.arange(2, dtype=jnp.int32)[None, None, :]).astype(jnp.float32)
    const_weight = lax.optimization_barrier(jnp.sum(gate_probs[:, :, None] * const_pick, axis=1))
    self_weight = copy_weight + lax.optimization_barrier(jnp.sum(const_weight * const_alpha[:, :, 0], axis=1))
    mixture = ffn_mix + self_weight[:, None] * normed + exact_dot(const_weight * const_alpha[:, :, 1], const_vec)
    return hidden + mixture

def reference(inputs, block_ids, expert_ids, prev_scores, gain_one, w_qkv, w_out, gain_two, w_router, w_residual, w_const, const_vec, w_gate, w_up, w_down, cotangent):
    slot_token, slot_pick = slot_tables(expert_ids)
    floats = tuple((tensor.astype(jnp.float32) for tensor in (inputs, gain_one, w_qkv, w_out, gain_two, w_router, w_residual, w_const, const_vec, w_gate, w_up, w_down, prev_scores)))

    def layer_forward(*parameters):
        return forward(*parameters, expert_ids, block_ids, slot_token, slot_pick)
    output, pullback = jax.vjp(layer_forward, *floats)
    gradients = pullback(cotangent.astype(jnp.float32))
    return (output.astype(jnp.bfloat16), gradients[0], gradients[12], gradients[1], gradients[2], gradients[3], gradients[4], gradients[5], gradients[6], gradients[7], gradients[8], gradients[9], gradients[10], gradients[11])
```

```python
import functools
import math

import jax
import jax.numpy as jnp
from jax import lax
from jax.experimental import pallas as pl
from jax.experimental.pallas import tpu as pltpu
from jax.sharding import Mesh
from jax.sharding import PartitionSpec as P

HEAD_DIM = 64
EXPERTS = 8
ROUTES = 12
CAP = 128
D = 768
HALF = 384
TOK = 256
SEQ = 4096
KT = 512

MESH = pl.DeviceIdType.MESH
AXES = ("n", "zl", "x", "y", "c")
SIZES = dict(n=2, zl=2, x=4, y=4, c=2, z=4)
WIDE = ("zl", "x", "y", "c")
VMEM_LIMIT = 60 * 1024 * 1024

epsilon = 1e-06
highest = lax.Precision.HIGHEST
f32 = jnp.float32
bf16 = jnp.bfloat16


def exact_dot(left_side, right_side):
    return jnp.dot(left_side, right_side, precision=highest, preferred_element_type=f32)


def dot_dims(left_side, right_side, left_dim, right_dim):
    return lax.dot_general(
        left_side, right_side, (((left_dim,), (right_dim,)), ((), ())), preferred_element_type=f32
    )


def pair_softmax(logit_pairs):
    pair_top = jnp.max(logit_pairs, axis=-1, keepdims=True)
    pair_exp = jnp.exp(logit_pairs - pair_top)
    return pair_exp / jnp.sum(pair_exp, axis=-1, keepdims=True)


def coords():
    place = {axis: lax.axis_index(axis) for axis in AXES}
    place["z"] = place["n"] * 2 + place["zl"]
    return place


def moved(place, shift):
    target = {}
    for axis, steps in shift.items():
        value = lax.rem(place[axis] + steps, SIZES[axis])
        if axis == "z":
            target["n"] = value // 2
            target["zl"] = lax.rem(value, 2)
        else:
            target[axis] = value
    return target


def shifts_of(axes):
    found = [{}]
    for axis in axes:
        found = [dict(one, **{axis: k}) for one in found for k in range(SIZES[axis])]
    return [{a: k for a, k in one.items() if k} for one in found if any(one.values())]


def reverse(shift):
    return {axis: (SIZES[axis] - steps) % SIZES[axis] for axis, steps in shift.items()}


def rank_of(place, axes, shift=None):
    rank = 0
    for axis in axes:
        value = place[axis]
        if shift and axis in shift:
            value = lax.rem(value + shift[axis], SIZES[axis])
        rank = rank * SIZES[axis] + value
    return rank


def greet_start(place, shifts):
    barrier = pltpu.get_barrier_semaphore()
    for shift in shifts:
        pl.semaphore_signal(barrier, inc=1, device_id=moved(place, shift), device_id_type=MESH)


def greet_end(shifts):
    pl.semaphore_wait(pltpu.get_barrier_semaphore(), len(shifts))


def greet(place, shifts):
    greet_start(place, shifts)
    greet_end(shifts)


def push(source, target, send_sem, recv_sem, device):
    copy = pltpu.make_async_remote_copy(
        src_ref=source,
        dst_ref=target,
        send_sem=send_sem,
        recv_sem=recv_sem,
        device_id=device,
        device_id_type=MESH,
    )
    copy.start()
    return copy


def in_vmem(count):
    return [pl.BlockSpec(memory_space=pltpu.VMEM)] * count


def comm_params(collective_id):
    return pltpu.CompilerParams(
        collective_id=collective_id, has_side_effects=True, vmem_limit_bytes=VMEM_LIMIT
    )


def shape_of(shape, dtype):
    return jax.ShapeDtypeStruct(shape, dtype)


def unique(shift_lists):
    seen = []
    for shifts in shift_lists:
        for shift in shifts:
            if shift not in seen:
                seen.append(shift)
    return seen


def diagonal(size):
    rows = lax.broadcasted_iota(jnp.int32, (size, size), 0)
    return rows == lax.broadcasted_iota(jnp.int32, (size, size), 1)


def to_row(value):
    size = value.shape[0]
    return jnp.sum(jnp.where(diagonal(size), value, jnp.zeros_like(value)), axis=0, keepdims=True)


def to_column(value):
    size = min(value.shape[1], 128)
    mask = diagonal(size)
    return jnp.concatenate(
        [
            jnp.sum(
                jnp.where(mask, value[:, k * size : (k + 1) * size], jnp.zeros((), value.dtype)),
                axis=1,
                keepdims=True,
            )
            for k in range(value.shape[1] // size)
        ],
        axis=0,
    )


ORDERS = (("x", "y", "z"), ("y", "z", "x"), ("z", "x", "y"))
PART = 16


def make_plan(ids_ref, cot_ref, hit_ref, table_ref, rows_ref):
    tokens = 2 * TOK
    expert = lax.broadcasted_iota(jnp.int32, (tokens, 128), 1)
    ids = [to_column(ids_ref[k : k + 1, :]) for k in range(2)]
    table_ref[...] = jnp.zeros_like(table_ref)
    named = ((expert == ids[0]) | (expert == ids[1])).astype(bf16)
    before = lax.broadcasted_iota(jnp.int32, (tokens, tokens), 1) < lax.broadcasted_iota(
        jnp.int32, (tokens, tokens), 0
    )
    ranks = dot_dims(before.astype(bf16), named, 1, 0)
    slot = lax.broadcasted_iota(jnp.int32, (CAP * 2, tokens), 0)
    rows = []
    for k in range(2):
        rank = jnp.sum(jnp.where(expert == ids[k], ranks, 0.0), axis=1, keepdims=True)
        place = jnp.where(ids[k] < EXPERTS, ids[k] * CAP + rank.astype(jnp.int32), -1)
        table_ref[:, k : k + 1] = ids[k]
        table_ref[:, 2 + k : 3 + k] = place
        rows.append(to_row(place))
    for j in range(4):
        first = j * 2 * CAP
        hit = ((slot + first == rows[0]) | (slot + first == rows[1])).astype(bf16)
        hit_ref[first : first + 2 * CAP, :] = hit
        held = dot_dims(hit[:, :TOK], cot_ref[0], 1, 0) + dot_dims(hit[:, TOK:], cot_ref[1], 1, 0)
        held = held.astype(bf16)
        for i in range(4):
            rows_ref[j * 4 + i] = held[i * 64 : (i + 1) * 64, :]


def gather_all(w_qkv, w_out, inputs, cotangent, gains, tables, expert_ids):
    swaps_in = [
        (inputs, 1),
        (cotangent, 1),
        (shape_of((1, PART, HALF), bf16), 2),
        (shape_of((1, HALF, 128), bf16), 2),
    ]
    extra = len(swaps_in)
    given = [w_qkv, w_out, inputs, cotangent, expert_ids, *gains, *tables]
    peers = unique([shifts_of((a,)) for a in ("x", "y", "z", "c")])

    def kernel(*refs):
        qkv_ref, out_ref, in_ref, cot_ref, ids_ref = refs[:5]
        small_refs = refs[5 : len(given)]
        rest = refs[len(given) :]
        parts, swapped = rest[:3], rest[3 : 3 + extra]
        hit_ref, slots_ref, rows_ref = rest[3 + extra : 6 + extra]
        gain_s, table_s, send, recv, sib_send, sib_recv, swap_send, swap_recv = rest[6 + extra :]
        ins = (in_ref, cot_ref, gain_s, table_s)
        place = coords()
        core = place["c"]
        block = jnp.concatenate([qkv_ref[...].astype(f32), out_ref[...].astype(f32)], axis=0)
        block = block.astype(bf16)
        for k in range(3):
            first, second, third = (place[a] for a in ORDERS[k])
            parts[k][core, third, second, first] = block[k * PART : (k + 1) * PART, :]
        greet_start(place, peers)
        rows = [ref[...].astype(f32) for ref in small_refs[: len(gains)]]
        rows.append(jnp.zeros((PART - sum(row.shape[0] for row in rows), HALF), f32))
        gain_s[0] = jnp.concatenate(rows, axis=0).astype(bf16)
        lanes = [ref[...].astype(f32) for ref in small_refs[len(gains) :]]
        lanes.append(jnp.zeros((128 - sum(lane.shape[0] for lane in lanes), HALF), f32))
        table_s[0] = jnp.concatenate(lanes, axis=0).T.astype(bf16)
        greet_end(peers)
        stages = []
        for k in range(3):
            first, second, third = (place[a] for a in ORDERS[k])
            spot = parts[k].at[core, third, second, first]
            stages.append(
                [
                    push(spot, spot, send.at[k, 0, d], recv.at[k, 0, d], moved(place, {ORDERS[k][0]: d + 1}))
                    for d in range(3)
                ]
            )
        swaps = swap_start(place, swaps_in, ins, swapped, swap_send, swap_recv)
        make_plan(ids_ref, cot_ref, hit_ref, slots_ref, rows_ref)
        later = []
        for k in range(3):
            first, second, third = (place[a] for a in ORDERS[k])
            for copy in stages[k]:
                copy.wait_recv()
            spot = parts[k].at[core, third, second]
            later.append(
                [
                    push(spot, spot, send.at[k, 1, d], recv.at[k, 1, d], moved(place, {ORDERS[k][1]: d + 1}))
                    for d in range(3)
                ]
            )
        last, sibling = [], []
        for k in range(3):
            third = place[ORDERS[k][2]]
            for copy in later[k]:
                copy.wait_recv()
            spot = parts[k].at[core, third]
            last.append(
                [
                    push(spot, spot, send.at[k, 2, d], recv.at[k, 2, d], moved(place, {ORDERS[k][2]: d + 1}))
                    for d in range(3)
                ]
            )
            sibling.append(push(spot, spot, sib_send.at[k, 0], sib_recv.at[k, 0], moved(place, {"c": 1})))
        for d in range(3):
            for k in range(3):
                third = place[ORDERS[k][2]]
                last[k][d].wait_recv()
                spot = parts[k].at[core, lax.rem(third + 3 - d, 4)]
                sibling.append(
                    push(spot, spot, sib_send.at[k, d + 1], sib_recv.at[k, d + 1], moved(place, {"c": 1}))
                )
        for copy in sibling + swaps:
            copy.wait_recv()
        for k in range(3):
            for copy in stages[k] + later[k] + last[k]:
                copy.wait_send()
        for copy in sibling + swaps:
            copy.wait_send()

    whole = shape_of((2, 4, 4, 4, PART, HALF), bf16)
    return pl.pallas_call(
        kernel,
        out_shape=[whole] * 3
        + swap_shapes(swaps_in)
        + [
            shape_of((EXPERTS * CAP, 2 * TOK), bf16),
            shape_of((2 * TOK, 128), jnp.int32),
            shape_of((16, 64, HALF), bf16),
        ],
        in_specs=in_vmem(len(given)),
        out_specs=in_vmem(6 + extra),
        scratch_shapes=[
            pltpu.VMEM((1, PART, HALF), bf16),
            pltpu.VMEM((1, HALF, 128), bf16),
            pltpu.SemaphoreType.DMA((3, 3, 3)),
            pltpu.SemaphoreType.DMA((3, 3, 3)),
            pltpu.SemaphoreType.DMA((3, 4)),
            pltpu.SemaphoreType.DMA((3, 4)),
            pltpu.SemaphoreType.DMA((extra,)),
            pltpu.SemaphoreType.DMA((extra,)),
        ],
        compiler_params=comm_params(1),
        name="gather_weights",
    )(*given)


def swap_shapes(swaps_in):
    return [shape_of((2,) + a.shape[1:], a.dtype) for a, _ in swaps_in]


def swap_start(place, swaps_in, ins, swapped, send, recv):
    n = place["n"]
    copies = []
    for i, (_, share) in enumerate(swaps_in):
        copies.append(
            push(ins[i].at[(1 - n) // share], swapped[i].at[n], send.at[i], recv.at[i], moved(place, {"z": 2}))
        )
        swapped[i][n] = ins[i][n // share]
    return copies


def blocks_of_weights():
    for zl in range(2):
        for x in range(4):
            for y in range(4):
                for c in range(2):
                    for n in range(2):
                        at = dict(x=x, y=y, z=2 * n + zl)
                        spots = [(c, at[o[2]], at[o[1]], at[o[0]]) for o in ORDERS]
                        yield ((zl * 4 + x) * 4 + y) * 2 + c, slice(n * HALF, (n + 1) * HALF), spots


def project_forward(parts, x_halves, vectors):
    def kernel(pa, pb, pc, x_ref, vec_ref, wq_ref, wo_ref, q_ref, kv_ref, pq_ref, proj_ref, scaled_ref, inv_ref, wq_s, wo_s):
        parts = (pa, pb, pc)
        for w, cols, spots in blocks_of_weights():
            blocks = [parts[k][spots[k]].astype(f32) for k in range(3)]
            wq_s[w * 36 : w * 36 + 16, cols] = blocks[0]
            wq_s[w * 36 + 16 : w * 36 + 32, cols] = blocks[1]
            wq_s[w * 36 + 32 : w * 36 + 36, cols] = blocks[2][:4]
            wo_s[w * 12 : w * 12 + 12, cols] = blocks[2][4:]
        for j in range(9):
            wq_ref[j * 256 : (j + 1) * 256, :] = wq_s[j * 256 : (j + 1) * 256, :].astype(bf16)
        for j in range(3):
            wo_ref[j * 256 : (j + 1) * 256, :] = wo_s[j * 256 : (j + 1) * 256, :].astype(bf16)
        x = jnp.concatenate([x_ref[0], x_ref[1]], axis=1).astype(f32)
        gain = jnp.concatenate([vec_ref[0, 0:1], vec_ref[1, 0:1]], axis=1).astype(f32)
        inv = lax.rsqrt(jnp.mean(x * x, axis=1, keepdims=True) + epsilon)
        scaled = (x * gain).astype(bf16)
        scaled_ref[...] = scaled
        inv_ref[...] = inv
        inv_row = to_row(inv)
        for s in range(3):
            for y in range(4):
                first = s * D + y * 192
                if s == 0:
                    project = dot_dims(wq_ref[first : first + 192, :], scaled, 1, 1)
                    pq_ref[y] = project
                    q_ref[y] = (inv_row * project).astype(bf16)
                else:
                    project = dot_dims(scaled, wq_ref[first : first + 192, :], 1, 1)
                    proj_ref[(s - 1) * 4 + y] = project
                    value = (inv * project).astype(bf16)
                    for h in range(3):
                        spot = h * 128 + (s - 1) * HEAD_DIM
                        kv_ref[y, :, spot : spot + HEAD_DIM] = value[:, h * HEAD_DIM : (h + 1) * HEAD_DIM]

    return pl.pallas_call(
        kernel,
        out_shape=[
            shape_of((3 * D, D), bf16),
            shape_of((D, D), bf16),
            shape_of((4, 192, TOK), bf16),
            shape_of((4, TOK, HALF), bf16),
            shape_of((4, 192, TOK), f32),
            shape_of((8, TOK, 192), f32),
            shape_of((TOK, D), bf16),
            shape_of((TOK, 1), f32),
        ],
        in_specs=in_vmem(5),
        out_specs=in_vmem(8),
        scratch_shapes=[pltpu.VMEM((3 * D, D), f32), pltpu.VMEM((D, D), f32)],
        compiler_params=pltpu.CompilerParams(vmem_limit_bytes=VMEM_LIMIT),
        name="project_forward",
    )(*parts, x_halves, vectors)


SCALARS = ("inv", "gate0", "gate1", "a00", "a01", "a10", "a11", "cw0", "cw1", "self", "vec0", "vec1")
RAW = 32


def column(table, name):
    spot = SCALARS.index(name)
    return table[:, spot : spot + 1]


def vector_rows(vec_ref, first, count):
    both = [vec_ref[half, first : first + count].astype(f32) for half in range(2)]
    return jnp.concatenate(both, axis=1)


def exact_dims(left_side, right_side, left_dim, right_dim):
    return lax.dot_general(
        left_side,
        right_side,
        (((left_dim,), (right_dim,)), ((), ())),
        precision=highest,
        preferred_element_type=f32,
    )


def router_table(rc_ref):
    return jnp.concatenate([rc_ref[half, :, :16].astype(f32) for half in range(2)], axis=0)


def middle_forward(
    own_tokens, at_ref, x_ref, wo_ref, vec_ref, rc_ref, prev_ref, res_ref, plan_ref,
    hidden_ref, normed_ref, base_ref, table_ref, gates_ref,
):
    hidden = jnp.concatenate([x_ref[0], x_ref[1]], axis=1).astype(f32)
    for y in range(4):
        hidden = hidden + dot_dims(at_ref[y], wo_ref[y * 192 : (y + 1) * 192, :], 0, 0)
    hidden_ref[...] = hidden
    gain = vector_rows(vec_ref, 1, 1)
    inv = lax.rsqrt(jnp.mean(hidden * hidden, axis=1, keepdims=True) + epsilon)
    weighted = hidden * gain
    normed = (hidden * inv * gain).astype(bf16)
    normed_ref[...] = normed
    raw = exact_dims(weighted, router_table(rc_ref), 1, 0)
    logits = inv * raw[:, :ROUTES] + exact_dims(prev_ref[:, own_tokens], res_ref[...].astype(f32), 0, 0)
    route = lax.broadcasted_iota(jnp.int32, (TOK, ROUTES), 1)
    e0, e1 = plan_ref[own_tokens, 0:1], plan_ref[own_tokens, 1:2]
    l0 = jnp.sum(jnp.where(route == e0, logits, 0.0), axis=1, keepdims=True)
    l1 = jnp.sum(jnp.where(route == e1, logits, 0.0), axis=1, keepdims=True)

    def softmax_two(first, second):
        top = jnp.maximum(first, second)
        a, b = jnp.exp(first - top), jnp.exp(second - top)
        return a / (a + b), b / (a + b)

    gate0, gate1 = softmax_two(l0, l1)
    coeff = [inv * raw[:, ROUTES + i : ROUTES + i + 1] for i in range(4)]
    a00, a01 = softmax_two(coeff[0], coeff[1])
    a10, a11 = softmax_two(coeff[2], coeff[3])

    def chosen(expert):
        return jnp.where(e0 == expert, gate0, 0.0) + jnp.where(e1 == expert, gate1, 0.0)

    cw0, cw1 = chosen(EXPERTS + 2), chosen(EXPERTS + 3)
    own = chosen(EXPERTS + 1) + cw0 * a00 + cw1 * a10
    vec0, vec1 = cw0 * a01, cw1 * a11
    const = vector_rows(vec_ref, 2, 2)
    base = hidden + own * normed.astype(f32) + vec0 * const[0:1] + vec1 * const[1:2]
    for half in range(2):
        base_ref[half] = base[:, half * HALF : (half + 1) * HALF].astype(bf16)
    values = dict(
        inv=inv, gate0=gate0, gate1=gate1, a00=a00, a01=a01, a10=a10, a11=a11, cw0=cw0, cw1=cw1,
        self=own, vec0=vec0, vec1=vec1,
    )
    lane = lax.broadcasted_iota(jnp.int32, (TOK, 128), 1)
    table = jnp.zeros((TOK, 128), f32)
    for i, name in enumerate(SCALARS):
        table = jnp.where(lane == i, values[name], table)
    table_ref[...] = table
    table_ref[:, RAW : RAW + 16] = raw
    slot = lax.broadcasted_iota(jnp.int32, (TOK, EXPERTS * CAP), 1)
    s0, s1 = plan_ref[own_tokens, 2:3], plan_ref[own_tokens, 3:4]
    slot_gates = jnp.where(slot == s0, gate0, 0.0) + jnp.where(slot == s1, gate1, 0.0)
    slot_gates = jnp.sum(slot_gates, axis=0, keepdims=True)
    gates_ref[...] = jnp.zeros_like(gates_ref)
    for b in range(16):
        gates_ref[b, 0:1, 0:64] = slot_gates[:, b * 64 : (b + 1) * 64]


ROUTE_AXES = ("zl", "x", "n")


def experts_step(attended, x_halves, wo, vectors, routers, prev, residual, plan, hit, grad_rows, weights):
    shifts = shifts_of(ROUTE_AXES)
    count = len(shifts)
    rows = 2 * TOK
    peers = unique([shifts, [{"c": 1}]])
    one = weights.shape[2:]

    def kernel(
        at_ref, x_ref, wo_ref, vec_ref, rc_ref, prev_ref, res_ref, plan_ref, hit_ref, gr_ref, w_hbm,
        hidden_ref, normed_ref, base_ref, table_ref, out_ref, slots_ref, dots_out, sum_ref, far_ref, far_other_ref,
        gates_s, sending, half, row_s, arrived, gates_in, w, dw, dw_in, x, xt, g, gate_col, dy, dyt, units_s, dgate_s,
        dup_s, dx_acc, out_acc, dx_s, dot_s, p_send, p_recv,
        w_sem, e_send, e_recv, g_send, g_recv, r_send, r_recv, b_send, b_recv, d_send, d_recv,
    ):
        place = coords()
        n, y, c = place["n"], place["y"], place["c"]
        me = rank_of(place, ROUTE_AXES)
        sibling = moved(place, {"c": 1})
        greet_start(place, peers)
        loads = [
            pltpu.make_async_copy(w_hbm.at[i, p], w.at[i, p], w_sem.at[i, p]) for p in range(8) for i in range(2)
        ]
        for load in loads:
            load.start()
        own_tokens = pl.ds(pl.multiple_of(n * TOK, 128), TOK)
        middle_forward(
            own_tokens, at_ref, x_ref, wo_ref, vec_ref, rc_ref, prev_ref, res_ref, plan_ref,
            hidden_ref, normed_ref, base_ref, table_ref, gates_s,
        )
        sending[...] = normed_ref[:, pl.ds(pl.multiple_of((1 - n) * HALF, 128), HALF)]
        greet_end(peers)
        swap = push(sending, half.at[n], p_send, p_recv, moved(place, {"n": 1}))
        copies = []
        for j, shift in enumerate(shifts):
            to = rank_of(place, ROUTE_AXES, shift)
            copies.append(push(gates_s.at[to], gates_in.at[me], g_send.at[j], g_recv.at[j], moved(place, shift)))
        half[n] = normed_ref[:, pl.ds(pl.multiple_of(n * HALF, 128), HALF)]
        gates_in[me] = gates_s[me]
        for source in range(8):
            for side in range(2):
                g[source * 64 : (source + 1) * 64, side * HALF : (side + 1) * HALF] = gr_ref[2 * source + side]
        swap.wait_recv()
        for e in range(4):
            span = slice(e * 256, (e + 1) * 256)
            block = dot_dims(hit_ref[span, :TOK], half[0], 1, 0) + dot_dims(hit_ref[span, TOK:], half[1], 1, 0)
            block = block.astype(bf16)
            for i in range(4):
                row_s[e * 4 + i] = block[i * 64 : (i + 1) * 64, :]
        for j, shift in enumerate(shifts):
            to = rank_of(place, ROUTE_AXES, shift)
            copies.append(push(row_s.at[to], arrived.at[me], r_send.at[j], r_recv.at[j], moved(place, shift)))
        arrived[me] = row_s[me]
        for copy in copies[:count]:
            copy.wait_recv()
        for source in range(8):
            both = gates_in[2 * source, 0:1, 0:64] + gates_in[2 * source + 1, 0:1, 0:64]
            gate_col[source * 64 : (source + 1) * 64, :] = to_column(both)
        dffn = (g[...].astype(f32) * gate_col[...]).astype(bf16)
        dy[...] = dffn
        dyt[...] = dffn.T
        dx_acc[...] = jnp.zeros_like(dx_acc)
        out_acc[...] = jnp.zeros_like(out_acc)
        for copy in copies[count:]:
            copy.wait_recv()
        for source in range(8):
            for side in range(2):
                x[source * 64 : (source + 1) * 64, side * HALF : (side + 1) * HALF] = arrived[2 * source + side]
        xt[...] = x[...].T
        sides = (slice(0, HALF), slice(HALF, D))

        def units_step(p, carry):
            gate = sum(dot_dims(x[:, s], w[i, p, 0], 1, 0) for i, s in enumerate(sides))
            up = sum(dot_dims(x[:, s], w[i, p, 1], 1, 0) for i, s in enumerate(sides))
            dunits = sum(dot_dims(dy[:, s], w[i, p, 2], 1, 0) for i, s in enumerate(sides))
            sig = 1.0 / (1.0 + jnp.exp(-gate))
            active = gate * sig
            units = (active * up).astype(bf16)
            slope = sig * (1.0 + gate * (1.0 - sig))
            dgate = (dunits * up * slope).astype(bf16)
            dup = (dunits * active).astype(bf16)
            units_s[p], dgate_s[p], dup_s[p] = units, dgate, dup
            for i, s in enumerate(sides):
                out_acc[:, s] += dot_dims(units, w[i, p, 2], 1, 1)
                dx_acc[:, s] += dot_dims(dgate, w[i, p, 0], 1, 1) + dot_dims(dup, w[i, p, 1], 1, 1)
            return carry

        for load in loads:
            load.wait()
        lax.fori_loop(0, 8, units_step, 0)
        dot_s[...] = jnp.zeros_like(dot_s)
        for source in range(8):
            span = slice(source * 64, (source + 1) * 64)
            for side in range(2):
                dx_s[2 * source + side] = dx_acc[span, sides[side]].astype(bf16)
        back = []
        for j, shift in enumerate(shifts):
            to = rank_of(place, ROUTE_AXES, shift)
            back.append(push(dx_s.at[to], slots_ref.at[me], b_send.at[j], b_recv.at[j], moved(place, shift)))
        for source in range(8):
            span = slice(source * 64, (source + 1) * 64)
            dots = jnp.sum(g[span, :].astype(f32) * out_acc[span, :], axis=1, keepdims=True)
            dot_s[source, 0:1, 0:64] = to_row(dots)
        for j, shift in enumerate(shifts):
            to = rank_of(place, ROUTE_AXES, shift)
            back.append(push(dot_s.at[to // 2], dots_out.at[me], d_send.at[j], d_recv.at[j], moved(place, shift)))
        slots_ref[me] = dx_s[me]
        dots_out[me] = dot_s[me // 2]
        for source in range(8):
            span = slice(source * 64, (source + 1) * 64)
            for side in range(2):
                out_ref[2 * source + side] = (out_acc[span, sides[side]] * gate_col[span, :]).astype(bf16)

        grad_copies = {}
        for core in (1 - c, c):
            for d in (2, 1, 3, 0):
                p = 2 * lax.rem(y + d, 4) + core
                for i, s in enumerate(sides):
                    dw[i, p, 0] = dot_dims(xt[s, :], dgate_s[p], 1, 0).astype(bf16)
                    dw[i, p, 1] = dot_dims(xt[s, :], dup_s[p], 1, 0).astype(bf16)
                    dw[i, p, 2] = dot_dims(dyt[s, :], units_s[p], 1, 0).astype(bf16)
                    if core is not c:
                        grad_copies[d, i] = push(
                            dw.at[i, p], dw_in.at[d, i], e_send.at[d, i], e_recv.at[d, i], sibling
                        )
        for d in (2, 1, 3, 0):
            totals = []
            for i in range(2):
                grad_copies[d, i].wait_recv()
                total = dw[i, 2 * lax.rem(y + d, 4) + c].astype(f32) + dw_in[d, i].astype(f32)
                totals.append(total.astype(bf16))
            if d == 2:
                far_ref[...] = jnp.where(n == 0, totals[0], totals[1])
                far_other_ref[...] = jnp.where(n == 0, totals[1], totals[0])
            else:
                sum_ref[(d + 1) // 2, 0], sum_ref[(d + 1) // 2, 1] = totals
        for copy in back:
            copy.wait_recv()
        for copy in copies + back + list(grad_copies.values()):
            copy.wait_send()
        swap.wait_send()

    route = pltpu.SemaphoreType.DMA((count,))
    return pl.pallas_call(
        kernel,
        out_shape=[
            shape_of((TOK, D), f32),
            shape_of((TOK, D), bf16),
            shape_of((2, TOK, HALF), bf16),
            shape_of((TOK, 128), f32),
            shape_of((16, 64, HALF), bf16),
            shape_of((16, 64, HALF), bf16),
            shape_of((16, 8, 128), f32),
            shape_of((3, 2) + one, bf16),
            shape_of(one, bf16),
            shape_of(one, bf16),
        ],
        in_specs=in_vmem(10) + [pl.BlockSpec(memory_space=pl.ANY)],
        out_specs=in_vmem(10),
        scratch_shapes=[
            pltpu.VMEM((16, 8, 128), f32),
            pltpu.VMEM((TOK, HALF), bf16),
            pltpu.VMEM((2, TOK, HALF), bf16),
            pltpu.VMEM((16, 64, HALF), bf16),
            pltpu.VMEM((16, 64, HALF), bf16),
            pltpu.VMEM((16, 8, 128), f32),
            pltpu.VMEM(weights.shape, bf16),
            pltpu.VMEM(weights.shape, bf16),
            pltpu.VMEM((4, 2) + one, bf16),
            pltpu.VMEM((rows, D), bf16),
            pltpu.VMEM((D, rows), bf16),
            pltpu.VMEM((rows, D), bf16),
            pltpu.VMEM((rows, 1), f32),
            pltpu.VMEM((rows, D), bf16),
            pltpu.VMEM((D, rows), bf16),
            pltpu.VMEM((8, rows, 256), bf16),
            pltpu.VMEM((8, rows, 256), bf16),
            pltpu.VMEM((8, rows, 256), bf16),
            pltpu.VMEM((rows, D), f32),
            pltpu.VMEM((rows, D), f32),
            pltpu.VMEM((16, 64, HALF), bf16),
            pltpu.VMEM((8, 8, 128), f32),
            pltpu.SemaphoreType.DMA,
            pltpu.SemaphoreType.DMA,
            pltpu.SemaphoreType.DMA((2, 8)),
            pltpu.SemaphoreType.DMA((4, 2)),
            pltpu.SemaphoreType.DMA((4, 2)),
        ]
        + [route] * 8,
        compiler_params=comm_params(6),
        name="experts_step",
    )(attended, x_halves, wo, vectors, routers, prev, residual, plan, hit, grad_rows, weights)


def middle_backward(slot_grads, hit, g_halves, hidden, normed, table, vectors, routers, dots, plan, prev, residual, wo):
    def kernel(
        rows_ref, hit_ref, g_ref, hidden_ref, normed_ref, table_ref, vec_ref, rc_ref, dots_ref, plan_ref, prev_ref,
        res_ref, wo_ref, hg_ref, og_ref, heads_ref, small_ref, gprev_ref, dn, row, sending, other, p_send, p_recv,
    ):
        place = coords()
        n = place["n"]
        neighbour = [{"n": 1}]
        greet_start(place, neighbour)
        rows = rows_ref[...].reshape(EXPERTS * CAP, HALF)
        theirs = hit_ref[:, pl.ds(pl.multiple_of((1 - n) * TOK, 128), TOK)]
        sending[...] = dot_dims(theirs, rows, 0, 0).astype(bf16)
        greet_end(neighbour)
        swap = push(sending, other, p_send, p_recv, moved(place, {"n": 1}))
        mine = hit_ref[:, pl.ds(pl.multiple_of(n * TOK, 128), TOK)]
        dn[:, pl.ds(pl.multiple_of(n * HALF, 128), HALF)] = dot_dims(mine, rows, 0, 0)
        own_tokens = pl.ds(pl.multiple_of(n * TOK, 128), TOK)
        for b in range(16):
            row[:, b * 64 : (b + 1) * 64] = dots_ref[b, 0:1, 0:64]
        table = table_ref[...]
        val = {name: column(table, name) for name in SCALARS}
        raw = table_ref[:, RAW : RAW + 16]
        g = jnp.concatenate([g_ref[0], g_ref[1]], axis=1).astype(f32)
        hidden = hidden_ref[...]
        gain = vector_rows(vec_ref, 1, 1)
        const = vector_rows(vec_ref, 2, 2)
        weighted = hidden * gain
        normed = normed_ref[...].astype(f32)
        slot = lax.broadcasted_iota(jnp.int32, (TOK, EXPERTS * CAP), 1)
        e0, e1 = plan_ref[own_tokens, 0:1], plan_ref[own_tokens, 1:2]
        dots = row[...]

        def total(array):
            return jnp.sum(array, axis=1, keepdims=True)

        dot_self = total(g * normed)
        dot_vec = [total(g * const[j : j + 1]) for j in range(2)]
        const_dots = [
            val["a00"] * dot_self + val["a01"] * dot_vec[0],
            val["a10"] * dot_self + val["a11"] * dot_vec[1],
        ]

        def gate_dot(expert, places):
            result = total(jnp.where(slot == places, dots, 0.0))
            result = result + jnp.where(expert == EXPERTS + 1, dot_self, 0.0)
            for j in range(2):
                result = result + jnp.where(expert == EXPERTS + 2 + j, const_dots[j], 0.0)
            return result

        d0, d1 = gate_dot(e0, plan_ref[own_tokens, 2:3]), gate_dot(e1, plan_ref[own_tokens, 3:4])
        mean = val["gate0"] * d0 + val["gate1"] * d1
        route = lax.broadcasted_iota(jnp.int32, (TOK, 16), 1)
        grads = jnp.where(route == e0, val["gate0"] * (d0 - mean), 0.0)
        grads = grads + jnp.where(route == e1, val["gate1"] * (d1 - mean), 0.0)
        logits_grad = grads[:, :ROUTES]
        for j in range(2):
            first, second = val["a%d0" % j], val["a%d1" % j]
            weight = val["cw%d" % j]
            da, db = weight * dot_self, weight * dot_vec[j]
            middle = first * da + second * db
            grads = jnp.where(route == ROUTES + 2 * j, first * (da - middle), grads)
            grads = jnp.where(route == ROUTES + 2 * j + 1, second * (db - middle), grads)
        inv = val["inv"]
        scaled_grads = inv * grads
        weighted_grad = exact_dims(scaled_grads, router_table(rc_ref), 1, 1)
        swap.wait_recv()
        dn[:, pl.ds(pl.multiple_of((1 - n) * HALF, 128), HALF)] = other[...].astype(f32)
        normed_grad = dn[...] + val["self"] * g
        inv_grad = total(normed_grad * weighted) + total(grads * raw)
        small_ref[...] = jnp.zeros_like(small_ref)
        small_ref[0:16, :D] = exact_dims(scaled_grads, weighted, 0, 0)
        small_ref[16:17, :D] = jnp.sum(val["vec0"] * g, axis=0, keepdims=True)
        small_ref[17:18, :D] = jnp.sum(val["vec1"] * g, axis=0, keepdims=True)
        small_ref[18:19, :D] = jnp.sum(normed_grad * hidden * inv + weighted_grad * hidden, axis=0, keepdims=True)
        small_ref[0:ROUTES, D : D + ROUTES] = exact_dims(prev_ref[:, own_tokens], logits_grad, 1, 0)
        gprev_ref[...] = jnp.zeros_like(gprev_ref)
        gprev_ref[0, 0:ROUTES, :] = exact_dims(res_ref[...].astype(f32), logits_grad, 1, 1)
        hidden_grad = (
            g
            + normed_grad * inv * gain
            + weighted_grad * gain
            - (inv_grad * (inv * inv * inv) / D) * hidden
        )
        hg_ref[...] = hidden_grad
        out_grad = hidden_grad.astype(bf16)
        og_ref[...] = out_grad
        for y in range(4):
            heads_ref[y] = dot_dims(wo_ref[y * 192 : (y + 1) * 192, :], out_grad, 1, 1).astype(bf16)
        swap.wait_send()

    return pl.pallas_call(
        kernel,
        out_shape=[
            shape_of((TOK, D), f32),
            shape_of((TOK, D), bf16),
            shape_of((4, 192, TOK), bf16),
            shape_of((24, D + 128), f32),
            shape_of((1, 16, TOK), f32),
        ],
        in_specs=in_vmem(13),
        out_specs=in_vmem(5),
        scratch_shapes=[
            pltpu.VMEM((TOK, D), f32),
            pltpu.VMEM((1, EXPERTS * CAP), f32),
            pltpu.VMEM((TOK, HALF), bf16),
            pltpu.VMEM((TOK, HALF), bf16),
            pltpu.SemaphoreType.DMA,
            pltpu.SemaphoreType.DMA,
        ],
        compiler_params=comm_params(7),
        name="middle_backward",
    )(slot_grads, hit, g_halves, hidden, normed, table, vectors, routers, dots, plan, prev, residual, wo)


def key_ids(ids_ref, place, block, tile):
    return ids_ref[(place["zl"] * 4 + place["x"]) * 8 + 2 * block + tile]


def query_ids(ids_ref, place, chunk):
    row = (place["zl"] * 4 + place["x"]) * 8 + 2 * chunk + place["c"]
    return ids_ref[row, :, pl.ds(pl.multiple_of(place["n"] * TOK, 128), TOK)]


def for_chunks(block, part, whole_chunks, partial_chunk):
    masked = [
        (block, 0, 1),
        (block, 1, jnp.minimum(part, 1)),
        (block - 1, 0, jnp.where((part == 3) & (block > 0), 1, 0)),
    ]
    for chunk, tile, times in masked:

        def body(_, carry, chunk=chunk, tile=tile):
            partial_chunk(chunk, tile)
            return carry

        if isinstance(times, int):
            partial_chunk(chunk, tile)
        else:
            lax.fori_loop(0, times, body, 0)
    yield
    lax.fori_loop(block + 1, 4, lambda j, carry: (whole_chunks(j), carry)[1], 0)
    yield


def attend(queries, pairs, grad_rows, block_ids):
    route_shifts = shifts_of(ROUTE_AXES)
    peers = unique([shifts_of(("y",)), [{"n": 1}], [{"c": 1}], route_shifts])

    def kernel(
        q_in, kv_in, rows_in, ids_ref, at_out, q_out, kv_out, of_ref, lse_ref, rows_out,
        q_now, o_now, top_s, total_s, acc_s,
        q_send, q_recv, y_send, y_recv, n_send, n_recv, c_send, c_recv, o_send, o_recv, r_send, r_recv,
    ):
        place = coords()
        y, c, n = place["y"], place["c"], place["n"]
        part = 2 * c + n
        partner, sibling = moved(place, {"n": 1}), moved(place, {"c": 1})
        me = rank_of(place, ROUTE_AXES)
        kv_out[y, c, n] = kv_in[y]
        q_now[y] = q_in[y]
        greet(place, peers)
        query_copies, row_copies = [], []
        pair_copies, across, beside, onward = {}, {}, {}, {}

        def spread(d):
            spot = kv_out.at[lax.rem(y + 4 - d, 4), c, n]
            across[d] = push(spot, spot, n_send.at[d], n_recv.at[d], partner)
            beside[d] = push(spot, spot, c_send.at[0, d], c_recv.at[0, d], sibling)

        def pass_on(d):
            across[d].wait_recv()
            spot = kv_out.at[lax.rem(y + 4 - d, 4), c, 1 - n]
            onward[d] = push(spot, spot, c_send.at[1, d], c_recv.at[1, d], sibling)

        def send_pairs(d):
            target = lax.rem(y + d, 4)
            pair_copies[d] = push(
                kv_in.at[target], kv_out.at[y, c, n], y_send.at[d], y_recv.at[d], moved(place, {"y": d})
            )

        def send_rows():
            for j, shift in enumerate(route_shifts):
                to = rank_of(place, ROUTE_AXES, shift)
                row_copies.append(
                    push(rows_in.at[to], rows_out.at[me], r_send.at[j], r_recv.at[j], moved(place, shift))
                )
            rows_out[me] = rows_in[me]

        send_pairs(1)
        send_pairs(3)
        spread(0)
        for d in (1, 3, 2):
            target = lax.rem(y + d, 4)
            query_copies.append(
                push(q_in.at[target], q_now.at[y], q_send.at[d], q_recv.at[d], moved(place, {"y": d}))
            )
        send_pairs(2)
        top_s[...] = jnp.full_like(top_s, -1e30)
        total_s[...] = jnp.zeros_like(total_s)
        acc_s[...] = jnp.zeros_like(acc_s)
        q_out[...] = jnp.zeros_like(q_out)
        pass_on(0)
        for d in (1, 3):
            pair_copies[d].wait_recv()
            spread(d)
        for copy in query_copies:
            copy.wait_recv()
        for j in range(4):
            for h in range(3):
                q_out[j, h, :HEAD_DIM, :] = q_now[j, h * HEAD_DIM : (h + 1) * HEAD_DIM, :] * 0.125

        def update(j, block, tiles, masked):
            if masked:
                allowed = [to_column(key_ids(ids_ref, place, block, t)) <= query_ids(ids_ref, place, j) for t in tiles]
            k_tiles = {}
            scores = {}
            for h in range(3):
                lanes = slice(h * 128, (h + 1) * 128)
                for t in tiles:
                    k_tiles[h, t] = kv_out[block, t, :, :, lanes].reshape(KT, 128)
                    scores[h, t] = dot_dims(k_tiles[h, t], q_out[j, h], 1, 0)
            state = []
            for h in range(3):
                mine = [scores[h, t] for t in tiles]
                if masked:
                    mine = [jnp.where(a, s, -1e30) for a, s in zip(allowed, mine)]
                old = top_s[j, h]
                top = old
                for s in mine:
                    top = jnp.maximum(top, jnp.max(s, axis=0, keepdims=True))
                decay = jnp.exp(old - top)
                total = total_s[j, h] * decay
                acc = acc_s[j, h] * decay
                for t, s in zip(tiles, mine):
                    p = jnp.exp(s - top)
                    total = total + jnp.sum(p, axis=0, keepdims=True)
                    acc = acc + dot_dims(k_tiles[h, t], p.astype(bf16), 0, 0)
                state.append((top, total, acc))
            for h in range(3):
                top_s[j, h], total_s[j, h], acc_s[j, h] = state[h]

        def second_pairs():
            pair_copies[2].wait_recv()
            spread(2)
            pass_on(1)
            send_rows()

        between = {0: second_pairs, 1: lambda: pass_on(3), 3: lambda: pass_on(2), 2: lambda: None}
        for d in (0, 1, 3, 2):
            beside[d].wait_recv()
            onward[d].wait_recv()
            block = lax.rem(y + 4 - d, 4)
            halves = for_chunks(
                block,
                part,
                lambda j, block=block: update(j, block, (0, 1), False),
                lambda j, t, block=block: update(j, block, (t,), True),
            )
            next(halves)
            between[d]()
            next(halves)

        out_copies = []
        for d in (2, 1, 3, 0):
            j = lax.rem(y + d, 4)
            for h in range(3):
                total = total_s[j, h]
                span = slice(h * HEAD_DIM, (h + 1) * HEAD_DIM)
                out = acc_s[j, h, HEAD_DIM:, :] * (1.0 / total)
                of_ref[j, span, :] = out
                o_now[j, span, :] = out.astype(bf16)
                lse_ref[j, h] = top_s[j, h] + jnp.log(total)
            if d:
                out_copies.append(
                    push(o_now.at[j], at_out.at[y], o_send.at[d], o_recv.at[d], moved(place, {"y": d}))
                )
            else:
                at_out[y] = o_now[y]
        for copy in out_copies + row_copies:
            copy.wait_recv()
        sent = query_copies + list(pair_copies.values()) + row_copies + out_copies
        for copy in sent + list(across.values()) + list(beside.values()) + list(onward.values()):
            copy.wait_send()

    four = pltpu.SemaphoreType.DMA((4,))
    return pl.pallas_call(
        kernel,
        out_shape=[
            shape_of((4, 192, TOK), bf16),
            shape_of((4, 3, 128, TOK), bf16),
            shape_of((4, 2, 2, TOK, HALF), bf16),
            shape_of((4, 192, TOK), f32),
            shape_of((4, 3, 1, TOK), f32),
            shape_of(grad_rows.shape, bf16),
        ],
        in_specs=in_vmem(4),
        out_specs=in_vmem(6),
        scratch_shapes=[
            pltpu.VMEM((4, 192, TOK), bf16),
            pltpu.VMEM((4, 192, TOK), bf16),
            pltpu.VMEM((4, 3, 1, TOK), f32),
            pltpu.VMEM((4, 3, 1, TOK), f32),
            pltpu.VMEM((4, 3, 128, TOK), f32),
            four,
            four,
            four,
            four,
            four,
            four,
            pltpu.SemaphoreType.DMA((2, 4)),
            pltpu.SemaphoreType.DMA((2, 4)),
            four,
            four,
            pltpu.SemaphoreType.DMA((len(route_shifts),)),
            pltpu.SemaphoreType.DMA((len(route_shifts),)),
        ],
        compiler_params=comm_params(2),
        name="attend",
    )(queries, pairs, grad_rows, block_ids)


def attend_backward(grads, queries, pairs, attended, logs, block_ids, out_rows, small, weight_sums, swaps_in):
    extra = len(swaps_in)
    route_shifts = shifts_of(ROUTE_AXES)
    peers = unique([shifts_of(("y",)), shifts_of(("x",)), shifts_of(("z",)), [{"c": 1}], route_shifts])
    turns = ("c", "x", "y", "z")
    order = (1, 3, 2, 0)

    def kernel(*refs):
        g_in, q_ref, kv_ref, of_ref, lse_ref, ids_ref, rows_in, small_in, sums_ref = refs[:9]
        ins = refs[9 : 9 + extra]
        dq_out, dkv_out, rows_out, small_out, sum_out, sum_other = refs[9 + extra : 15 + extra]
        swapped = refs[15 + extra : 15 + 2 * extra]
        (
            g_now, g_pad, delta_s, dq_acc, dq_now, acc, own_sum, to_sibling, from_sibling, to_other, from_other, kept, ready,
            small_now, small_in_flight, g_send, g_recv, c_send, c_recv, n_send, n_recv, y_send, y_recv,
            q_send, q_recv, r_send, r_recv, s_send, s_recv, p_send, p_recv, sum_in, w_send, w_recv, own_sem,
        ) = refs[15 + 2 * extra :]
        place = coords()
        y, c, n = place["y"], place["c"], place["n"]
        part = 2 * c + n
        partner, sibling = moved(place, {"n": 1}), moved(place, {"c": 1})
        me = rank_of(place, ROUTE_AXES)
        greet(place, peers)
        grad_copies, row_copies = [], []
        for d in (2, 1, 3):
            target = lax.rem(y + d, 4)
            grad_copies.append(
                push(g_in.at[target], g_now.at[y], g_send.at[d], g_recv.at[d], moved(place, {"y": d}))
            )
        g_now[y] = g_in[y]
        small_now[0] = small_in[...]

        def small_start(turn):
            axis = turns[turn]
            return [
                push(
                    small_now.at[turn],
                    small_in_flight.at[turn, d],
                    s_send.at[turn, d],
                    s_recv.at[turn, d],
                    moved(place, {axis: d + 1}),
                )
                for d in range(SIZES[axis] - 1)
            ]

        def small_end(turn, copies):
            total = small_now[turn]
            for d, copy in enumerate(copies):
                copy.wait_recv()
                total = total + small_in_flight[turn, d]
            if turn < 3:
                small_now[turn + 1] = total
            else:
                small_out[...] = total

        small_copies = [small_start(0)]
        swaps = swap_start(place, swaps_in, ins, swapped, p_send, p_recv)
        for j, shift in enumerate(route_shifts):
            to = rank_of(place, ROUTE_AXES, shift)
            row_copies.append(
                push(rows_in.at[to], rows_out.at[me], r_send.at[j], r_recv.at[j], moved(place, shift))
            )
        rows_out[me] = rows_in[me]
        dq_acc[...] = jnp.zeros_like(dq_acc)
        g_pad[...] = jnp.zeros_like(g_pad)
        for copy in grad_copies:
            copy.wait_recv()
        weight_copies = []
        for d in (1, 3):
            for i in range(2):
                weight_copies.append(
                    push(
                        sums_ref.at[(d + 1) // 2, i], sum_in.at[d // 2, i], w_send.at[d // 2, i], w_recv.at[d // 2, i],
                        moved(place, {"y": d}),
                    )
                )
        own_load = pltpu.make_async_copy(sums_ref.at[0], own_sum, own_sem)
        own_load.start()
        for j in range(4):
            inner = g_now[j].astype(f32) * of_ref[j]
            for h in range(3):
                span = slice(h * HEAD_DIM, (h + 1) * HEAD_DIM)
                g_pad[j, h, HEAD_DIM:, :] = g_now[j, span, :]
                delta_s[j, h] = jnp.sum(inner[span, :], axis=0, keepdims=True)

        def update(j, block, tiles, masked):
            if masked:
                allowed = {t: to_column(key_ids(ids_ref, place, block, t)) <= query_ids(ids_ref, place, j) for t in tiles}
            places = [(t, h) for t in tiles for h in range(3)]
            k_tiles, scores, grads, both, dq = {}, {}, {}, {}, {}
            for t, h in places:
                k = kv_ref[block, t, :, :, h * 128 : (h + 1) * 128].reshape(KT, 128)
                k_tiles[t, h] = k
                scores[t, h] = dot_dims(k, q_ref[j, h], 1, 0)
                grads[t, h] = dot_dims(k, g_pad[j, h], 1, 0)
            for t, h in places:
                p = jnp.exp(scores[t, h] - lse_ref[j, h])
                if masked:
                    p = jnp.where(allowed[t], p, 0.0)
                ds = (p * (grads[t, h] - delta_s[j, h])).astype(bf16)
                both[t, h] = dot_dims(ds, q_ref[j, h], 1, 1) + dot_dims(p.astype(bf16), g_pad[j, h], 1, 1)
                more = dot_dims(k_tiles[t, h], ds, 0, 0)
                dq[h] = dq[h] + more if h in dq else more
            for t, h in places:
                acc[t, :, :, h * 128 : (h + 1) * 128] += both[t, h].reshape(2, TOK, 128)
            for h in range(3):
                dq_acc[j, h] += dq[h]

        beside, across, homeward = {}, {}, []

        def send_beside(d):
            to_sibling[d] = acc[1 - c].astype(bf16)
            beside[d] = push(to_sibling.at[d], from_sibling.at[d], c_send.at[d], c_recv.at[d], sibling)
            kept[d] = acc[c]

        def send_across(d):
            beside[d].wait_recv()
            to_other[d] = (kept[d, 1 - n] + from_sibling[d, 1 - n].astype(f32)).astype(bf16)
            across[d] = push(to_other.at[d], from_other.at[d], n_send.at[d], n_recv.at[d], partner)

        def send_home(d):
            across[d].wait_recv()
            total = kept[d, n] + from_sibling[d, n].astype(f32) + from_other[d].astype(f32)
            if d:
                ready[d] = total.astype(bf16)
                homeward.append(
                    push(ready.at[d], dkv_out.at[y], y_send.at[d], y_recv.at[d], moved(place, {"y": d}))
                )
            else:
                dkv_out[y] = total.astype(bf16)

        for step, d in enumerate(order):
            block = lax.rem(y + d, 4)
            acc[...] = jnp.zeros_like(acc)
            halves = for_chunks(
                block,
                part,
                lambda j, block=block: update(j, block, (0, 1), False),
                lambda j, t, block=block: update(j, block, (t,), True),
            )
            next(halves)
            if step:
                send_across(order[step - 1])
                small_end(step - 1, small_copies[step - 1])
                small_copies.append(small_start(step))
            if step > 1:
                send_home(order[step - 2])
            next(halves)
            send_beside(d)
        query_copies = []
        for d in (2, 1, 3, 0):
            j = lax.rem(y + d, 4)
            grad = jnp.concatenate([dq_acc[j, h, :HEAD_DIM, :] for h in range(3)], axis=0)
            grad = (grad * 0.125).astype(bf16)
            if d:
                dq_now[j] = grad
                query_copies.append(
                    push(dq_now.at[j], dq_out.at[y], q_send.at[d], q_recv.at[d], moved(place, {"y": d}))
                )
            else:
                dq_out[y] = grad
        send_home(order[2])
        send_across(order[3])
        small_end(3, small_copies[3])
        send_home(order[3])
        for copy in weight_copies:
            copy.wait_recv()
        own_load.wait()
        totals = []
        for i in range(2):
            total = own_sum[i].astype(f32) + sum_in[0, i].astype(f32) + sum_in[1, i].astype(f32)
            totals.append(total.astype(bf16))
        sum_out[...] = jnp.where(n == 0, totals[0], totals[1])
        sum_other[...] = jnp.where(n == 0, totals[1], totals[0])
        for copy in homeward + query_copies + row_copies + swaps:
            copy.wait_recv()
        sent = grad_copies + row_copies + swaps + query_copies + homeward + weight_copies
        for copy in sent + list(beside.values()) + list(across.values()):
            copy.wait_send()
        for copies in small_copies:
            for copy in copies:
                copy.wait_send()

    four = pltpu.SemaphoreType.DMA((4,))
    return pl.pallas_call(
        kernel,
        out_shape=[
            shape_of((4, 192, TOK), bf16),
            shape_of((4, TOK, HALF), bf16),
            shape_of(out_rows.shape, bf16),
            shape_of(small.shape, f32),
            shape_of(weight_sums.shape[2:], bf16),
            shape_of(weight_sums.shape[2:], bf16),
        ]
        + swap_shapes(swaps_in),
        in_specs=in_vmem(8) + [pl.BlockSpec(memory_space=pl.ANY)] + in_vmem(extra),
        out_specs=in_vmem(6 + extra),
        scratch_shapes=[
            pltpu.VMEM((4, 192, TOK), bf16),
            pltpu.VMEM((4, 3, 128, TOK), bf16),
            pltpu.VMEM((4, 3, 1, TOK), f32),
            pltpu.VMEM((4, 3, 128, TOK), f32),
            pltpu.VMEM((4, 192, TOK), bf16),
            pltpu.VMEM((2, 2, TOK, HALF), f32),
            pltpu.VMEM(weight_sums.shape[1:], bf16),
            pltpu.VMEM((4, 2, TOK, HALF), bf16),
            pltpu.VMEM((4, 2, TOK, HALF), bf16),
            pltpu.VMEM((4, TOK, HALF), bf16),
            pltpu.VMEM((4, TOK, HALF), bf16),
            pltpu.VMEM((4, 2, TOK, HALF), f32),
            pltpu.VMEM((4, TOK, HALF), bf16),
            pltpu.VMEM((4,) + small.shape, f32),
            pltpu.VMEM((4, 3) + small.shape, f32),
        ]
        + [four] * 10
        + [pltpu.SemaphoreType.DMA((len(route_shifts),))] * 2
        + [pltpu.SemaphoreType.DMA((4, 3))] * 2
        + [pltpu.SemaphoreType.DMA((extra,))] * 2
        + [pltpu.VMEM((2,) + weight_sums.shape[1:], bf16)]
        + [pltpu.SemaphoreType.DMA((2, 2))] * 2
        + [pltpu.SemaphoreType.DMA],
        compiler_params=comm_params(3),
        name="attend_backward",
    )(
        grads, queries, pairs, attended, logs, block_ids, out_rows, small, weight_sums,
        *[a for a, _ in swaps_in],
    )


def project_backward(
    dq_ref, dkv_ref, pq_ref, proj_ref, inv_ref, scaled_ref, wq_ref, x_ref, vec_ref, hg_ref, at_ref, og_ref,
    pa, pb, pc, grad_ref, gain_ref, dw_s, dwo_s,
):
    inv = inv_ref[...]
    scaled = scaled_ref[...]
    dscaled = jnp.zeros((TOK, D), f32)
    dinv = jnp.zeros((TOK, 192), f32)
    dinv_row = jnp.zeros((1, TOK), f32)
    inv_row = to_row(inv)
    for s in range(3):
        for y in range(4):
            first = s * D + y * 192
            if s == 0:
                d = dq_ref[y].astype(f32)
                dinv_row = dinv_row + jnp.sum(d * pq_ref[y], axis=0, keepdims=True)
                dproject = (inv_row * d).astype(bf16)
                dscaled = dscaled + dot_dims(dproject, wq_ref[first : first + 192, :], 0, 0)
                dw_s[first : first + 192, :] = dot_dims(dproject, scaled, 1, 0)
                continue
            d = jnp.concatenate(
                [
                    dkv_ref[y, :, h * 128 + (s - 1) * HEAD_DIM : h * 128 + s * HEAD_DIM]
                    for h in range(3)
                ],
                axis=1,
            ).astype(f32)
            dinv = dinv + d * proj_ref[(s - 1) * 4 + y]
            dproject = (inv * d).astype(bf16)
            dscaled = dscaled + dot_dims(dproject, wq_ref[first : first + 192, :], 1, 0)
            dw_s[first : first + 192, :] = dot_dims(dproject, scaled, 0, 0)
    for y in range(4):
        dwo_s[y * 192 : (y + 1) * 192, :] = dot_dims(at_ref[y], og_ref[...], 1, 0)
    for w, cols, spots in blocks_of_weights():
        pa[spots[0]] = dw_s[w * 36 : w * 36 + 16, cols].astype(bf16)
        pb[spots[1]] = dw_s[w * 36 + 16 : w * 36 + 32, cols].astype(bf16)
        pc[spots[2]] = jnp.concatenate(
            [dw_s[w * 36 + 32 : w * 36 + 36, cols], dwo_s[w * 12 : w * 12 + 12, cols]], axis=0
        ).astype(bf16)
    x = jnp.concatenate([x_ref[0], x_ref[1]], axis=1).astype(f32)
    gain = jnp.concatenate([vec_ref[0, 0:1], vec_ref[1, 0:1]], axis=1).astype(f32)
    gain_ref[0] = jnp.zeros_like(gain_ref[0])
    gain_ref[0, 0:1, :] = jnp.sum(dscaled * x, axis=0, keepdims=True)
    dinv = jnp.sum(dinv, axis=1, keepdims=True) + to_column(dinv_row)
    grad = hg_ref[...] + dscaled * gain - (dinv * (inv * inv * inv) / D) * x
    for half in range(2):
        grad_ref[half] = grad[:, half * HALF : (half + 1) * HALF].astype(bf16)


def scatter_sums(given):
    swaps_in = [(shape_of((2, TOK, HALF), bf16), 1)]
    small = shape_of((8, D), f32)
    extra = len(swaps_in)
    peers = unique([shifts_of((a,)) for a in ("x", "y", "z", "c")])
    turns = ("c", "x", "y", "z")
    count = len(given)

    def kernel(*refs):
        block_out, small_out = refs[count : count + 2]
        swapped = refs[count + 2 : count + 2 + extra]
        rest = refs[count + 2 + extra :]
        parts_in, grad_s, dw_s, dwo_s = rest[:3], rest[3], rest[4], rest[5]
        rest = rest[6:]
        from_sibling, sum_three, sum_two, sum_one = rest[0:3], rest[3:6], rest[6:9], rest[9:12]
        in_three, in_two, in_one = rest[12:15], rest[15:18], rest[18:21]
        (
            small_now,
            small_in_flight,
            c_send,
            c_recv,
            send,
            recv,
            s_send,
            s_recv,
            p_send,
            p_recv,
        ) = rest[21:]
        place = coords()
        core = place["c"]
        ins = (grad_s,)
        greet_start(place, peers)
        project_backward(*refs[:count], *parts_in, grad_s, small_now, dw_s, dwo_s)
        greet_end(peers)
        beside = []
        for j in range(4):
            for k in range(3):
                third = lax.rem(place[ORDERS[k][2]] + (j + 1), 4)
                beside.append(
                    push(
                        parts_in[k].at[1 - core, third],
                        from_sibling[k].at[third],
                        c_send.at[k, j],
                        c_recv.at[k, j],
                        moved(place, {"c": 1}),
                    )
                )

        def small_start(turn):
            axis = turns[turn]
            return [
                push(
                    small_now.at[turn],
                    small_in_flight.at[turn, d],
                    s_send.at[turn, d],
                    s_recv.at[turn, d],
                    moved(place, {axis: d + 1}),
                )
                for d in range(SIZES[axis] - 1)
            ]

        def small_end(turn, copies):
            total = small_now[turn]
            for d, copy in enumerate(copies):
                copy.wait_recv()
                total = total + small_in_flight[turn, d]
            if turn < 3:
                small_now[turn + 1] = total
            else:
                small_out[...] = total

        small_copies = [small_start(0)]
        threes = [[] for _ in range(3)]
        for j in range(4):
            for k in range(3):
                third = lax.rem(place[ORDERS[k][2]] + (j + 1), 4)
                beside[j * 3 + k].wait_recv()
                sum_three[k][third] = (
                    parts_in[k][core, third].astype(f32) + from_sibling[k][third].astype(f32)
                ).astype(bf16)
                if j < 3:
                    threes[k].append(
                        push(
                            sum_three[k].at[third],
                            in_three[k].at[j],
                            send.at[k, 0, j],
                            recv.at[k, 0, j],
                            moved(place, {ORDERS[k][2]: j + 1}),
                        )
                    )
        swaps = swap_start(place, swaps_in, ins, swapped, p_send, p_recv)
        small_end(0, small_copies[0])
        small_copies.append(small_start(1))
        twos = [[] for _ in range(3)]
        for k in range(3):
            for copy in threes[k]:
                copy.wait_recv()
            third = place[ORDERS[k][2]]
            total = sum_three[k][third].astype(f32)
            for j in range(3):
                total = total + in_three[k][j].astype(f32)
            sum_two[k][...] = total.astype(bf16)
            for j in range(3):
                second = lax.rem(place[ORDERS[k][1]] + (j + 1), 4)
                twos[k].append(
                    push(
                        sum_two[k].at[second],
                        in_two[k].at[j],
                        send.at[k, 1, j],
                        recv.at[k, 1, j],
                        moved(place, {ORDERS[k][1]: j + 1}),
                    )
                )
        small_end(1, small_copies[1])
        small_copies.append(small_start(2))
        ones = [[] for _ in range(3)]
        for k in range(3):
            for copy in twos[k]:
                copy.wait_recv()
            second = place[ORDERS[k][1]]
            total = sum_two[k][second].astype(f32)
            for j in range(3):
                total = total + in_two[k][j].astype(f32)
            sum_one[k][...] = total.astype(bf16)
            for j in range(3):
                first = lax.rem(place[ORDERS[k][0]] + (j + 1), 4)
                ones[k].append(
                    push(
                        sum_one[k].at[first],
                        in_one[k].at[j],
                        send.at[k, 2, j],
                        recv.at[k, 2, j],
                        moved(place, {ORDERS[k][0]: j + 1}),
                    )
                )
        small_end(2, small_copies[2])
        small_copies.append(small_start(3))
        for k in range(3):
            for copy in ones[k]:
                copy.wait_recv()
            first = place[ORDERS[k][0]]
            total = sum_one[k][first].astype(f32)
            for j in range(3):
                total = total + in_one[k][j].astype(f32)
            block_out[k * PART : (k + 1) * PART, :] = total
        small_end(3, small_copies[3])
        for copy in swaps:
            copy.wait_recv()
        for copy in beside + swaps:
            copy.wait_send()
        for k in range(3):
            for copy in threes[k] + twos[k] + ones[k]:
                copy.wait_send()
        for copies in small_copies:
            for copy in copies:
                copy.wait_send()

    three = pltpu.VMEM((4, 4, 4, PART, HALF), bf16)
    two = pltpu.VMEM((4, 4, PART, HALF), bf16)
    one = pltpu.VMEM((4, PART, HALF), bf16)
    return pl.pallas_call(
        kernel,
        out_shape=[shape_of((3 * PART, HALF), f32), small] + swap_shapes(swaps_in),
        in_specs=in_vmem(count),
        out_specs=in_vmem(2 + extra),
        scratch_shapes=[pltpu.VMEM((2, 4, 4, 4, PART, HALF), bf16)] * 3
        + [pltpu.VMEM((2, TOK, HALF), bf16), pltpu.VMEM((3 * D, D), f32), pltpu.VMEM((D, D), f32)]
        + [three] * 3
        + [three] * 3
        + [two] * 3
        + [one] * 3
        + [pltpu.VMEM((3, 4, 4, PART, HALF), bf16)] * 3
        + [pltpu.VMEM((3, 4, PART, HALF), bf16)] * 3
        + [pltpu.VMEM((3, PART, HALF), bf16)] * 3
        + [
            pltpu.VMEM((4,) + small.shape, f32),
            pltpu.VMEM((4, 3) + small.shape, f32),
            pltpu.SemaphoreType.DMA((3, 4)),
            pltpu.SemaphoreType.DMA((3, 4)),
            pltpu.SemaphoreType.DMA((3, 3, 3)),
            pltpu.SemaphoreType.DMA((3, 3, 3)),
            pltpu.SemaphoreType.DMA((4, 3)),
            pltpu.SemaphoreType.DMA((4, 3)),
            pltpu.SemaphoreType.DMA((extra,)),
            pltpu.SemaphoreType.DMA((extra,)),
        ],
        compiler_params=comm_params(4),
        name="scatter_sums",
    )(*given)


def finish(grad_block, gain_sum, grad_halves, small, grad_prev, expert_sums, base, out_slots, hit):
    def kernel(
        block_ref, gain_ref, halves_ref, small_ref, prev_ref, s0_ref, s1_ref, s2_ref, s3_ref, base_ref, slots_ref, hit_ref,
        layer_out, g_inputs, g_prev, g_gain_one, g_qkv, g_out, g_gain_two, g_router, g_residual, g_const, g_vec,
        g_gate, g_up, g_down,
    ):
        n = lax.axis_index("n")
        cols = pl.ds(pl.multiple_of(n * HALF, 128), HALF)
        mixture = dot_dims(hit_ref[...], slots_ref[...].reshape(EXPERTS * CAP, HALF), 0, 0)
        for side in range(2):
            span = slice(side * TOK, (side + 1) * TOK)
            layer_out[span, :] = (base_ref[side].astype(f32) + mixture[span, :]).astype(bf16)
            g_inputs[span, :] = halves_ref[side].astype(f32)
            g_prev[:, span] = prev_ref[side, :ROUTES, :]
        g_gain_one[...] = gain_ref[0:1, cols]
        block = block_ref[...]
        g_qkv[...] = block[:36, :]
        g_out[...] = block[36:48, :]
        g_router[...] = small_ref[:ROUTES, cols]
        g_const[...] = small_ref[ROUTES:16, cols]
        g_vec[...] = small_ref[16:18, cols]
        g_gain_two[...] = small_ref[18:19, cols]
        g_residual[...] = small_ref[0:ROUTES, D : D + ROUTES]
        for i, target in enumerate((g_gate, g_up, g_down)):
            total = sum(ref[i].astype(f32) for ref in (s0_ref, s1_ref, s2_ref, s3_ref))
            target[...] = total if i < 2 else total.T

    shapes = [
        shape_of((2 * TOK, HALF), bf16),
        shape_of((2 * TOK, HALF), f32),
        shape_of((ROUTES, 2 * TOK), f32),
        shape_of((1, HALF), f32),
        shape_of((36, HALF), f32),
        shape_of((12, HALF), f32),
        shape_of((1, HALF), f32),
        shape_of((ROUTES, HALF), f32),
        shape_of((ROUTES, ROUTES), f32),
        shape_of((4, HALF), f32),
        shape_of((2, HALF), f32),
        shape_of((HALF, 256), f32),
        shape_of((HALF, 256), f32),
        shape_of((256, HALF), f32),
    ]
    return pl.pallas_call(
        kernel,
        out_shape=shapes,
        in_specs=in_vmem(12),
        out_specs=in_vmem(len(shapes)),
        compiler_params=pltpu.CompilerParams(vmem_limit_bytes=VMEM_LIMIT),
        name="finish",
    )(grad_block, gain_sum, grad_halves, small, grad_prev, *expert_sums, base, out_slots, hit)


def shards(
    inputs,
    block_ids,
    expert_ids,
    prev_scores,
    gain_one,
    w_qkv,
    w_out,
    gain_two,
    w_router,
    w_residual,
    w_const,
    const_vec,
    w_gate,
    w_up,
    w_down,
    cotangent,
):
    expert_block = jnp.stack([w_gate, w_up, w_down.T])
    weights = lax.all_gather(expert_block, ("n", "y", "c"), axis=0, tiled=False).reshape(2, 8, 3, HALF, 256)

    *parts, x_halves, g_halves, vectors, routers, hit, plan, grad_rows = gather_all(
        w_qkv.T,
        w_out,
        inputs.reshape(2, TOK, HALF),
        cotangent.reshape(2, TOK, HALF),
        [gain_one[None], gain_two[None], const_vec],
        [w_router.T, w_const.T],
        expert_ids.T,
    )
    wq, wo, queries, pairs, project_q, project, scaled, inv_one = project_forward(parts, x_halves, vectors)
    blocks = block_ids.reshape(64, 1, 512)
    prev = prev_scores.T
    attended, queries, pairs, attended_f, logs, grad_rows = attend(queries, pairs, grad_rows, blocks)
    hidden, normed, base, table, out_rows, slot_grads, dots, weight_sums, far, far_other = experts_step(
        attended, x_halves, wo, vectors, routers, prev, w_residual, plan, hit, grad_rows, weights
    )
    two_on = [(i, (i + 2) % 4) for i in range(4)]
    far = lax.ppermute(far, "y", two_on)
    far_other = lax.ppermute(
        far_other, ("n", "y"), [(4 * k + i, 4 * (1 - k) + j) for k in range(2) for i, j in two_on]
    )
    hidden_grad, out_grad, heads_grad, small, grad_prev = middle_backward(
        slot_grads, hit, g_halves, hidden, normed, table, vectors, routers, dots, plan, prev, w_residual, wo
    )
    dq, dkv, out_slots, small, near, near_other, grad_prev, base = attend_backward(
        heads_grad, queries, pairs, attended_f, logs, blocks, out_rows, small, weight_sums,
        [(grad_prev, 2), (base, 1)],
    )
    near_other = lax.ppermute(near_other, "n", [(0, 1), (1, 0)])
    grad_block, gain_sum, grad_halves = scatter_sums(
        [
            dq, dkv, project_q, project, inv_one, scaled, wq, x_halves, vectors, hidden_grad, attended, out_grad,
        ]
    )
    outputs = finish(
        grad_block, gain_sum, grad_halves, small, grad_prev, (near, near_other, far, far_other), base, out_slots, hit
    )
    turned = {2, 4, 7, 9}
    return tuple(
        out.reshape(HALF) if i in (3, 6) else out.T if i in turned else out for i, out in enumerate(outputs)
    )


def solution(mesh):
    fine = Mesh(mesh.devices.reshape(2, 2, 4, 4, 2), AXES)
    return jax.shard_map(
        shards,
        mesh=fine,
        in_specs=(
            P(WIDE, "n"),
            P(),
            P(WIDE, None),
            P(WIDE, None),
            P("n"),
            P("n", WIDE),
            P(WIDE, "n"),
            P("n"),
            P("n", None),
            P(),
            P("n", None),
            P(None, "n"),
            P("n", WIDE),
            P("n", WIDE),
            P(WIDE, "n"),
            P(WIDE, "n"),
        ),
        out_specs=(
            P(WIDE, "n"),
            P(WIDE, "n"),
            P(WIDE, None),
            P("n"),
            P("n", WIDE),
            P(WIDE, "n"),
            P("n"),
            P("n", None),
            P(),
            P("n", None),
            P(None, "n"),
            P("n", WIDE),
            P("n", WIDE),
            P(WIDE, "n"),
        ),
        check_vma=False,
    )
```

```python
import functools
import math

import jax
import jax.numpy as jnp
from jax import lax
from jax.experimental import pallas as pl
from jax.experimental.pallas import tpu as pltpu
from jax.sharding import Mesh
from jax.sharding import PartitionSpec as P

HEAD_DIM = 64
EXPERTS = 8
ROUTES = 12
CAP = 128
D = 768
HALF = 384
TOK = 256
SEQ = 4096
KT = 512

MESH = pl.DeviceIdType.MESH
AXES = ("n", "zl", "x", "y", "c")
SIZES = dict(n=2, zl=2, x=4, y=4, c=2, z=4)
WIDE = ("zl", "x", "y", "c")
VMEM_LIMIT = 60 * 1024 * 1024

epsilon = 1e-06
highest = lax.Precision.HIGHEST
f32 = jnp.float32
bf16 = jnp.bfloat16


def exact_dot(left_side, right_side):
    return jnp.dot(left_side, right_side, precision=highest, preferred_element_type=f32)


def dot_dims(left_side, right_side, left_dim, right_dim):
    return lax.dot_general(
        left_side, right_side, (((left_dim,), (right_dim,)), ((), ())), preferred_element_type=f32
    )


def pair_softmax(logit_pairs):
    pair_top = jnp.max(logit_pairs, axis=-1, keepdims=True)
    pair_exp = jnp.exp(logit_pairs - pair_top)
    return pair_exp / jnp.sum(pair_exp, axis=-1, keepdims=True)


def coords():
    place = {axis: lax.axis_index(axis) for axis in AXES}
    place["z"] = place["n"] * 2 + place["zl"]
    return place


def moved(place, shift):
    target = {}
    for axis, steps in shift.items():
        value = lax.rem(place[axis] + steps, SIZES[axis])
        if axis == "z":
            target["n"] = value // 2
            target["zl"] = lax.rem(value, 2)
        else:
            target[axis] = value
    return target


def shifts_of(axes):
    found = [{}]
    for axis in axes:
        found = [dict(one, **{axis: k}) for one in found for k in range(SIZES[axis])]
    return [{a: k for a, k in one.items() if k} for one in found if any(one.values())]


def reverse(shift):
    return {axis: (SIZES[axis] - steps) % SIZES[axis] for axis, steps in shift.items()}


def rank_of(place, axes, shift=None):
    rank = 0
    for axis in axes:
        value = place[axis]
        if shift and axis in shift:
            value = lax.rem(value + shift[axis], SIZES[axis])
        rank = rank * SIZES[axis] + value
    return rank


def greet_start(place, shifts):
    barrier = pltpu.get_barrier_semaphore()
    for shift in shifts:
        pl.semaphore_signal(barrier, inc=1, device_id=moved(place, shift), device_id_type=MESH)


def greet_end(shifts):
    pl.semaphore_wait(pltpu.get_barrier_semaphore(), len(shifts))


def greet(place, shifts):
    greet_start(place, shifts)
    greet_end(shifts)


def push(source, target, send_sem, recv_sem, device):
    copy = pltpu.make_async_remote_copy(
        src_ref=source,
        dst_ref=target,
        send_sem=send_sem,
        recv_sem=recv_sem,
        device_id=device,
        device_id_type=MESH,
    )
    copy.start()
    return copy


def in_vmem(count):
    return [pl.BlockSpec(memory_space=pltpu.VMEM)] * count


def comm_params(collective_id):
    return pltpu.CompilerParams(
        collective_id=collective_id, has_side_effects=True, vmem_limit_bytes=VMEM_LIMIT
    )


def shape_of(shape, dtype):
    return jax.ShapeDtypeStruct(shape, dtype)


def unique(shift_lists):
    seen = []
    for shifts in shift_lists:
        for shift in shifts:
            if shift not in seen:
                seen.append(shift)
    return seen


def diagonal(size):
    rows = lax.broadcasted_iota(jnp.int32, (size, size), 0)
    return rows == lax.broadcasted_iota(jnp.int32, (size, size), 1)


def to_row(value):
    size = value.shape[0]
    return jnp.sum(jnp.where(diagonal(size), value, jnp.zeros_like(value)), axis=0, keepdims=True)


def to_column(value):
    size = min(value.shape[1], 128)
    mask = diagonal(size)
    return jnp.concatenate(
        [
            jnp.sum(
                jnp.where(mask, value[:, k * size : (k + 1) * size], jnp.zeros((), value.dtype)),
                axis=1,
                keepdims=True,
            )
            for k in range(value.shape[1] // size)
        ],
        axis=0,
    )


ORDERS = (("x", "y", "z"), ("y", "z", "x"), ("z", "x", "y"))
PART = 16


def make_plan(ids_ref, cot_ref, hit_ref, table_ref, rows_ref):
    tokens = 2 * TOK
    expert = lax.broadcasted_iota(jnp.int32, (tokens, 128), 1)
    ids = [to_column(ids_ref[k : k + 1, :]) for k in range(2)]
    table_ref[...] = jnp.zeros_like(table_ref)
    named = ((expert == ids[0]) | (expert == ids[1])).astype(bf16)
    before = lax.broadcasted_iota(jnp.int32, (tokens, tokens), 1) < lax.broadcasted_iota(
        jnp.int32, (tokens, tokens), 0
    )
    ranks = dot_dims(before.astype(bf16), named, 1, 0)
    slot = lax.broadcasted_iota(jnp.int32, (CAP * 2, tokens), 0)
    rows = []
    for k in range(2):
        rank = jnp.sum(jnp.where(expert == ids[k], ranks, 0.0), axis=1, keepdims=True)
        place = jnp.where(ids[k] < EXPERTS, ids[k] * CAP + rank.astype(jnp.int32), -1)
        table_ref[:, k : k + 1] = ids[k]
        table_ref[:, 2 + k : 3 + k] = place
        rows.append(to_row(place))
    for j in range(4):
        first = j * 2 * CAP
        hit = ((slot + first == rows[0]) | (slot + first == rows[1])).astype(bf16)
        hit_ref[first : first + 2 * CAP, :] = hit
        held = dot_dims(hit[:, :TOK], cot_ref[0], 1, 0) + dot_dims(hit[:, TOK:], cot_ref[1], 1, 0)
        held = held.astype(bf16)
        for i in range(4):
            rows_ref[j * 4 + i] = held[i * 64 : (i + 1) * 64, :]


def swap_shapes(swaps_in):
    return [shape_of((2,) + a.shape[1:], a.dtype) for a, _ in swaps_in]


def swap_start(place, swaps_in, ins, swapped, send, recv):
    n = place["n"]
    copies = []
    for i, (_, share) in enumerate(swaps_in):
        copies.append(
            push(ins[i].at[(1 - n) // share], swapped[i].at[n], send.at[i], recv.at[i], moved(place, {"z": 2}))
        )
        swapped[i][n] = ins[i][n // share]
    return copies


def blocks_of_weights():
    for zl in range(2):
        for x in range(4):
            for y in range(4):
                for c in range(2):
                    for n in range(2):
                        at = dict(x=x, y=y, z=2 * n + zl)
                        spots = [(c, at[o[2]], at[o[1]], at[o[0]]) for o in ORDERS]
                        yield ((zl * 4 + x) * 4 + y) * 2 + c, slice(n * HALF, (n + 1) * HALF), spots


def project_forward(
    parts, x_ref, vec_ref, wq_ref, wo_ref, q_ref, kv_ref, pq_ref, proj_ref, scaled_ref, inv_ref, wq_s, wo_s
):
    for w, cols, spots in blocks_of_weights():
        blocks = [parts[k][spots[k]].astype(f32) for k in range(3)]
        wq_s[w * 36 : w * 36 + 16, cols] = blocks[0]
        wq_s[w * 36 + 16 : w * 36 + 32, cols] = blocks[1]
        wq_s[w * 36 + 32 : w * 36 + 36, cols] = blocks[2][:4]
        wo_s[w * 12 : w * 12 + 12, cols] = blocks[2][4:]
    for j in range(9):
        wq_ref[j * 256 : (j + 1) * 256, :] = wq_s[j * 256 : (j + 1) * 256, :].astype(bf16)
    for j in range(3):
        wo_ref[j * 256 : (j + 1) * 256, :] = wo_s[j * 256 : (j + 1) * 256, :].astype(bf16)
    x = jnp.concatenate([x_ref[0], x_ref[1]], axis=1).astype(f32)
    gain = jnp.concatenate([vec_ref[0, 0:1], vec_ref[1, 0:1]], axis=1).astype(f32)
    inv = lax.rsqrt(jnp.mean(x * x, axis=1, keepdims=True) + epsilon)
    scaled = (x * gain).astype(bf16)
    scaled_ref[...] = scaled
    inv_ref[...] = inv
    inv_row = to_row(inv)
    for s in range(3):
        for y in range(4):
            first = s * D + y * 192
            if s == 0:
                project = dot_dims(wq_ref[first : first + 192, :], scaled, 1, 1)
                pq_ref[y] = project
                q_ref[y] = (inv_row * project).astype(bf16)
            else:
                project = dot_dims(scaled, wq_ref[first : first + 192, :], 1, 1)
                proj_ref[(s - 1) * 4 + y] = project
                value = (inv * project).astype(bf16)
                for h in range(3):
                    spot = h * 128 + (s - 1) * HEAD_DIM
                    kv_ref[y, :, spot : spot + HEAD_DIM] = value[:, h * HEAD_DIM : (h + 1) * HEAD_DIM]


SCALARS = ("inv", "gate0", "gate1", "a00", "a01", "a10", "a11", "cw0", "cw1", "self", "vec0", "vec1")
RAW = 32


def column(table, name):
    spot = SCALARS.index(name)
    return table[:, spot : spot + 1]


def vector_rows(vec_ref, first, count):
    both = [vec_ref[half, first : first + count].astype(f32) for half in range(2)]
    return jnp.concatenate(both, axis=1)


def exact_dims(left_side, right_side, left_dim, right_dim):
    return lax.dot_general(
        left_side,
        right_side,
        (((left_dim,), (right_dim,)), ((), ())),
        precision=highest,
        preferred_element_type=f32,
    )


def router_table(rc_ref):
    return jnp.concatenate([rc_ref[half, :, :16].astype(f32) for half in range(2)], axis=0)


def middle_forward(
    own_tokens, at_ref, x_ref, wo_ref, vec_ref, rc_ref, prev_ref, res_ref, plan_ref,
    hidden_ref, normed_ref, base_ref, table_ref, gates_ref,
):
    hidden = jnp.concatenate([x_ref[0], x_ref[1]], axis=1).astype(f32)
    for y in range(4):
        hidden = hidden + dot_dims(at_ref[y], wo_ref[y * 192 : (y + 1) * 192, :], 0, 0)
    hidden_ref[...] = hidden
    gain = vector_rows(vec_ref, 1, 1)
    inv = lax.rsqrt(jnp.mean(hidden * hidden, axis=1, keepdims=True) + epsilon)
    weighted = hidden * gain
    normed = (hidden * inv * gain).astype(bf16)
    normed_ref[...] = normed
    raw = exact_dims(weighted, router_table(rc_ref), 1, 0)
    logits = inv * raw[:, :ROUTES] + exact_dims(prev_ref[:, own_tokens], res_ref[...].astype(f32), 0, 0)
    route = lax.broadcasted_iota(jnp.int32, (TOK, ROUTES), 1)
    e0, e1 = plan_ref[own_tokens, 0:1], plan_ref[own_tokens, 1:2]
    l0 = jnp.sum(jnp.where(route == e0, logits, 0.0), axis=1, keepdims=True)
    l1 = jnp.sum(jnp.where(route == e1, logits, 0.0), axis=1, keepdims=True)

    def softmax_two(first, second):
        top = jnp.maximum(first, second)
        a, b = jnp.exp(first - top), jnp.exp(second - top)
        return a / (a + b), b / (a + b)

    gate0, gate1 = softmax_two(l0, l1)
    coeff = [inv * raw[:, ROUTES + i : ROUTES + i + 1] for i in range(4)]
    a00, a01 = softmax_two(coeff[0], coeff[1])
    a10, a11 = softmax_two(coeff[2], coeff[3])

    def chosen(expert):
        return jnp.where(e0 == expert, gate0, 0.0) + jnp.where(e1 == expert, gate1, 0.0)

    cw0, cw1 = chosen(EXPERTS + 2), chosen(EXPERTS + 3)
    own = chosen(EXPERTS + 1) + cw0 * a00 + cw1 * a10
    vec0, vec1 = cw0 * a01, cw1 * a11
    const = vector_rows(vec_ref, 2, 2)
    base = hidden + own * normed.astype(f32) + vec0 * const[0:1] + vec1 * const[1:2]
    for half in range(2):
        base_ref[half] = base[:, half * HALF : (half + 1) * HALF].astype(bf16)
    values = dict(
        inv=inv, gate0=gate0, gate1=gate1, a00=a00, a01=a01, a10=a10, a11=a11, cw0=cw0, cw1=cw1,
        self=own, vec0=vec0, vec1=vec1,
    )
    lane = lax.broadcasted_iota(jnp.int32, (TOK, 128), 1)
    table = jnp.zeros((TOK, 128), f32)
    for i, name in enumerate(SCALARS):
        table = jnp.where(lane == i, values[name], table)
    table_ref[...] = table
    table_ref[:, RAW : RAW + 16] = raw
    slot = lax.broadcasted_iota(jnp.int32, (TOK, EXPERTS * CAP), 1)
    s0, s1 = plan_ref[own_tokens, 2:3], plan_ref[own_tokens, 3:4]
    slot_gates = jnp.where(slot == s0, gate0, 0.0) + jnp.where(slot == s1, gate1, 0.0)
    slot_gates = jnp.sum(slot_gates, axis=0, keepdims=True)
    gates_ref[...] = jnp.zeros_like(gates_ref)
    for b in range(16):
        gates_ref[b, 0:1, 0:64] = slot_gates[:, b * 64 : (b + 1) * 64]


ROUTE_AXES = ("zl", "x", "n")


def experts_step(attended, x_halves, wo, vectors, routers, prev, residual, plan, hit, grad_rows, weights):
    shifts = shifts_of(ROUTE_AXES)
    count = len(shifts)
    rows = 2 * TOK
    one = weights.shape[2:]
    peers = unique([shifts, [{"c": 1}]])

    def kernel(
        at_ref, x_ref, wo_ref, vec_ref, rc_ref, prev_ref, res_ref, plan_ref, hit_ref, gr_ref, w_hbm,
        hidden_ref, normed_ref, base_ref, table_ref, out_ref, slots_ref, dots_out, dw_hbm,
        gates_s, sending, half, row_s, arrived, gates_in, w, dw, x, xt, g, gate_col, dy, dyt, acts, acts_in,
        x_in, dy_in, xt_in, dyt_in, dx_acc, out_acc, dx_s, dot_s, p_send, p_recv,
        w_sem, c_send, c_recv, dw_sem, x_send, x_recv, a_send, a_recv, g_send, g_recv, r_send, r_recv, b_send, b_recv, d_send, d_recv,
    ):
        place = coords()
        n, c = place["n"], place["c"]
        me = rank_of(place, ROUTE_AXES)
        sibling = moved(place, {"c": 1})
        greet_start(place, peers)
        places = [(k, i) for k in range(4) for i in range(2)]
        loads = [pltpu.make_async_copy(w_hbm.at[i, k], w.at[i, 2 * k + c], w_sem.at[k, i]) for k, i in places]
        for load in loads:
            load.start()
        greet_end(peers)
        beside = [
            push(w_hbm.at[i, k], w.at[i, 2 * k + c], c_send.at[k, i], c_recv.at[k, i], sibling) for k, i in places
        ]
        own_tokens = pl.ds(pl.multiple_of(n * TOK, 128), TOK)
        middle_forward(
            own_tokens, at_ref, x_ref, wo_ref, vec_ref, rc_ref, prev_ref, res_ref, plan_ref,
            hidden_ref, normed_ref, base_ref, table_ref, gates_s,
        )
        sending[...] = normed_ref[:, pl.ds(pl.multiple_of((1 - n) * HALF, 128), HALF)]
        swap = push(sending, half.at[n], p_send, p_recv, moved(place, {"n": 1}))
        copies = []
        for j, shift in enumerate(shifts):
            to = rank_of(place, ROUTE_AXES, shift)
            copies.append(push(gates_s.at[to], gates_in.at[me], g_send.at[j], g_recv.at[j], moved(place, shift)))
        half[n] = normed_ref[:, pl.ds(pl.multiple_of(n * HALF, 128), HALF)]
        gates_in[me] = gates_s[me]
        for source in range(8):
            for side in range(2):
                g[source * 64 : (source + 1) * 64, side * HALF : (side + 1) * HALF] = gr_ref[2 * source + side]
        swap.wait_recv()
        for e in range(4):
            span = slice(e * 256, (e + 1) * 256)
            block = dot_dims(hit_ref[span, :TOK], half[0], 1, 0) + dot_dims(hit_ref[span, TOK:], half[1], 1, 0)
            block = block.astype(bf16)
            for i in range(4):
                row_s[e * 4 + i] = block[i * 64 : (i + 1) * 64, :]
        for j, shift in enumerate(shifts):
            to = rank_of(place, ROUTE_AXES, shift)
            copies.append(push(row_s.at[to], arrived.at[me], r_send.at[j], r_recv.at[j], moved(place, shift)))
        arrived[me] = row_s[me]
        for copy in copies[:count]:
            copy.wait_recv()
        for source in range(8):
            both = gates_in[2 * source, 0:1, 0:64] + gates_in[2 * source + 1, 0:1, 0:64]
            gate_col[source * 64 : (source + 1) * 64, :] = to_column(both)
        dffn = (g[...].astype(f32) * gate_col[...]).astype(bf16)
        dy[...] = dffn
        dyt[...] = dffn.T
        dx_acc[...] = jnp.zeros_like(dx_acc)
        out_acc[...] = jnp.zeros_like(out_acc)
        for copy in copies[count:]:
            copy.wait_recv()
        for source in range(8):
            for side in range(2):
                x[source * 64 : (source + 1) * 64, side * HALF : (side + 1) * HALF] = arrived[2 * source + side]
        row_copies = [
            push(x, x_in, x_send.at[0], x_recv.at[0], sibling),
            push(dy, dy_in, x_send.at[1], x_recv.at[1], sibling),
        ]
        xt[...] = x[...].T
        sides = (slice(0, HALF), slice(HALF, D))

        def act_copy(k):
            return pltpu.make_async_remote_copy(
                src_ref=acts.at[1 - c, k],
                dst_ref=acts_in.at[k],
                send_sem=a_send.at[k],
                recv_sem=a_recv.at[k],
                device_id=sibling,
                device_id_type=MESH,
            )

        def units_step(core, k):
            p = 2 * k + core
            gate = sum(dot_dims(x[:, s], w[i, p, 0], 1, 0) for i, s in enumerate(sides))
            up = sum(dot_dims(x[:, s], w[i, p, 1], 1, 0) for i, s in enumerate(sides))
            dunits = sum(dot_dims(dy[:, s], w[i, p, 2], 1, 0) for i, s in enumerate(sides))
            sig = 1.0 / (1.0 + jnp.exp(-gate))
            active = gate * sig
            units = (active * up).astype(bf16)
            slope = sig * (1.0 + gate * (1.0 - sig))
            dgate = (dunits * up * slope).astype(bf16)
            dup = (dunits * active).astype(bf16)
            acts[core, k, 0], acts[core, k, 1], acts[core, k, 2] = dgate, dup, units
            for i, s in enumerate(sides):
                out_acc[:, s] += dot_dims(units, w[i, p, 2], 1, 1)
                dx_acc[:, s] += dot_dims(dgate, w[i, p, 0], 1, 1) + dot_dims(dup, w[i, p, 1], 1, 1)

        def their_step(k, carry):
            units_step(1 - c, k)
            act_copy(k).start()
            return carry

        def own_step(k, carry):
            units_step(c, k)
            return carry

        for load in loads:
            load.wait()
        for copy in beside:
            copy.wait_recv()
        lax.fori_loop(0, 4, their_step, 0)
        lax.fori_loop(0, 4, own_step, 0)
        dot_s[...] = jnp.zeros_like(dot_s)
        for source in range(8):
            span = slice(source * 64, (source + 1) * 64)
            for side in range(2):
                dx_s[2 * source + side] = dx_acc[span, sides[side]].astype(bf16)
        back = []
        for j, shift in enumerate(shifts):
            to = rank_of(place, ROUTE_AXES, shift)
            back.append(push(dx_s.at[to], slots_ref.at[me], b_send.at[j], b_recv.at[j], moved(place, shift)))
        for source in range(8):
            span = slice(source * 64, (source + 1) * 64)
            dots = jnp.sum(g[span, :].astype(f32) * out_acc[span, :], axis=1, keepdims=True)
            dot_s[source, 0:1, 0:64] = to_row(dots)
        for j, shift in enumerate(shifts):
            to = rank_of(place, ROUTE_AXES, shift)
            back.append(push(dot_s.at[to // 2], dots_out.at[me], d_send.at[j], d_recv.at[j], moved(place, shift)))
        slots_ref[me] = dx_s[me]
        dots_out[me] = dot_s[me // 2]
        for source in range(8):
            span = slice(source * 64, (source + 1) * 64)
            for side in range(2):
                out_ref[2 * source + side] = (out_acc[span, sides[side]] * gate_col[span, :]).astype(bf16)

        for copy in row_copies:
            copy.wait_recv()
        xt_in[...] = x_in[...].T
        dyt_in[...] = dy_in[...].T
        stores = []
        for k in range(4):
            act_copy(k).wait_recv()
            for i, s in enumerate(sides):
                for j, (mine, theirs) in enumerate(((xt, xt_in), (xt, xt_in), (dyt, dyt_in))):
                    total = dot_dims(mine[s, :], acts[c, k, j], 1, 0) + dot_dims(theirs[s, :], acts_in[k, j], 1, 0)
                    dw[i, k, j] = total.astype(bf16)
                store = pltpu.make_async_copy(dw.at[i, k], dw_hbm.at[i, k], dw_sem.at[i, k])
                store.start()
                stores.append(store)
        for copy in back:
            copy.wait_recv()
        for copy in copies + back + beside + row_copies:
            copy.wait_send()
        for k in range(4):
            act_copy(k).wait_send()
        swap.wait_send()
        for store in stores:
            store.wait()

    route = pltpu.SemaphoreType.DMA((count,))
    return pl.pallas_call(
        kernel,
        out_shape=[
            shape_of((TOK, D), f32),
            shape_of((TOK, D), bf16),
            shape_of((2, TOK, HALF), bf16),
            shape_of((TOK, 128), f32),
            shape_of((16, 64, HALF), bf16),
            shape_of((16, 64, HALF), bf16),
            shape_of((16, 8, 128), f32),
            shape_of((2, 4) + one, bf16),
        ],
        in_specs=in_vmem(10) + [pl.BlockSpec(memory_space=pl.ANY)],
        out_specs=in_vmem(7) + [pl.BlockSpec(memory_space=pl.ANY)],
        scratch_shapes=[
            pltpu.VMEM((16, 8, 128), f32),
            pltpu.VMEM((TOK, HALF), bf16),
            pltpu.VMEM((2, TOK, HALF), bf16),
            pltpu.VMEM((16, 64, HALF), bf16),
            pltpu.VMEM((16, 64, HALF), bf16),
            pltpu.VMEM((16, 8, 128), f32),
            pltpu.VMEM((2, 8) + one, bf16),
            pltpu.VMEM((2, 4) + one, bf16),
            pltpu.VMEM((rows, D), bf16),
            pltpu.VMEM((D, rows), bf16),
            pltpu.VMEM((rows, D), bf16),
            pltpu.VMEM((rows, 1), f32),
            pltpu.VMEM((rows, D), bf16),
            pltpu.VMEM((D, rows), bf16),
            pltpu.VMEM((2, 4, 3, rows, 256), bf16),
            pltpu.VMEM((4, 3, rows, 256), bf16),
            pltpu.VMEM((rows, D), bf16),
            pltpu.VMEM((rows, D), bf16),
            pltpu.VMEM((D, rows), bf16),
            pltpu.VMEM((D, rows), bf16),
            pltpu.VMEM((rows, D), f32),
            pltpu.VMEM((rows, D), f32),
            pltpu.VMEM((16, 64, HALF), bf16),
            pltpu.VMEM((8, 8, 128), f32),
            pltpu.SemaphoreType.DMA,
            pltpu.SemaphoreType.DMA,
            pltpu.SemaphoreType.DMA((4, 2)),
            pltpu.SemaphoreType.DMA((4, 2)),
            pltpu.SemaphoreType.DMA((4, 2)),
            pltpu.SemaphoreType.DMA((2, 4)),
            pltpu.SemaphoreType.DMA((2,)),
            pltpu.SemaphoreType.DMA((2,)),
            pltpu.SemaphoreType.DMA((4,)),
            pltpu.SemaphoreType.DMA((4,)),
        ]
        + [route] * 8,
        compiler_params=comm_params(6),
        name="experts_step",
    )(attended, x_halves, wo, vectors, routers, prev, residual, plan, hit, grad_rows, weights)


def middle_backward(slot_grads, hit, g_halves, hidden, normed, table, vectors, routers, dots, plan, prev, residual, wo):
    def kernel(
        rows_ref, hit_ref, g_ref, hidden_ref, normed_ref, table_ref, vec_ref, rc_ref, dots_ref, plan_ref, prev_ref,
        res_ref, wo_ref, hg_ref, og_ref, heads_ref, small_ref, gprev_ref, dn, row, sending, other, p_send, p_recv,
    ):
        place = coords()
        n = place["n"]
        neighbour = [{"n": 1}]
        greet_start(place, neighbour)
        rows = rows_ref[...].reshape(EXPERTS * CAP, HALF)
        theirs = hit_ref[:, pl.ds(pl.multiple_of((1 - n) * TOK, 128), TOK)]
        sending[...] = dot_dims(theirs, rows, 0, 0).astype(bf16)
        greet_end(neighbour)
        swap = push(sending, other, p_send, p_recv, moved(place, {"n": 1}))
        mine = hit_ref[:, pl.ds(pl.multiple_of(n * TOK, 128), TOK)]
        dn[:, pl.ds(pl.multiple_of(n * HALF, 128), HALF)] = dot_dims(mine, rows, 0, 0)
        own_tokens = pl.ds(pl.multiple_of(n * TOK, 128), TOK)
        for b in range(16):
            row[:, b * 64 : (b + 1) * 64] = dots_ref[b, 0:1, 0:64]
        table = table_ref[...]
        val = {name: column(table, name) for name in SCALARS}
        raw = table_ref[:, RAW : RAW + 16]
        g = jnp.concatenate([g_ref[0], g_ref[1]], axis=1).astype(f32)
        hidden = hidden_ref[...]
        gain = vector_rows(vec_ref, 1, 1)
        const = vector_rows(vec_ref, 2, 2)
        weighted = hidden * gain
        normed = normed_ref[...].astype(f32)
        slot = lax.broadcasted_iota(jnp.int32, (TOK, EXPERTS * CAP), 1)
        e0, e1 = plan_ref[own_tokens, 0:1], plan_ref[own_tokens, 1:2]
        dots = row[...]

        def total(array):
            return jnp.sum(array, axis=1, keepdims=True)

        dot_self = total(g * normed)
        dot_vec = [total(g * const[j : j + 1]) for j in range(2)]
        const_dots = [
            val["a00"] * dot_self + val["a01"] * dot_vec[0],
            val["a10"] * dot_self + val["a11"] * dot_vec[1],
        ]

        def gate_dot(expert, places):
            result = total(jnp.where(slot == places, dots, 0.0))
            result = result + jnp.where(expert == EXPERTS + 1, dot_self, 0.0)
            for j in range(2):
                result = result + jnp.where(expert == EXPERTS + 2 + j, const_dots[j], 0.0)
            return result

        d0, d1 = gate_dot(e0, plan_ref[own_tokens, 2:3]), gate_dot(e1, plan_ref[own_tokens, 3:4])
        mean = val["gate0"] * d0 + val["gate1"] * d1
        route = lax.broadcasted_iota(jnp.int32, (TOK, 16), 1)
        grads = jnp.where(route == e0, val["gate0"] * (d0 - mean), 0.0)
        grads = grads + jnp.where(route == e1, val["gate1"] * (d1 - mean), 0.0)
        logits_grad = grads[:, :ROUTES]
        for j in range(2):
            first, second = val["a%d0" % j], val["a%d1" % j]
            weight = val["cw%d" % j]
            da, db = weight * dot_self, weight * dot_vec[j]
            middle = first * da + second * db
            grads = jnp.where(route == ROUTES + 2 * j, first * (da - middle), grads)
            grads = jnp.where(route == ROUTES + 2 * j + 1, second * (db - middle), grads)
        inv = val["inv"]
        scaled_grads = inv * grads
        weighted_grad = exact_dims(scaled_grads, router_table(rc_ref), 1, 1)
        swap.wait_recv()
        dn[:, pl.ds(pl.multiple_of((1 - n) * HALF, 128), HALF)] = other[...].astype(f32)
        normed_grad = dn[...] + val["self"] * g
        inv_grad = total(normed_grad * weighted) + total(grads * raw)
        small_ref[...] = jnp.zeros_like(small_ref)
        small_ref[0:16, :D] = exact_dims(scaled_grads, weighted, 0, 0)
        small_ref[16:17, :D] = jnp.sum(val["vec0"] * g, axis=0, keepdims=True)
        small_ref[17:18, :D] = jnp.sum(val["vec1"] * g, axis=0, keepdims=True)
        small_ref[18:19, :D] = jnp.sum(normed_grad * hidden * inv + weighted_grad * hidden, axis=0, keepdims=True)
        small_ref[0:ROUTES, D : D + ROUTES] = exact_dims(prev_ref[:, own_tokens], logits_grad, 1, 0)
        gprev_ref[...] = jnp.zeros_like(gprev_ref)
        gprev_ref[0, 0:ROUTES, :] = exact_dims(res_ref[...].astype(f32), logits_grad, 1, 1)
        hidden_grad = (
            g
            + normed_grad * inv * gain
            + weighted_grad * gain
            - (inv_grad * (inv * inv * inv) / D) * hidden
        )
        hg_ref[...] = hidden_grad
        out_grad = hidden_grad.astype(bf16)
        og_ref[...] = out_grad
        for y in range(4):
            heads_ref[y] = dot_dims(wo_ref[y * 192 : (y + 1) * 192, :], out_grad, 1, 1).astype(bf16)
        swap.wait_send()

    return pl.pallas_call(
        kernel,
        out_shape=[
            shape_of((TOK, D), f32),
            shape_of((TOK, D), bf16),
            shape_of((4, 192, TOK), bf16),
            shape_of((24, D + 128), f32),
            shape_of((1, 16, TOK), f32),
        ],
        in_specs=in_vmem(13),
        out_specs=in_vmem(5),
        scratch_shapes=[
            pltpu.VMEM((TOK, D), f32),
            pltpu.VMEM((1, EXPERTS * CAP), f32),
            pltpu.VMEM((TOK, HALF), bf16),
            pltpu.VMEM((TOK, HALF), bf16),
            pltpu.SemaphoreType.DMA,
            pltpu.SemaphoreType.DMA,
        ],
        compiler_params=comm_params(7),
        name="middle_backward",
    )(slot_grads, hit, g_halves, hidden, normed, table, vectors, routers, dots, plan, prev, residual, wo)


def key_ids(ids_ref, place, block, tile):
    return ids_ref[(place["zl"] * 4 + place["x"]) * 8 + 2 * block + tile]


def query_ids(ids_ref, place, chunk):
    row = (place["zl"] * 4 + place["x"]) * 8 + 2 * chunk + place["c"]
    return ids_ref[row, :, pl.ds(pl.multiple_of(place["n"] * TOK, 128), TOK)]


def for_chunks(block, part, whole_chunks, partial_chunk):
    masked = [
        (block, 0, 1),
        (block, 1, jnp.minimum(part, 1)),
        (block - 1, 0, jnp.where((part == 3) & (block > 0), 1, 0)),
    ]
    for chunk, tile, times in masked:

        def body(_, carry, chunk=chunk, tile=tile):
            partial_chunk(chunk, tile)
            return carry

        if isinstance(times, int):
            partial_chunk(chunk, tile)
        else:
            lax.fori_loop(0, times, body, 0)
    yield
    lax.fori_loop(block + 1, 4, lambda j, carry: (whole_chunks(j), carry)[1], 0)
    yield


def front(w_qkv, w_out, inputs, cotangent, gains, tables, expert_ids, block_ids, experts):
    swaps_in = [
        (inputs, 1),
        (cotangent, 1),
        (shape_of((1, PART, HALF), bf16), 2),
        (shape_of((1, HALF, 128), bf16), 2),
    ]
    extra = len(swaps_in)
    given = [w_qkv, w_out, inputs, cotangent, expert_ids, *gains, *tables]
    count = len(given)
    route_shifts = shifts_of(ROUTE_AXES)
    peers = unique([shifts_of((a,)) for a in ("x", "y", "z", "c")] + [[{"n": 1}], route_shifts])

    def kernel(*refs):
        qkv_ref, out_ref, in_ref, cot_ref, ids_ref = refs[:5]
        small_refs = refs[5:count]
        bid_ref, wg_ref, wu_ref, wd_ref = refs[count : count + 4]
        rest = refs[count + 4 :]
        swapped = rest[:extra]
        x_out, _, vec_out, _ = swapped
        (
            hit_ref, plan_ref, wo_out, scaled_out, inv_out, at_out, q_out, of_ref, lse_ref, rows_done,
            wq_out, pq_out, proj_out, kv_out, ew_out,
        ) = rest[extra : extra + 15]
        parts = rest[extra + 15 : extra + 18]
        (
            gain_s, table_s, block_s, rows_in, wq_s, wo_s, wq_v, pq_v, proj_v, kv_v, q_in, kv_in,
            q_now, o_now, top_s, total_s, acc_s,
            send, recv, sib_send, sib_recv, swap_send, swap_recv, e_send, e_recv, save_sem,
            q_send, q_recv, y_send, y_recv, n_send, n_recv, c_send, c_recv, o_send, o_recv, r_send, r_recv,
        ) = rest[extra + 18 :]
        ins = (in_ref, cot_ref, gain_s, table_s)
        place = coords()
        y, c, n = place["y"], place["c"], place["n"]
        core = c
        part = 2 * c + n
        partner, sibling = moved(place, {"n": 1}), moved(place, {"c": 1})
        me = rank_of(place, ROUTE_AXES)
        greet_start(place, peers)
        block = jnp.concatenate([qkv_ref[...].astype(f32), out_ref[...].astype(f32)], axis=0)
        block = block.astype(bf16)
        for k in range(3):
            first, second, third = (place[a] for a in ORDERS[k])
            parts[k][core, third, second, first] = block[k * PART : (k + 1) * PART, :]
        rows = [ref[...].astype(f32) for ref in small_refs[: len(gains)]]
        rows.append(jnp.zeros((PART - sum(row.shape[0] for row in rows), HALF), f32))
        gain_s[0] = jnp.concatenate(rows, axis=0).astype(bf16)
        lanes = [ref[...].astype(f32) for ref in small_refs[len(gains) :]]
        lanes.append(jnp.zeros((128 - sum(lane.shape[0] for lane in lanes), HALF), f32))
        table_s[0] = jnp.concatenate(lanes, axis=0).T.astype(bf16)
        block_s[0], block_s[1], block_s[2] = wg_ref[...], wu_ref[...], wd_ref[...].T
        greet_end(peers)
        stages = []
        for k in range(3):
            first, second, third = (place[a] for a in ORDERS[k])
            spot = parts[k].at[core, third, second, first]
            stages.append(
                [
                    push(spot, spot, send.at[k, 0, d], recv.at[k, 0, d], moved(place, {ORDERS[k][0]: d + 1}))
                    for d in range(3)
                ]
            )
        swaps = swap_start(place, swaps_in, ins, swapped, swap_send, swap_recv)
        later = []
        for k in range(3):
            first, second, third = (place[a] for a in ORDERS[k])
            for copy in stages[k]:
                copy.wait_recv()
            spot = parts[k].at[core, third, second]
            later.append(
                [
                    push(spot, spot, send.at[k, 1, d], recv.at[k, 1, d], moved(place, {ORDERS[k][1]: d + 1}))
                    for d in range(3)
                ]
            )
        last, gather_beside = [], []
        for k in range(3):
            third = place[ORDERS[k][2]]
            for copy in later[k]:
                copy.wait_recv()
            spot = parts[k].at[core, third]
            last.append(
                [
                    push(spot, spot, send.at[k, 2, d], recv.at[k, 2, d], moved(place, {ORDERS[k][2]: d + 1}))
                    for d in range(3)
                ]
            )
            gather_beside.append(push(spot, spot, sib_send.at[k, 0], sib_recv.at[k, 0], sibling))
        other_half = push(block_s, ew_out.at[n, y], e_send.at[0, 0], e_recv.at[0, 0], partner)
        bulk = [
            push(block_s, ew_out.at[n, y], e_send.at[0, d], e_recv.at[0, d], moved(place, {"y": d}))
            for d in (1, 3, 2)
        ]
        keep = pltpu.make_async_copy(block_s, ew_out.at[n, y], save_sem.at[0])
        keep.start()
        make_plan(ids_ref, cot_ref, hit_ref, plan_ref, rows_in)
        for d in range(3):
            for k in range(3):
                third = place[ORDERS[k][2]]
                last[k][d].wait_recv()
                spot = parts[k].at[core, lax.rem(third + 3 - d, 4)]
                gather_beside.append(
                    push(spot, spot, sib_send.at[k, d + 1], sib_recv.at[k, d + 1], sibling)
                )
        for copy in gather_beside + swaps:
            copy.wait_recv()
        project_forward(
            parts, x_out, vec_out, wq_v, wo_out, q_in, kv_in, pq_v, proj_v, scaled_out, inv_out, wq_s, wo_s
        )
        saves = [
            pltpu.make_async_copy(here, there, save_sem.at[i + 1])
            for i, (here, there) in enumerate(((wq_v, wq_out), (pq_v, pq_out), (proj_v, proj_out)))
        ]
        for save in saves:
            save.start()
        kv_v[y, c, n] = kv_in[y]
        q_now[y] = q_in[y]
        query_copies, row_copies = [], []
        pair_copies, across, beside, onward = {}, {}, {}, {}

        def spread(d):
            spot = kv_v.at[lax.rem(y + 4 - d, 4), c, n]
            across[d] = push(spot, spot, n_send.at[d], n_recv.at[d], partner)
            beside[d] = push(spot, spot, c_send.at[0, d], c_recv.at[0, d], sibling)

        def pass_on(d):
            across[d].wait_recv()
            spot = kv_v.at[lax.rem(y + 4 - d, 4), c, 1 - n]
            onward[d] = push(spot, spot, c_send.at[1, d], c_recv.at[1, d], sibling)

        def send_pairs(d):
            target = lax.rem(y + d, 4)
            pair_copies[d] = push(
                kv_in.at[target], kv_v.at[y, c, n], y_send.at[d], y_recv.at[d], moved(place, {"y": d})
            )

        def send_rows():
            for j, shift in enumerate(route_shifts):
                to = rank_of(place, ROUTE_AXES, shift)
                row_copies.append(
                    push(rows_in.at[to], rows_done.at[me], r_send.at[j], r_recv.at[j], moved(place, shift))
                )
            rows_done[me] = rows_in[me]

        send_pairs(1)
        send_pairs(3)
        spread(0)
        for d in (1, 3, 2):
            target = lax.rem(y + d, 4)
            query_copies.append(
                push(q_in.at[target], q_now.at[y], q_send.at[d], q_recv.at[d], moved(place, {"y": d}))
            )
        send_pairs(2)
        top_s[...] = jnp.full_like(top_s, -1e30)
        total_s[...] = jnp.zeros_like(total_s)
        acc_s[...] = jnp.zeros_like(acc_s)
        q_out[...] = jnp.zeros_like(q_out)
        pass_on(0)
        for d in (1, 3):
            pair_copies[d].wait_recv()
            spread(d)
        for copy in query_copies:
            copy.wait_recv()
        for j in range(4):
            for h in range(3):
                q_out[j, h, :HEAD_DIM, :] = q_now[j, h * HEAD_DIM : (h + 1) * HEAD_DIM, :] * 0.125

        def update(j, block, tiles, masked):
            if masked:
                allowed = [to_column(key_ids(bid_ref, place, block, t)) <= query_ids(bid_ref, place, j) for t in tiles]
            k_tiles = {}
            scores = {}
            for h in range(3):
                lanes = slice(h * 128, (h + 1) * 128)
                for t in tiles:
                    k_tiles[h, t] = kv_v[block, t, :, :, lanes].reshape(KT, 128)
                    scores[h, t] = dot_dims(k_tiles[h, t], q_out[j, h], 1, 0)
            state = []
            for h in range(3):
                mine = [scores[h, t] for t in tiles]
                if masked:
                    mine = [jnp.where(a, s, -1e30) for a, s in zip(allowed, mine)]
                old = top_s[j, h]
                top = old
                for s in mine:
                    top = jnp.maximum(top, jnp.max(s, axis=0, keepdims=True))
                decay = jnp.exp(old - top)
                total = total_s[j, h] * decay
                acc = acc_s[j, h] * decay
                for t, s in zip(tiles, mine):
                    p = jnp.exp(s - top)
                    total = total + jnp.sum(p, axis=0, keepdims=True)
                    acc = acc + dot_dims(k_tiles[h, t], p.astype(bf16), 0, 0)
                state.append((top, total, acc))
            for h in range(3):
                top_s[j, h], total_s[j, h], acc_s[j, h] = state[h]

        def second_pairs():
            pair_copies[2].wait_recv()
            spread(2)
            pass_on(1)
            send_rows()
            other_half.wait_recv()
            spot = ew_out.at[1 - n, y]
            for d in (1, 3, 2):
                bulk.append(push(spot, spot, e_send.at[1, d], e_recv.at[1, d], moved(place, {"y": d})))

        between = {0: second_pairs, 1: lambda: pass_on(3), 3: lambda: pass_on(2), 2: lambda: None}
        for d in (0, 1, 3, 2):
            beside[d].wait_recv()
            onward[d].wait_recv()
            block = lax.rem(y + 4 - d, 4)
            halves = for_chunks(
                block,
                part,
                lambda j, block=block: update(j, block, (0, 1), False),
                lambda j, t, block=block: update(j, block, (t,), True),
            )
            next(halves)
            between[d]()
            next(halves)

        save = pltpu.make_async_copy(kv_v, kv_out, save_sem.at[4])
        save.start()
        saves += [save, keep]
        out_copies = []
        for d in (2, 1, 3, 0):
            j = lax.rem(y + d, 4)
            for h in range(3):
                total = total_s[j, h]
                span = slice(h * HEAD_DIM, (h + 1) * HEAD_DIM)
                out = acc_s[j, h, HEAD_DIM:, :] * (1.0 / total)
                of_ref[j, span, :] = out
                o_now[j, span, :] = out.astype(bf16)
                lse_ref[j, h] = top_s[j, h] + jnp.log(total)
            if d:
                out_copies.append(
                    push(o_now.at[j], at_out.at[y], o_send.at[d], o_recv.at[d], moved(place, {"y": d}))
                )
            else:
                at_out[y] = o_now[y]
        for copy in out_copies + row_copies + bulk:
            copy.wait_recv()
        sent = query_copies + list(pair_copies.values()) + row_copies + out_copies
        for copy in sent + list(across.values()) + list(beside.values()) + list(onward.values()):
            copy.wait_send()
        for k in range(3):
            for copy in stages[k] + later[k] + last[k]:
                copy.wait_send()
        for copy in gather_beside + swaps + bulk + [other_half]:
            copy.wait_send()
        for save in saves:
            save.wait()

    four = pltpu.SemaphoreType.DMA((4,))
    any_place = pl.BlockSpec(memory_space=pl.ANY)
    one = (3, HALF, 256)
    return pl.pallas_call(
        kernel,
        out_shape=swap_shapes(swaps_in)
        + [
            shape_of((EXPERTS * CAP, 2 * TOK), bf16),
            shape_of((2 * TOK, 128), jnp.int32),
            shape_of((D, D), bf16),
            shape_of((TOK, D), bf16),
            shape_of((TOK, 1), f32),
            shape_of((4, 192, TOK), bf16),
            shape_of((4, 3, 128, TOK), bf16),
            shape_of((4, 192, TOK), f32),
            shape_of((4, 3, 1, TOK), f32),
            shape_of((16, 64, HALF), bf16),
            shape_of((3 * D, D), bf16),
            shape_of((4, 192, TOK), f32),
            shape_of((8, TOK, 192), f32),
            shape_of((4, 2, 2, TOK, HALF), bf16),
            shape_of((2, 4) + one, bf16),
        ],
        in_specs=in_vmem(count + 4),
        out_specs=in_vmem(extra + 10) + [any_place] * 5,
        scratch_shapes=[pltpu.VMEM((2, 4, 4, 4, PART, HALF), bf16)] * 3
        + [
            pltpu.VMEM((1, PART, HALF), bf16),
            pltpu.VMEM((1, HALF, 128), bf16),
            pltpu.VMEM(one, bf16),
            pltpu.VMEM((16, 64, HALF), bf16),
            pltpu.VMEM((3 * D, D), f32),
            pltpu.VMEM((D, D), f32),
            pltpu.VMEM((3 * D, D), bf16),
            pltpu.VMEM((4, 192, TOK), f32),
            pltpu.VMEM((8, TOK, 192), f32),
            pltpu.VMEM((4, 2, 2, TOK, HALF), bf16),
            pltpu.VMEM((4, 192, TOK), bf16),
            pltpu.VMEM((4, TOK, HALF), bf16),
            pltpu.VMEM((4, 192, TOK), bf16),
            pltpu.VMEM((4, 192, TOK), bf16),
            pltpu.VMEM((4, 3, 1, TOK), f32),
            pltpu.VMEM((4, 3, 1, TOK), f32),
            pltpu.VMEM((4, 3, 128, TOK), f32),
            pltpu.SemaphoreType.DMA((3, 3, 3)),
            pltpu.SemaphoreType.DMA((3, 3, 3)),
            pltpu.SemaphoreType.DMA((3, 4)),
            pltpu.SemaphoreType.DMA((3, 4)),
            four,
            four,
            pltpu.SemaphoreType.DMA((2, 4)),
            pltpu.SemaphoreType.DMA((2, 4)),
            pltpu.SemaphoreType.DMA((5,)),
            four,
            four,
            four,
            four,
            four,
            four,
            pltpu.SemaphoreType.DMA((2, 4)),
            pltpu.SemaphoreType.DMA((2, 4)),
            four,
            four,
            pltpu.SemaphoreType.DMA((len(route_shifts),)),
            pltpu.SemaphoreType.DMA((len(route_shifts),)),
        ],
        compiler_params=comm_params(1),
        name="front",
    )(*given, block_ids, *experts)


def attend_backward(grads, queries, pairs, attended, logs, block_ids, out_rows, small, weight_grads, swaps_in):
    extra = len(swaps_in)
    route_shifts = shifts_of(ROUTE_AXES)
    peers = unique([shifts_of(("y",)), shifts_of(("x",)), shifts_of(("z",)), [{"c": 1}], route_shifts])
    turns = ("c", "x", "y", "z")
    order = (1, 3, 2, 0)

    def kernel(*refs):
        g_in, q_ref, kv_ref, of_ref, lse_ref, ids_ref, rows_in, small_in, dw_ref = refs[:9]
        ins = refs[9 : 9 + extra]
        dq_out, dkv_out, rows_out, small_out, sum_out, sum_other = refs[9 + extra : 15 + extra]
        swapped = refs[15 + extra : 15 + 2 * extra]
        (
            g_now, g_pad, delta_s, dq_acc, dq_now, acc, to_sibling, from_sibling, to_other, from_other, kept, ready,
            small_now, small_in_flight, g_send, g_recv, c_send, c_recv, n_send, n_recv, y_send, y_recv,
            q_send, q_recv, r_send, r_recv, s_send, s_recv, p_send, p_recv, dw_own, dw_in, dw_on, own_sem, w_send, w_recv,
        ) = refs[15 + 2 * extra :]
        place = coords()
        y, c, n = place["y"], place["c"], place["n"]
        part = 2 * c + n
        partner, sibling = moved(place, {"n": 1}), moved(place, {"c": 1})
        me = rank_of(place, ROUTE_AXES)
        greet(place, peers)
        grad_copies, row_copies = [], []
        for d in (2, 1, 3):
            target = lax.rem(y + d, 4)
            grad_copies.append(
                push(g_in.at[target], g_now.at[y], g_send.at[d], g_recv.at[d], moved(place, {"y": d}))
            )
        g_now[y] = g_in[y]
        small_now[0] = small_in[...]

        def small_start(turn):
            axis = turns[turn]
            return [
                push(
                    small_now.at[turn],
                    small_in_flight.at[turn, d],
                    s_send.at[turn, d],
                    s_recv.at[turn, d],
                    moved(place, {axis: d + 1}),
                )
                for d in range(SIZES[axis] - 1)
            ]

        def small_end(turn, copies):
            total = small_now[turn]
            for d, copy in enumerate(copies):
                copy.wait_recv()
                total = total + small_in_flight[turn, d]
            if turn < 3:
                small_now[turn + 1] = total
            else:
                small_out[...] = total

        small_copies = [small_start(0)]
        swaps = swap_start(place, swaps_in, ins, swapped, p_send, p_recv)
        for j, shift in enumerate(route_shifts):
            to = rank_of(place, ROUTE_AXES, shift)
            row_copies.append(
                push(rows_in.at[to], rows_out.at[me], r_send.at[j], r_recv.at[j], moved(place, shift))
            )
        rows_out[me] = rows_in[me]
        dq_acc[...] = jnp.zeros_like(dq_acc)
        g_pad[...] = jnp.zeros_like(g_pad)
        for copy in grad_copies:
            copy.wait_recv()
        ways = (1, 3)
        two_on = lax.rem(y + 2, 4)
        weight_copies = [
            push(dw_ref.at[i, two_on], dw_in.at[0, i], w_send.at[0, i], w_recv.at[0, i], moved(place, {"y": d}))
            for i, d in enumerate(ways)
        ]
        weight_copies += [
            push(
                dw_ref.at[i, lax.rem(y + 4 - d, 4)], dw_in.at[1, i], w_send.at[1, i], w_recv.at[1, i],
                moved(place, {"y": 4 - d}),
            )
            for i, d in enumerate(ways)
        ]
        loads = [
            pltpu.make_async_copy(dw_ref.at[i, lax.rem(y + d * k, 4)], dw_own.at[k, i], own_sem.at[k, i])
            for i, d in enumerate(ways)
            for k in range(2)
        ]
        for load in loads:
            load.start()

        def weights_on():
            for load in loads:
                load.wait()
            for i, d in enumerate(ways):
                weight_copies[i].wait_recv()
                dw_on[i] = (dw_own[1, i].astype(f32) + dw_in[0, i].astype(f32)).astype(bf16)
                weight_copies.append(
                    push(dw_on.at[i], dw_in.at[2, i], w_send.at[2, i], w_recv.at[2, i], moved(place, {"y": d}))
                )

        for j in range(4):
            inner = g_now[j].astype(f32) * of_ref[j]
            for h in range(3):
                span = slice(h * HEAD_DIM, (h + 1) * HEAD_DIM)
                g_pad[j, h, HEAD_DIM:, :] = g_now[j, span, :]
                delta_s[j, h] = jnp.sum(inner[span, :], axis=0, keepdims=True)

        def update(j, block, tiles, masked):
            if masked:
                allowed = {t: to_column(key_ids(ids_ref, place, block, t)) <= query_ids(ids_ref, place, j) for t in tiles}
            places = [(t, h) for t in tiles for h in range(3)]
            k_tiles, scores, grads, both, dq = {}, {}, {}, {}, {}
            for t, h in places:
                k = kv_ref[block, t, :, :, h * 128 : (h + 1) * 128].reshape(KT, 128)
                k_tiles[t, h] = k
                scores[t, h] = dot_dims(k, q_ref[j, h], 1, 0)
                grads[t, h] = dot_dims(k, g_pad[j, h], 1, 0)
            for t, h in places:
                p = jnp.exp(scores[t, h] - lse_ref[j, h])
                if masked:
                    p = jnp.where(allowed[t], p, 0.0)
                ds = (p * (grads[t, h] - delta_s[j, h])).astype(bf16)
                both[t, h] = dot_dims(ds, q_ref[j, h], 1, 1) + dot_dims(p.astype(bf16), g_pad[j, h], 1, 1)
                more = dot_dims(k_tiles[t, h], ds, 0, 0)
                dq[h] = dq[h] + more if h in dq else more
            for t, h in places:
                acc[t, :, :, h * 128 : (h + 1) * 128] += both[t, h].reshape(2, TOK, 128)
            for h in range(3):
                dq_acc[j, h] += dq[h]

        beside, across, homeward = {}, {}, []

        def send_beside(d):
            to_sibling[d] = acc[1 - c].astype(bf16)
            beside[d] = push(to_sibling.at[d], from_sibling.at[d], c_send.at[d], c_recv.at[d], sibling)
            kept[d] = acc[c]

        def send_across(d):
            beside[d].wait_recv()
            to_other[d] = (kept[d, 1 - n] + from_sibling[d, 1 - n].astype(f32)).astype(bf16)
            across[d] = push(to_other.at[d], from_other.at[d], n_send.at[d], n_recv.at[d], partner)

        def send_home(d):
            across[d].wait_recv()
            total = kept[d, n] + from_sibling[d, n].astype(f32) + from_other[d].astype(f32)
            if d:
                ready[d] = total.astype(bf16)
                homeward.append(
                    push(ready.at[d], dkv_out.at[y], y_send.at[d], y_recv.at[d], moved(place, {"y": d}))
                )
            else:
                dkv_out[y] = total.astype(bf16)

        for step, d in enumerate(order):
            block = lax.rem(y + d, 4)
            acc[...] = jnp.zeros_like(acc)
            halves = for_chunks(
                block,
                part,
                lambda j, block=block: update(j, block, (0, 1), False),
                lambda j, t, block=block: update(j, block, (t,), True),
            )
            next(halves)
            if step:
                send_across(order[step - 1])
                small_end(step - 1, small_copies[step - 1])
                small_copies.append(small_start(step))
            if step > 1:
                send_home(order[step - 2])
            if step == 2:
                weights_on()
            next(halves)
            send_beside(d)
        query_copies = []
        for d in (2, 1, 3, 0):
            j = lax.rem(y + d, 4)
            grad = jnp.concatenate([dq_acc[j, h, :HEAD_DIM, :] for h in range(3)], axis=0)
            grad = (grad * 0.125).astype(bf16)
            if d:
                dq_now[j] = grad
                query_copies.append(
                    push(dq_now.at[j], dq_out.at[y], q_send.at[d], q_recv.at[d], moved(place, {"y": d}))
                )
            else:
                dq_out[y] = grad
        send_home(order[2])
        send_across(order[3])
        small_end(3, small_copies[3])
        send_home(order[3])
        for copy in weight_copies[2:]:
            copy.wait_recv()
        totals = []
        for i in range(2):
            total = dw_own[0, i].astype(f32) + dw_in[1, i].astype(f32) + dw_in[2, i].astype(f32)
            totals.append(total.astype(bf16))
        sum_out[...] = jnp.where(n == 0, totals[0], totals[1])
        sum_other[...] = jnp.where(n == 0, totals[1], totals[0])
        for copy in homeward + query_copies + row_copies + swaps:
            copy.wait_recv()
        sent = grad_copies + row_copies + swaps + query_copies + homeward + weight_copies
        for copy in sent + list(beside.values()) + list(across.values()):
            copy.wait_send()
        for copies in small_copies:
            for copy in copies:
                copy.wait_send()

    four = pltpu.SemaphoreType.DMA((4,))
    return pl.pallas_call(
        kernel,
        out_shape=[
            shape_of((4, 192, TOK), bf16),
            shape_of((4, TOK, HALF), bf16),
            shape_of(out_rows.shape, bf16),
            shape_of(small.shape, f32),
            shape_of(weight_grads.shape[2:], bf16),
            shape_of(weight_grads.shape[2:], bf16),
        ]
        + swap_shapes(swaps_in),
        in_specs=in_vmem(8) + [pl.BlockSpec(memory_space=pl.ANY)] + in_vmem(extra),
        out_specs=in_vmem(6 + extra),
        scratch_shapes=[
            pltpu.VMEM((4, 192, TOK), bf16),
            pltpu.VMEM((4, 3, 128, TOK), bf16),
            pltpu.VMEM((4, 3, 1, TOK), f32),
            pltpu.VMEM((4, 3, 128, TOK), f32),
            pltpu.VMEM((4, 192, TOK), bf16),
            pltpu.VMEM((2, 2, TOK, HALF), f32),
            pltpu.VMEM((4, 2, TOK, HALF), bf16),
            pltpu.VMEM((4, 2, TOK, HALF), bf16),
            pltpu.VMEM((4, TOK, HALF), bf16),
            pltpu.VMEM((4, TOK, HALF), bf16),
            pltpu.VMEM((4, 2, TOK, HALF), f32),
            pltpu.VMEM((4, TOK, HALF), bf16),
            pltpu.VMEM((4,) + small.shape, f32),
            pltpu.VMEM((4, 3) + small.shape, f32),
        ]
        + [four] * 10
        + [pltpu.SemaphoreType.DMA((len(route_shifts),))] * 2
        + [pltpu.SemaphoreType.DMA((4, 3))] * 2
        + [pltpu.SemaphoreType.DMA((extra,))] * 2
        + [
            pltpu.VMEM((2, 2) + weight_grads.shape[2:], bf16),
            pltpu.VMEM((3, 2) + weight_grads.shape[2:], bf16),
            pltpu.VMEM((2,) + weight_grads.shape[2:], bf16),
            pltpu.SemaphoreType.DMA((2, 2)),
            pltpu.SemaphoreType.DMA((3, 2)),
            pltpu.SemaphoreType.DMA((3, 2)),
        ],
        compiler_params=comm_params(3),
        name="attend_backward",
    )(
        grads, queries, pairs, attended, logs, block_ids, out_rows, small, weight_grads,
        *[a for a, _ in swaps_in],
    )


def project_backward(
    dq_ref, dkv_ref, pq_ref, proj_ref, inv_ref, scaled_ref, wq_ref, x_ref, vec_ref, hg_ref, at_ref, og_ref,
    pa, pb, pc, grad_ref, gain_ref, dw_s, dwo_s,
):
    inv = inv_ref[...]
    scaled = scaled_ref[...]
    dscaled = jnp.zeros((TOK, D), f32)
    dinv = jnp.zeros((TOK, 192), f32)
    dinv_row = jnp.zeros((1, TOK), f32)
    inv_row = to_row(inv)
    for s in range(3):
        for y in range(4):
            first = s * D + y * 192
            if s == 0:
                d = dq_ref[y].astype(f32)
                dinv_row = dinv_row + jnp.sum(d * pq_ref[y], axis=0, keepdims=True)
                dproject = (inv_row * d).astype(bf16)
                dscaled = dscaled + dot_dims(dproject, wq_ref[first : first + 192, :], 0, 0)
                dw_s[first : first + 192, :] = dot_dims(dproject, scaled, 1, 0)
                continue
            d = jnp.concatenate(
                [
                    dkv_ref[y, :, h * 128 + (s - 1) * HEAD_DIM : h * 128 + s * HEAD_DIM]
                    for h in range(3)
                ],
                axis=1,
            ).astype(f32)
            dinv = dinv + d * proj_ref[(s - 1) * 4 + y]
            dproject = (inv * d).astype(bf16)
            dscaled = dscaled + dot_dims(dproject, wq_ref[first : first + 192, :], 1, 0)
            dw_s[first : first + 192, :] = dot_dims(dproject, scaled, 0, 0)
    for y in range(4):
        dwo_s[y * 192 : (y + 1) * 192, :] = dot_dims(at_ref[y], og_ref[...], 1, 0)
    for w, cols, spots in blocks_of_weights():
        pa[spots[0]] = dw_s[w * 36 : w * 36 + 16, cols].astype(bf16)
        pb[spots[1]] = dw_s[w * 36 + 16 : w * 36 + 32, cols].astype(bf16)
        pc[spots[2]] = jnp.concatenate(
            [dw_s[w * 36 + 32 : w * 36 + 36, cols], dwo_s[w * 12 : w * 12 + 12, cols]], axis=0
        ).astype(bf16)
    x = jnp.concatenate([x_ref[0], x_ref[1]], axis=1).astype(f32)
    gain = jnp.concatenate([vec_ref[0, 0:1], vec_ref[1, 0:1]], axis=1).astype(f32)
    gain_ref[0] = jnp.zeros_like(gain_ref[0])
    gain_ref[0, 0:1, :] = jnp.sum(dscaled * x, axis=0, keepdims=True)
    dinv = jnp.sum(dinv, axis=1, keepdims=True) + to_column(dinv_row)
    grad = hg_ref[...] + dscaled * gain - (dinv * (inv * inv * inv) / D) * x
    for half in range(2):
        grad_ref[half] = grad[:, half * HALF : (half + 1) * HALF].astype(bf16)


def scatter_sums(given, weight_sum):
    swaps_in = [(shape_of((2, TOK, HALF), bf16), 1)]
    small = shape_of((8, D), f32)
    extra = len(swaps_in)
    peers = unique([shifts_of((a,)) for a in ("x", "y", "z", "c")])
    turns = ("c", "x", "y", "z")
    count = len(given)

    def kernel(*refs):
        weight_ref = refs[count]
        block_out, small_out, weight_out = refs[count + 1 : count + 4]
        swapped = refs[count + 4 : count + 4 + extra]
        rest = refs[count + 4 + extra :]
        parts_in, grad_s, dw_s, dwo_s = rest[:3], rest[3], rest[4], rest[5]
        rest = rest[6:]
        from_sibling, sum_three, sum_two, sum_one = rest[0:3], rest[3:6], rest[6:9], rest[9:12]
        in_three, in_two, in_one = rest[12:15], rest[15:18], rest[18:21]
        (
            small_now,
            small_in_flight,
            c_send,
            c_recv,
            send,
            recv,
            s_send,
            s_recv,
            p_send,
            p_recv,
            w_send,
            w_recv,
        ) = rest[21:]
        place = coords()
        core = place["c"]
        ins = (grad_s,)
        greet_start(place, peers)
        greet_end(peers)
        weight_copy = push(weight_ref, weight_out, w_send, w_recv, moved(place, {"z": 2}))
        project_backward(*refs[:count], *parts_in, grad_s, small_now, dw_s, dwo_s)
        beside = []
        for j in range(4):
            for k in range(3):
                third = lax.rem(place[ORDERS[k][2]] + (j + 1), 4)
                beside.append(
                    push(
                        parts_in[k].at[1 - core, third],
                        from_sibling[k].at[third],
                        c_send.at[k, j],
                        c_recv.at[k, j],
                        moved(place, {"c": 1}),
                    )
                )

        def small_start(turn):
            axis = turns[turn]
            return [
                push(
                    small_now.at[turn],
                    small_in_flight.at[turn, d],
                    s_send.at[turn, d],
                    s_recv.at[turn, d],
                    moved(place, {axis: d + 1}),
                )
                for d in range(SIZES[axis] - 1)
            ]

        def small_end(turn, copies):
            total = small_now[turn]
            for d, copy in enumerate(copies):
                copy.wait_recv()
                total = total + small_in_flight[turn, d]
            if turn < 3:
                small_now[turn + 1] = total
            else:
                small_out[...] = total

        small_copies = [small_start(0)]
        threes = [[] for _ in range(3)]
        for j in range(4):
            for k in range(3):
                third = lax.rem(place[ORDERS[k][2]] + (j + 1), 4)
                beside[j * 3 + k].wait_recv()
                sum_three[k][third] = (
                    parts_in[k][core, third].astype(f32) + from_sibling[k][third].astype(f32)
                ).astype(bf16)
                if j < 3:
                    threes[k].append(
                        push(
                            sum_three[k].at[third],
                            in_three[k].at[j],
                            send.at[k, 0, j],
                            recv.at[k, 0, j],
                            moved(place, {ORDERS[k][2]: j + 1}),
                        )
                    )
        swaps = swap_start(place, swaps_in, ins, swapped, p_send, p_recv)
        small_end(0, small_copies[0])
        small_copies.append(small_start(1))
        twos = [[] for _ in range(3)]
        for k in range(3):
            for copy in threes[k]:
                copy.wait_recv()
            third = place[ORDERS[k][2]]
            total = sum_three[k][third].astype(f32)
            for j in range(3):
                total = total + in_three[k][j].astype(f32)
            sum_two[k][...] = total.astype(bf16)
            for j in range(3):
                second = lax.rem(place[ORDERS[k][1]] + (j + 1), 4)
                twos[k].append(
                    push(
                        sum_two[k].at[second],
                        in_two[k].at[j],
                        send.at[k, 1, j],
                        recv.at[k, 1, j],
                        moved(place, {ORDERS[k][1]: j + 1}),
                    )
                )
        small_end(1, small_copies[1])
        small_copies.append(small_start(2))
        ones = [[] for _ in range(3)]
        for k in range(3):
            for copy in twos[k]:
                copy.wait_recv()
            second = place[ORDERS[k][1]]
            total = sum_two[k][second].astype(f32)
            for j in range(3):
                total = total + in_two[k][j].astype(f32)
            sum_one[k][...] = total.astype(bf16)
            for j in range(3):
                first = lax.rem(place[ORDERS[k][0]] + (j + 1), 4)
                ones[k].append(
                    push(
                        sum_one[k].at[first],
                        in_one[k].at[j],
                        send.at[k, 2, j],
                        recv.at[k, 2, j],
                        moved(place, {ORDERS[k][0]: j + 1}),
                    )
                )
        small_end(2, small_copies[2])
        small_copies.append(small_start(3))
        for k in range(3):
            for copy in ones[k]:
                copy.wait_recv()
            first = place[ORDERS[k][0]]
            total = sum_one[k][first].astype(f32)
            for j in range(3):
                total = total + in_one[k][j].astype(f32)
            block_out[k * PART : (k + 1) * PART, :] = total
        small_end(3, small_copies[3])
        for copy in swaps + [weight_copy]:
            copy.wait_recv()
        for copy in beside + swaps + [weight_copy]:
            copy.wait_send()
        for k in range(3):
            for copy in threes[k] + twos[k] + ones[k]:
                copy.wait_send()
        for copies in small_copies:
            for copy in copies:
                copy.wait_send()

    three = pltpu.VMEM((4, 4, 4, PART, HALF), bf16)
    two = pltpu.VMEM((4, 4, PART, HALF), bf16)
    one = pltpu.VMEM((4, PART, HALF), bf16)
    return pl.pallas_call(
        kernel,
        out_shape=[shape_of((3 * PART, HALF), f32), small, shape_of(weight_sum.shape, bf16)] + swap_shapes(swaps_in),
        in_specs=in_vmem(count + 1),
        out_specs=in_vmem(3 + extra),
        scratch_shapes=[pltpu.VMEM((2, 4, 4, 4, PART, HALF), bf16)] * 3
        + [pltpu.VMEM((2, TOK, HALF), bf16), pltpu.VMEM((3 * D, D), f32), pltpu.VMEM((D, D), f32)]
        + [three] * 3
        + [three] * 3
        + [two] * 3
        + [one] * 3
        + [pltpu.VMEM((3, 4, 4, PART, HALF), bf16)] * 3
        + [pltpu.VMEM((3, 4, PART, HALF), bf16)] * 3
        + [pltpu.VMEM((3, PART, HALF), bf16)] * 3
        + [
            pltpu.VMEM((4,) + small.shape, f32),
            pltpu.VMEM((4, 3) + small.shape, f32),
            pltpu.SemaphoreType.DMA((3, 4)),
            pltpu.SemaphoreType.DMA((3, 4)),
            pltpu.SemaphoreType.DMA((3, 3, 3)),
            pltpu.SemaphoreType.DMA((3, 3, 3)),
            pltpu.SemaphoreType.DMA((4, 3)),
            pltpu.SemaphoreType.DMA((4, 3)),
            pltpu.SemaphoreType.DMA((extra,)),
            pltpu.SemaphoreType.DMA((extra,)),
            pltpu.SemaphoreType.DMA,
            pltpu.SemaphoreType.DMA,
        ],
        compiler_params=comm_params(4),
        name="scatter_sums",
    )(*given, weight_sum)


def finish(grad_block, gain_sum, grad_halves, small, grad_prev, expert_sum, expert_other, base, out_slots, hit):
    def kernel(
        block_ref, gain_ref, halves_ref, small_ref, prev_ref, expert_ref, other_ref, base_ref, slots_ref, hit_ref,
        layer_out, g_inputs, g_prev, g_gain_one, g_qkv, g_out, g_gain_two, g_router, g_residual, g_const, g_vec,
        g_gate, g_up, g_down,
    ):
        n = lax.axis_index("n")
        cols = pl.ds(pl.multiple_of(n * HALF, 128), HALF)
        mixture = dot_dims(hit_ref[...], slots_ref[...].reshape(EXPERTS * CAP, HALF), 0, 0)
        for side in range(2):
            span = slice(side * TOK, (side + 1) * TOK)
            layer_out[span, :] = (base_ref[side].astype(f32) + mixture[span, :]).astype(bf16)
            g_inputs[span, :] = halves_ref[side].astype(f32)
            g_prev[:, span] = prev_ref[side, :ROUTES, :]
        g_gain_one[...] = gain_ref[0:1, cols]
        block = block_ref[...]
        g_qkv[...] = block[:36, :]
        g_out[...] = block[36:48, :]
        g_router[...] = small_ref[:ROUTES, cols]
        g_const[...] = small_ref[ROUTES:16, cols]
        g_vec[...] = small_ref[16:18, cols]
        g_gain_two[...] = small_ref[18:19, cols]
        g_residual[...] = small_ref[0:ROUTES, D : D + ROUTES]
        for i, target in enumerate((g_gate, g_up, g_down)):
            total = expert_ref[i].astype(f32) + other_ref[i].astype(f32)
            target[...] = total if i < 2 else total.T

    shapes = [
        shape_of((2 * TOK, HALF), bf16),
        shape_of((2 * TOK, HALF), f32),
        shape_of((ROUTES, 2 * TOK), f32),
        shape_of((1, HALF), f32),
        shape_of((36, HALF), f32),
        shape_of((12, HALF), f32),
        shape_of((1, HALF), f32),
        shape_of((ROUTES, HALF), f32),
        shape_of((ROUTES, ROUTES), f32),
        shape_of((4, HALF), f32),
        shape_of((2, HALF), f32),
        shape_of((HALF, 256), f32),
        shape_of((HALF, 256), f32),
        shape_of((256, HALF), f32),
    ]
    return pl.pallas_call(
        kernel,
        out_shape=shapes,
        in_specs=in_vmem(10),
        out_specs=in_vmem(len(shapes)),
        compiler_params=pltpu.CompilerParams(vmem_limit_bytes=VMEM_LIMIT),
        name="finish",
    )(grad_block, gain_sum, grad_halves, small, grad_prev, expert_sum, expert_other, base, out_slots, hit)


def shards(
    inputs,
    block_ids,
    expert_ids,
    prev_scores,
    gain_one,
    w_qkv,
    w_out,
    gain_two,
    w_router,
    w_residual,
    w_const,
    const_vec,
    w_gate,
    w_up,
    w_down,
    cotangent,
):
    blocks = block_ids.reshape(64, 1, 512)
    prev = prev_scores.T
    (
        x_halves, g_halves, vectors, routers, hit, plan, wo, scaled, inv_one, attended, queries, attended_f, logs,
        grad_rows, wq, project_q, project, pairs, weights,
    ) = front(
        w_qkv.T,
        w_out,
        inputs.reshape(2, TOK, HALF),
        cotangent.reshape(2, TOK, HALF),
        [gain_one[None], gain_two[None], const_vec],
        [w_router.T, w_const.T],
        expert_ids.T,
        blocks,
        [w_gate, w_up, w_down],
    )
    hidden, normed, base, table, out_rows, slot_grads, dots, expert_grads = experts_step(
        attended, x_halves, wo, vectors, routers, prev, w_residual, plan, hit, grad_rows, weights
    )
    hidden_grad, out_grad, heads_grad, small, grad_prev = middle_backward(
        slot_grads, hit, g_halves, hidden, normed, table, vectors, routers, dots, plan, prev, w_residual, wo
    )
    dq, dkv, out_slots, small, expert_sum, expert_other, grad_prev, base = attend_backward(
        heads_grad, queries, pairs, attended_f, logs, blocks, out_rows, small, expert_grads,
        [(grad_prev, 2), (base, 1)],
    )
    grad_block, gain_sum, expert_other, grad_halves = scatter_sums(
        [
            dq, dkv, project_q, project, inv_one, scaled, wq, x_halves, vectors, hidden_grad, attended, out_grad,
        ],
        expert_other,
    )
    outputs = finish(
        grad_block, gain_sum, grad_halves, small, grad_prev, expert_sum, expert_other, base, out_slots, hit
    )
    turned = {2, 4, 7, 9}
    return tuple(
        out.reshape(HALF) if i in (3, 6) else out.T if i in turned else out for i, out in enumerate(outputs)
    )


def solution(mesh):
    fine = Mesh(mesh.devices.reshape(2, 2, 4, 4, 2), AXES)
    return jax.shard_map(
        shards,
        mesh=fine,
        in_specs=(
            P(WIDE, "n"),
            P(),
            P(WIDE, None),
            P(WIDE, None),
            P("n"),
            P("n", WIDE),
            P(WIDE, "n"),
            P("n"),
            P("n", None),
            P(),
            P("n", None),
            P(None, "n"),
            P("n", WIDE),
            P("n", WIDE),
            P(WIDE, "n"),
            P(WIDE, "n"),
        ),
        out_specs=(
            P(WIDE, "n"),
            P(WIDE, "n"),
            P(WIDE, None),
            P("n"),
            P("n", WIDE),
            P(WIDE, "n"),
            P("n"),
            P("n", None),
            P(),
            P("n", None),
            P(None, "n"),
            P("n", WIDE),
            P("n", WIDE),
            P(WIDE, "n"),
        ),
        check_vma=False,
    )
```

```python
import functools
import math

import jax
import jax.numpy as jnp
from jax import lax
from jax.experimental import pallas as pl
from jax.experimental.pallas import tpu as pltpu
from jax.sharding import Mesh
from jax.sharding import PartitionSpec as P

HEAD_DIM = 64
EXPERTS = 8
ROUTES = 12
CAP = 128
D = 768
HALF = 384
TOK = 256
SEQ = 4096
KT = 512

MESH = pl.DeviceIdType.MESH
AXES = ("n", "zl", "x", "y", "c")
SIZES = dict(n=2, zl=2, x=4, y=4, c=2, z=4)
WIDE = ("zl", "x", "y", "c")
VMEM_LIMIT = 60 * 1024 * 1024

epsilon = 1e-06
highest = lax.Precision.HIGHEST
f32 = jnp.float32
bf16 = jnp.bfloat16


def exact_dot(left_side, right_side):
    return jnp.dot(left_side, right_side, precision=highest, preferred_element_type=f32)


def dot_dims(left_side, right_side, left_dim, right_dim):
    return lax.dot_general(
        left_side, right_side, (((left_dim,), (right_dim,)), ((), ())), preferred_element_type=f32
    )


def pair_softmax(logit_pairs):
    pair_top = jnp.max(logit_pairs, axis=-1, keepdims=True)
    pair_exp = jnp.exp(logit_pairs - pair_top)
    return pair_exp / jnp.sum(pair_exp, axis=-1, keepdims=True)


def coords():
    place = {axis: lax.axis_index(axis) for axis in AXES}
    place["z"] = place["n"] * 2 + place["zl"]
    return place


def moved(place, shift):
    target = {}
    for axis, steps in shift.items():
        value = lax.rem(place[axis] + steps, SIZES[axis])
        if axis == "z":
            target["n"] = value // 2
            target["zl"] = lax.rem(value, 2)
        else:
            target[axis] = value
    return target


def shifts_of(axes):
    found = [{}]
    for axis in axes:
        found = [dict(one, **{axis: k}) for one in found for k in range(SIZES[axis])]
    return [{a: k for a, k in one.items() if k} for one in found if any(one.values())]


def reverse(shift):
    return {axis: (SIZES[axis] - steps) % SIZES[axis] for axis, steps in shift.items()}


def rank_of(place, axes, shift=None):
    rank = 0
    for axis in axes:
        value = place[axis]
        if shift and axis in shift:
            value = lax.rem(value + shift[axis], SIZES[axis])
        rank = rank * SIZES[axis] + value
    return rank


def greet_start(place, shifts):
    barrier = pltpu.get_barrier_semaphore()
    for shift in shifts:
        pl.semaphore_signal(barrier, inc=1, device_id=moved(place, shift), device_id_type=MESH)


def greet_end(shifts):
    pl.semaphore_wait(pltpu.get_barrier_semaphore(), len(shifts))


def greet(place, shifts):
    greet_start(place, shifts)
    greet_end(shifts)


def push(source, target, send_sem, recv_sem, device):
    copy = pltpu.make_async_remote_copy(
        src_ref=source,
        dst_ref=target,
        send_sem=send_sem,
        recv_sem=recv_sem,
        device_id=device,
        device_id_type=MESH,
    )
    copy.start()
    return copy


def in_vmem(count):
    return [pl.BlockSpec(memory_space=pltpu.VMEM)] * count


def comm_params(collective_id):
    return pltpu.CompilerParams(
        collective_id=collective_id, has_side_effects=True, vmem_limit_bytes=VMEM_LIMIT
    )


def shape_of(shape, dtype):
    return jax.ShapeDtypeStruct(shape, dtype)


def unique(shift_lists):
    seen = []
    for shifts in shift_lists:
        for shift in shifts:
            if shift not in seen:
                seen.append(shift)
    return seen


def diagonal(size):
    rows = lax.broadcasted_iota(jnp.int32, (size, size), 0)
    return rows == lax.broadcasted_iota(jnp.int32, (size, size), 1)


def to_row(value):
    size = value.shape[0]
    return jnp.sum(jnp.where(diagonal(size), value, jnp.zeros_like(value)), axis=0, keepdims=True)


def to_column(value):
    size = min(value.shape[1], 128)
    mask = diagonal(size)
    return jnp.concatenate(
        [
            jnp.sum(
                jnp.where(mask, value[:, k * size : (k + 1) * size], jnp.zeros((), value.dtype)),
                axis=1,
                keepdims=True,
            )
            for k in range(value.shape[1] // size)
        ],
        axis=0,
    )


ORDERS = (("x", "y", "z"), ("y", "z", "x"), ("z", "x", "y"))
PART = 16


def make_plan(ids_ref, cot_ref, hit_ref, table_ref, rows_ref):
    tokens = 2 * TOK
    expert = lax.broadcasted_iota(jnp.int32, (tokens, 128), 1)
    ids = [to_column(ids_ref[k : k + 1, :]) for k in range(2)]
    table_ref[...] = jnp.zeros_like(table_ref)
    named = ((expert == ids[0]) | (expert == ids[1])).astype(bf16)
    before = lax.broadcasted_iota(jnp.int32, (tokens, tokens), 1) < lax.broadcasted_iota(
        jnp.int32, (tokens, tokens), 0
    )
    ranks = dot_dims(before.astype(bf16), named, 1, 0)
    slot = lax.broadcasted_iota(jnp.int32, (CAP * 2, tokens), 0)
    rows = []
    for k in range(2):
        rank = jnp.sum(jnp.where(expert == ids[k], ranks, 0.0), axis=1, keepdims=True)
        place = jnp.where(ids[k] < EXPERTS, ids[k] * CAP + rank.astype(jnp.int32), -1)
        table_ref[:, k : k + 1] = ids[k]
        table_ref[:, 2 + k : 3 + k] = place
        rows.append(to_row(place))
    for j in range(4):
        first = j * 2 * CAP
        hit = ((slot + first == rows[0]) | (slot + first == rows[1])).astype(bf16)
        hit_ref[first : first + 2 * CAP, :] = hit
        held = dot_dims(hit[:, :TOK], cot_ref[0], 1, 0) + dot_dims(hit[:, TOK:], cot_ref[1], 1, 0)
        held = held.astype(bf16)
        for i in range(4):
            rows_ref[j * 4 + i] = held[i * 64 : (i + 1) * 64, :]


def swap_shapes(swaps_in):
    return [shape_of((2,) + a.shape[1:], a.dtype) for a, _ in swaps_in]


def swap_start(place, swaps_in, ins, swapped, send, recv):
    n = place["n"]
    copies = []
    for i, (_, share) in enumerate(swaps_in):
        copies.append(
            push(ins[i].at[(1 - n) // share], swapped[i].at[n], send.at[i], recv.at[i], moved(place, {"z": 2}))
        )
        swapped[i][n] = ins[i][n // share]
    return copies


def blocks_of_weights():
    for zl in range(2):
        for x in range(4):
            for y in range(4):
                for c in range(2):
                    for n in range(2):
                        at = dict(x=x, y=y, z=2 * n + zl)
                        spots = [(c, at[o[2]], at[o[1]], at[o[0]]) for o in ORDERS]
                        yield ((zl * 4 + x) * 4 + y) * 2 + c, slice(n * HALF, (n + 1) * HALF), spots


def project_forward(
    parts, x_ref, vec_ref, wq_ref, wo_ref, q_ref, kv_ref, pq_ref, proj_ref, scaled_ref, inv_ref, wq_s, wo_s, send_pairs
):
    for w, cols, spots in blocks_of_weights():
        blocks = [parts[k][spots[k]].astype(f32) for k in range(3)]
        wq_s[w * 36 : w * 36 + 16, cols] = blocks[0]
        wq_s[w * 36 + 16 : w * 36 + 32, cols] = blocks[1]
        wq_s[w * 36 + 32 : w * 36 + 36, cols] = blocks[2][:4]
        wo_s[w * 12 : w * 12 + 12, cols] = blocks[2][4:]
    for j in range(9):
        wq_ref[j * 256 : (j + 1) * 256, :] = wq_s[j * 256 : (j + 1) * 256, :].astype(bf16)
    for j in range(3):
        wo_ref[j * 256 : (j + 1) * 256, :] = wo_s[j * 256 : (j + 1) * 256, :].astype(bf16)
    x = jnp.concatenate([x_ref[0], x_ref[1]], axis=1).astype(f32)
    gain = jnp.concatenate([vec_ref[0, 0:1], vec_ref[1, 0:1]], axis=1).astype(f32)
    inv = lax.rsqrt(jnp.mean(x * x, axis=1, keepdims=True) + epsilon)
    scaled = (x * gain).astype(bf16)
    scaled_ref[...] = scaled
    inv_ref[...] = inv
    inv_row = to_row(inv)
    for s in (1, 2, 0):
        if s == 0:
            send_pairs()
        for y in range(4):
            first = s * D + y * 192
            if s == 0:
                project = dot_dims(wq_ref[first : first + 192, :], scaled, 1, 1)
                pq_ref[y] = project
                q_ref[y] = (inv_row * project).astype(bf16)
            else:
                project = dot_dims(scaled, wq_ref[first : first + 192, :], 1, 1)
                proj_ref[(s - 1) * 4 + y] = project
                value = (inv * project).astype(bf16)
                for h in range(3):
                    spot = h * 128 + (s - 1) * HEAD_DIM
                    kv_ref[y, :, spot : spot + HEAD_DIM] = value[:, h * HEAD_DIM : (h + 1) * HEAD_DIM]


SCALARS = ("inv", "gate0", "gate1", "a00", "a01", "a10", "a11", "cw0", "cw1", "self", "vec0", "vec1")
RAW = 32


def column(table, name):
    spot = SCALARS.index(name)
    return table[:, spot : spot + 1]


def vector_rows(vec_ref, first, count):
    both = [vec_ref[half, first : first + count].astype(f32) for half in range(2)]
    return jnp.concatenate(both, axis=1)


def exact_dims(left_side, right_side, left_dim, right_dim):
    return lax.dot_general(
        left_side,
        right_side,
        (((left_dim,), (right_dim,)), ((), ())),
        precision=highest,
        preferred_element_type=f32,
    )


def router_table(rc_ref):
    return jnp.concatenate([rc_ref[half, :, :16].astype(f32) for half in range(2)], axis=0)


def middle_forward(
    own_tokens, send_normed, at_ref, x_ref, wo_ref, vec_ref, rc_ref, prev_ref, res_ref, plan_ref,
    hidden_ref, normed_ref, base_ref, table_ref, gates_ref,
):
    hidden = jnp.concatenate([x_ref[0], x_ref[1]], axis=1).astype(f32)
    for y in range(4):
        hidden = hidden + dot_dims(at_ref[y], wo_ref[y * 192 : (y + 1) * 192, :], 0, 0)
    hidden_ref[...] = hidden
    gain = vector_rows(vec_ref, 1, 1)
    inv = lax.rsqrt(jnp.mean(hidden * hidden, axis=1, keepdims=True) + epsilon)
    weighted = hidden * gain
    normed = (hidden * inv * gain).astype(bf16)
    normed_ref[...] = normed
    send_normed()
    raw = exact_dims(weighted, router_table(rc_ref), 1, 0)
    logits = inv * raw[:, :ROUTES] + exact_dims(prev_ref[:, own_tokens], res_ref[...].astype(f32), 0, 0)
    route = lax.broadcasted_iota(jnp.int32, (TOK, ROUTES), 1)
    e0, e1 = plan_ref[own_tokens, 0:1], plan_ref[own_tokens, 1:2]
    l0 = jnp.sum(jnp.where(route == e0, logits, 0.0), axis=1, keepdims=True)
    l1 = jnp.sum(jnp.where(route == e1, logits, 0.0), axis=1, keepdims=True)

    def softmax_two(first, second):
        top = jnp.maximum(first, second)
        a, b = jnp.exp(first - top), jnp.exp(second - top)
        return a / (a + b), b / (a + b)

    gate0, gate1 = softmax_two(l0, l1)
    coeff = [inv * raw[:, ROUTES + i : ROUTES + i + 1] for i in range(4)]
    a00, a01 = softmax_two(coeff[0], coeff[1])
    a10, a11 = softmax_two(coeff[2], coeff[3])

    def chosen(expert):
        return jnp.where(e0 == expert, gate0, 0.0) + jnp.where(e1 == expert, gate1, 0.0)

    cw0, cw1 = chosen(EXPERTS + 2), chosen(EXPERTS + 3)
    own = chosen(EXPERTS + 1) + cw0 * a00 + cw1 * a10
    vec0, vec1 = cw0 * a01, cw1 * a11
    const = vector_rows(vec_ref, 2, 2)
    base = hidden + own * normed.astype(f32) + vec0 * const[0:1] + vec1 * const[1:2]
    for half in range(2):
        base_ref[half] = base[:, half * HALF : (half + 1) * HALF].astype(bf16)
    values = dict(
        inv=inv, gate0=gate0, gate1=gate1, a00=a00, a01=a01, a10=a10, a11=a11, cw0=cw0, cw1=cw1,
        self=own, vec0=vec0, vec1=vec1,
    )
    lane = lax.broadcasted_iota(jnp.int32, (TOK, 128), 1)
    table = jnp.zeros((TOK, 128), f32)
    for i, name in enumerate(SCALARS):
        table = jnp.where(lane == i, values[name], table)
    table_ref[...] = table
    table_ref[:, RAW : RAW + 16] = raw
    slot = lax.broadcasted_iota(jnp.int32, (TOK, EXPERTS * CAP), 1)
    s0, s1 = plan_ref[own_tokens, 2:3], plan_ref[own_tokens, 3:4]
    slot_gates = jnp.where(slot == s0, gate0, 0.0) + jnp.where(slot == s1, gate1, 0.0)
    slot_gates = jnp.sum(slot_gates, axis=0, keepdims=True)
    gates_ref[...] = jnp.zeros_like(gates_ref)
    for b in range(16):
        gates_ref[b, 0:1, 0:64] = slot_gates[:, b * 64 : (b + 1) * 64]


ROUTE_AXES = ("zl", "x", "n")


def experts_step(attended, x_halves, wo, vectors, routers, prev, residual, plan, hit, grad_rows, weights):
    shifts = shifts_of(ROUTE_AXES)
    count = len(shifts)
    rows = 2 * TOK
    one = weights.shape[2:]
    peers = unique([shifts, [{"c": 1}]])

    def kernel(
        at_ref, x_ref, wo_ref, vec_ref, rc_ref, prev_ref, res_ref, plan_ref, hit_ref, gr_ref, w_hbm,
        hidden_ref, normed_ref, base_ref, table_ref, out_ref, slots_ref, dots_out, dw_hbm,
        gates_s, sending, half, row_s, arrived, gates_in, w, dw, x, xt, g, gate_col, dy, dyt, acts, acts_in,
        x_in, dy_in, xt_in, dyt_in, dx_acc, out_acc, dx_s, dot_s, p_send, p_recv,
        w_sem, c_send, c_recv, dw_sem, x_send, x_recv, a_send, a_recv, g_send, g_recv, r_send, r_recv, b_send, b_recv, d_send, d_recv,
    ):
        place = coords()
        n, c = place["n"], place["c"]
        me = rank_of(place, ROUTE_AXES)
        sibling = moved(place, {"c": 1})
        greet_start(place, peers)
        places = [(k, i) for k in range(4) for i in range(2)]
        loads = [pltpu.make_async_copy(w_hbm.at[i, k], w.at[i, 2 * k + c], w_sem.at[k, i]) for k, i in places]
        for load in loads:
            load.start()
        greet_end(peers)
        beside = [
            push(w_hbm.at[i, k], w.at[i, 2 * k + c], c_send.at[k, i], c_recv.at[k, i], sibling) for k, i in places
        ]
        own_tokens = pl.ds(pl.multiple_of(n * TOK, 128), TOK)
        swaps = []

        def send_normed():
            sending[...] = normed_ref[:, pl.ds(pl.multiple_of((1 - n) * HALF, 128), HALF)]
            swaps.append(push(sending, half.at[n], p_send, p_recv, moved(place, {"n": 1})))

        middle_forward(
            own_tokens, send_normed, at_ref, x_ref, wo_ref, vec_ref, rc_ref, prev_ref, res_ref, plan_ref,
            hidden_ref, normed_ref, base_ref, table_ref, gates_s,
        )
        swap = swaps[0]
        copies = []
        for j, shift in enumerate(shifts):
            to = rank_of(place, ROUTE_AXES, shift)
            copies.append(push(gates_s.at[to], gates_in.at[me], g_send.at[j], g_recv.at[j], moved(place, shift)))
        half[n] = normed_ref[:, pl.ds(pl.multiple_of(n * HALF, 128), HALF)]
        gates_in[me] = gates_s[me]
        for source in range(8):
            for side in range(2):
                g[source * 64 : (source + 1) * 64, side * HALF : (side + 1) * HALF] = gr_ref[2 * source + side]
        swap.wait_recv()
        for e in range(4):
            span = slice(e * 256, (e + 1) * 256)
            block = dot_dims(hit_ref[span, :TOK], half[0], 1, 0) + dot_dims(hit_ref[span, TOK:], half[1], 1, 0)
            block = block.astype(bf16)
            for i in range(4):
                row_s[e * 4 + i] = block[i * 64 : (i + 1) * 64, :]
        for j, shift in enumerate(shifts):
            to = rank_of(place, ROUTE_AXES, shift)
            copies.append(push(row_s.at[to], arrived.at[me], r_send.at[j], r_recv.at[j], moved(place, shift)))
        arrived[me] = row_s[me]
        for copy in copies[:count]:
            copy.wait_recv()
        for source in range(8):
            both = gates_in[2 * source, 0:1, 0:64] + gates_in[2 * source + 1, 0:1, 0:64]
            gate_col[source * 64 : (source + 1) * 64, :] = to_column(both)
        dffn = (g[...].astype(f32) * gate_col[...]).astype(bf16)
        dy[...] = dffn
        dyt[...] = dffn.T
        dx_acc[...] = jnp.zeros_like(dx_acc)
        out_acc[...] = jnp.zeros_like(out_acc)
        for copy in copies[count:]:
            copy.wait_recv()
        for source in range(8):
            for side in range(2):
                x[source * 64 : (source + 1) * 64, side * HALF : (side + 1) * HALF] = arrived[2 * source + side]
        row_copies = [
            push(x, x_in, x_send.at[0], x_recv.at[0], sibling),
            push(dy, dy_in, x_send.at[1], x_recv.at[1], sibling),
        ]
        xt[...] = x[...].T
        sides = (slice(0, HALF), slice(HALF, D))

        def act_copy(k):
            return pltpu.make_async_remote_copy(
                src_ref=acts.at[1 - c, k],
                dst_ref=acts_in.at[k],
                send_sem=a_send.at[k],
                recv_sem=a_recv.at[k],
                device_id=sibling,
                device_id_type=MESH,
            )

        def units_step(core, k):
            p = 2 * k + core
            gate = sum(dot_dims(x[:, s], w[i, p, 0], 1, 0) for i, s in enumerate(sides))
            up = sum(dot_dims(x[:, s], w[i, p, 1], 1, 0) for i, s in enumerate(sides))
            dunits = sum(dot_dims(dy[:, s], w[i, p, 2], 1, 0) for i, s in enumerate(sides))
            sig = 1.0 / (1.0 + jnp.exp(-gate))
            active = gate * sig
            units = (active * up).astype(bf16)
            slope = sig * (1.0 + gate * (1.0 - sig))
            dgate = (dunits * up * slope).astype(bf16)
            dup = (dunits * active).astype(bf16)
            acts[core, k, 0], acts[core, k, 1], acts[core, k, 2] = dgate, dup, units
            for i, s in enumerate(sides):
                out_acc[:, s] += dot_dims(units, w[i, p, 2], 1, 1)
                dx_acc[:, s] += dot_dims(dgate, w[i, p, 0], 1, 1) + dot_dims(dup, w[i, p, 1], 1, 1)

        def their_step(k, carry):
            units_step(1 - c, k)
            act_copy(k).start()
            return carry

        def own_step(k, carry):
            units_step(c, k)
            return carry

        for load in loads:
            load.wait()
        for copy in beside:
            copy.wait_recv()
        lax.fori_loop(0, 4, their_step, 0)
        lax.fori_loop(0, 4, own_step, 0)
        dot_s[...] = jnp.zeros_like(dot_s)
        for source in range(8):
            span = slice(source * 64, (source + 1) * 64)
            for side in range(2):
                dx_s[2 * source + side] = dx_acc[span, sides[side]].astype(bf16)
        back = []
        for j, shift in enumerate(shifts):
            to = rank_of(place, ROUTE_AXES, shift)
            back.append(push(dx_s.at[to], slots_ref.at[me], b_send.at[j], b_recv.at[j], moved(place, shift)))
        for source in range(8):
            span = slice(source * 64, (source + 1) * 64)
            dots = jnp.sum(g[span, :].astype(f32) * out_acc[span, :], axis=1, keepdims=True)
            dot_s[source, 0:1, 0:64] = to_row(dots)
        for j, shift in enumerate(shifts):
            to = rank_of(place, ROUTE_AXES, shift)
            back.append(push(dot_s.at[to // 2], dots_out.at[me], d_send.at[j], d_recv.at[j], moved(place, shift)))
        slots_ref[me] = dx_s[me]
        dots_out[me] = dot_s[me // 2]
        for source in range(8):
            span = slice(source * 64, (source + 1) * 64)
            for side in range(2):
                out_ref[2 * source + side] = (out_acc[span, sides[side]] * gate_col[span, :]).astype(bf16)

        for copy in row_copies:
            copy.wait_recv()
        xt_in[...] = x_in[...].T
        dyt_in[...] = dy_in[...].T
        stores = []
        for k in range(4):
            act_copy(k).wait_recv()
            for i, s in enumerate(sides):
                for j, (mine, theirs) in enumerate(((xt, xt_in), (xt, xt_in), (dyt, dyt_in))):
                    total = dot_dims(mine[s, :], acts[c, k, j], 1, 0) + dot_dims(theirs[s, :], acts_in[k, j], 1, 0)
                    dw[i, k, j] = total.astype(bf16)
                store = pltpu.make_async_copy(dw.at[i, k], dw_hbm.at[i, k], dw_sem.at[i, k])
                store.start()
                stores.append(store)
        for copy in back:
            copy.wait_recv()
        for copy in copies + back + beside + row_copies:
            copy.wait_send()
        for k in range(4):
            act_copy(k).wait_send()
        swap.wait_send()
        for store in stores:
            store.wait()

    route = pltpu.SemaphoreType.DMA((count,))
    return pl.pallas_call(
        kernel,
        out_shape=[
            shape_of((TOK, D), f32),
            shape_of((TOK, D), bf16),
            shape_of((2, TOK, HALF), bf16),
            shape_of((TOK, 128), f32),
            shape_of((16, 64, HALF), bf16),
            shape_of((16, 64, HALF), bf16),
            shape_of((16, 8, 128), f32),
            shape_of((2, 4) + one, bf16),
        ],
        in_specs=in_vmem(10) + [pl.BlockSpec(memory_space=pl.ANY)],
        out_specs=in_vmem(7) + [pl.BlockSpec(memory_space=pl.ANY)],
        scratch_shapes=[
            pltpu.VMEM((16, 8, 128), f32),
            pltpu.VMEM((TOK, HALF), bf16),
            pltpu.VMEM((2, TOK, HALF), bf16),
            pltpu.VMEM((16, 64, HALF), bf16),
            pltpu.VMEM((16, 64, HALF), bf16),
            pltpu.VMEM((16, 8, 128), f32),
            pltpu.VMEM((2, 8) + one, bf16),
            pltpu.VMEM((2, 4) + one, bf16),
            pltpu.VMEM((rows, D), bf16),
            pltpu.VMEM((D, rows), bf16),
            pltpu.VMEM((rows, D), bf16),
            pltpu.VMEM((rows, 1), f32),
            pltpu.VMEM((rows, D), bf16),
            pltpu.VMEM((D, rows), bf16),
            pltpu.VMEM((2, 4, 3, rows, 256), bf16),
            pltpu.VMEM((4, 3, rows, 256), bf16),
            pltpu.VMEM((rows, D), bf16),
            pltpu.VMEM((rows, D), bf16),
            pltpu.VMEM((D, rows), bf16),
            pltpu.VMEM((D, rows), bf16),
            pltpu.VMEM((rows, D), f32),
            pltpu.VMEM((rows, D), f32),
            pltpu.VMEM((16, 64, HALF), bf16),
            pltpu.VMEM((8, 8, 128), f32),
            pltpu.SemaphoreType.DMA,
            pltpu.SemaphoreType.DMA,
            pltpu.SemaphoreType.DMA((4, 2)),
            pltpu.SemaphoreType.DMA((4, 2)),
            pltpu.SemaphoreType.DMA((4, 2)),
            pltpu.SemaphoreType.DMA((2, 4)),
            pltpu.SemaphoreType.DMA((2,)),
            pltpu.SemaphoreType.DMA((2,)),
            pltpu.SemaphoreType.DMA((4,)),
            pltpu.SemaphoreType.DMA((4,)),
        ]
        + [route] * 8,
        compiler_params=comm_params(6),
        name="experts_step",
    )(attended, x_halves, wo, vectors, routers, prev, residual, plan, hit, grad_rows, weights)


def key_ids(ids_ref, place, block, tile):
    return ids_ref[(place["zl"] * 4 + place["x"]) * 8 + 2 * block + tile]


def query_ids(ids_ref, place, chunk):
    row = (place["zl"] * 4 + place["x"]) * 8 + 2 * chunk + place["c"]
    return ids_ref[row, :, pl.ds(pl.multiple_of(place["n"] * TOK, 128), TOK)]


def for_chunks(block, part, whole_chunks, partial_chunk):
    masked = [
        (block, 0, 1),
        (block, 1, jnp.minimum(part, 1)),
        (block - 1, 0, jnp.where((part == 3) & (block > 0), 1, 0)),
    ]
    for chunk, tile, times in masked:

        def body(_, carry, chunk=chunk, tile=tile):
            partial_chunk(chunk, tile)
            return carry

        if isinstance(times, int):
            partial_chunk(chunk, tile)
        else:
            lax.fori_loop(0, times, body, 0)
    yield
    lax.fori_loop(block + 1, 4, lambda j, carry: (whole_chunks(j), carry)[1], 0)
    yield


def front(w_qkv, w_out, inputs, cotangent, gains, tables, expert_ids, block_ids, experts):
    swaps_in = [
        (inputs, 1),
        (cotangent, 1),
        (shape_of((1, PART, HALF), bf16), 2),
        (shape_of((1, HALF, 128), bf16), 2),
    ]
    extra = len(swaps_in)
    given = [w_qkv, w_out, inputs, cotangent, expert_ids, *gains, *tables]
    count = len(given)
    route_shifts = shifts_of(ROUTE_AXES)
    peers = unique([shifts_of((a,)) for a in ("x", "y", "z", "c")] + [[{"n": 1}], route_shifts])

    def kernel(*refs):
        qkv_ref, out_ref, in_ref, cot_ref, ids_ref = refs[:5]
        small_refs = refs[5:count]
        bid_ref, wg_ref, wu_ref, wd_ref = refs[count : count + 4]
        rest = refs[count + 4 :]
        swapped = rest[:extra]
        x_out, _, vec_out, _ = swapped
        (
            hit_ref, plan_ref, wo_out, scaled_out, inv_out, at_out, q_out, of_ref, lse_ref, rows_done,
            wq_out, pq_out, proj_out, kv_out, ew_out,
        ) = rest[extra : extra + 15]
        parts = rest[extra + 15 : extra + 18]
        (
            gain_s, table_s, block_s, rows_in, wq_s, wo_s, wq_v, pq_v, proj_v, kv_v, q_in, kv_in,
            q_now, o_now, top_s, total_s, acc_s,
            send, recv, sib_send, sib_recv, swap_send, swap_recv, e_send, e_recv, save_sem,
            q_send, q_recv, y_send, y_recv, n_send, n_recv, c_send, c_recv, o_send, o_recv, r_send, r_recv,
        ) = rest[extra + 18 :]
        ins = (in_ref, cot_ref, gain_s, table_s)
        place = coords()
        y, c, n = place["y"], place["c"], place["n"]
        core = c
        part = 2 * c + n
        partner, sibling = moved(place, {"n": 1}), moved(place, {"c": 1})
        me = rank_of(place, ROUTE_AXES)
        greet_start(place, peers)
        block = jnp.concatenate([qkv_ref[...].astype(f32), out_ref[...].astype(f32)], axis=0)
        block = block.astype(bf16)
        for k in range(3):
            first, second, third = (place[a] for a in ORDERS[k])
            parts[k][core, third, second, first] = block[k * PART : (k + 1) * PART, :]
        rows = [ref[...].astype(f32).reshape(-1, HALF) for ref in small_refs[: len(gains)]]
        rows.append(jnp.zeros((PART - sum(row.shape[0] for row in rows), HALF), f32))
        gain_s[0] = jnp.concatenate(rows, axis=0).astype(bf16)
        lanes = [ref[...].astype(f32) for ref in small_refs[len(gains) :]]
        lanes.append(jnp.zeros((128 - sum(lane.shape[0] for lane in lanes), HALF), f32))
        table_s[0] = jnp.concatenate(lanes, axis=0).T.astype(bf16)
        block_s[0], block_s[1], block_s[2] = wg_ref[...], wu_ref[...], wd_ref[...].T
        greet_end(peers)
        stages = []
        for k in range(3):
            first, second, third = (place[a] for a in ORDERS[k])
            spot = parts[k].at[core, third, second, first]
            stages.append(
                [
                    push(spot, spot, send.at[k, 0, d], recv.at[k, 0, d], moved(place, {ORDERS[k][0]: d + 1}))
                    for d in range(3)
                ]
            )
        swaps = swap_start(place, swaps_in, ins, swapped, swap_send, swap_recv)
        later = []
        for k in range(3):
            first, second, third = (place[a] for a in ORDERS[k])
            for copy in stages[k]:
                copy.wait_recv()
            spot = parts[k].at[core, third, second]
            later.append(
                [
                    push(spot, spot, send.at[k, 1, d], recv.at[k, 1, d], moved(place, {ORDERS[k][1]: d + 1}))
                    for d in range(3)
                ]
            )
        last, gather_beside = [], []
        for k in range(3):
            third = place[ORDERS[k][2]]
            for copy in later[k]:
                copy.wait_recv()
            spot = parts[k].at[core, third]
            last.append(
                [
                    push(spot, spot, send.at[k, 2, d], recv.at[k, 2, d], moved(place, {ORDERS[k][2]: d + 1}))
                    for d in range(3)
                ]
            )
            gather_beside.append(push(spot, spot, sib_send.at[k, 0], sib_recv.at[k, 0], sibling))
        other_half = push(block_s, ew_out.at[n, y], e_send.at[0, 0], e_recv.at[0, 0], partner)
        bulk = [
            push(block_s, ew_out.at[n, y], e_send.at[0, d], e_recv.at[0, d], moved(place, {"y": d}))
            for d in (1, 3, 2)
        ]
        keep = pltpu.make_async_copy(block_s, ew_out.at[n, y], save_sem.at[0])
        keep.start()
        make_plan(ids_ref, cot_ref, hit_ref, plan_ref, rows_in)
        for d in range(3):
            for k in range(3):
                third = place[ORDERS[k][2]]
                last[k][d].wait_recv()
                spot = parts[k].at[core, lax.rem(third + 3 - d, 4)]
                gather_beside.append(
                    push(spot, spot, sib_send.at[k, d + 1], sib_recv.at[k, d + 1], sibling)
                )
        for copy in gather_beside + swaps:
            copy.wait_recv()
        query_copies, row_copies = [], []
        pair_copies, across, beside, onward = {}, {}, {}, {}

        def spread(d):
            spot = kv_v.at[lax.rem(y + 4 - d, 4), c, n]
            across[d] = push(spot, spot, n_send.at[d], n_recv.at[d], partner)
            beside[d] = push(spot, spot, c_send.at[0, d], c_recv.at[0, d], sibling)

        def pass_on(d):
            across[d].wait_recv()
            spot = kv_v.at[lax.rem(y + 4 - d, 4), c, 1 - n]
            onward[d] = push(spot, spot, c_send.at[1, d], c_recv.at[1, d], sibling)

        def send_pairs(d):
            target = lax.rem(y + d, 4)
            pair_copies[d] = push(
                kv_in.at[target], kv_v.at[y, c, n], y_send.at[d], y_recv.at[d], moved(place, {"y": d})
            )

        def send_rows():
            for j, shift in enumerate(route_shifts):
                to = rank_of(place, ROUTE_AXES, shift)
                row_copies.append(
                    push(rows_in.at[to], rows_done.at[me], r_send.at[j], r_recv.at[j], moved(place, shift))
                )
            rows_done[me] = rows_in[me]

        def first_pairs():
            kv_v[y, c, n] = kv_in[y]
            send_pairs(1)
            send_pairs(3)
            spread(0)

        project_forward(
            parts, x_out, vec_out, wq_v, wo_out, q_in, kv_in, pq_v, proj_v, scaled_out, inv_out, wq_s, wo_s,
            first_pairs,
        )
        saves = [
            pltpu.make_async_copy(here, there, save_sem.at[i + 1])
            for i, (here, there) in enumerate(((wq_v, wq_out), (pq_v, pq_out), (proj_v, proj_out)))
        ]
        for save in saves:
            save.start()
        q_now[y] = q_in[y]
        for d in (1, 3, 2):
            target = lax.rem(y + d, 4)
            query_copies.append(
                push(q_in.at[target], q_now.at[y], q_send.at[d], q_recv.at[d], moved(place, {"y": d}))
            )
        send_pairs(2)
        top_s[...] = jnp.full_like(top_s, -1e30)
        total_s[...] = jnp.zeros_like(total_s)
        acc_s[...] = jnp.zeros_like(acc_s)
        q_out[...] = jnp.zeros_like(q_out)
        pass_on(0)
        for d in (1, 3):
            pair_copies[d].wait_recv()
            spread(d)
        for copy in query_copies:
            copy.wait_recv()
        for j in range(4):
            for h in range(3):
                q_out[j, h, :HEAD_DIM, :] = q_now[j, h * HEAD_DIM : (h + 1) * HEAD_DIM, :] * 0.125

        def update(j, block, tiles, masked):
            if masked:
                allowed = [to_column(key_ids(bid_ref, place, block, t)) <= query_ids(bid_ref, place, j) for t in tiles]
            k_tiles = {}
            scores = {}
            for h in range(3):
                lanes = slice(h * 128, (h + 1) * 128)
                for t in tiles:
                    k_tiles[h, t] = kv_v[block, t, :, :, lanes].reshape(KT, 128)
                    scores[h, t] = dot_dims(k_tiles[h, t], q_out[j, h], 1, 0)
            state = []
            for h in range(3):
                mine = [scores[h, t] for t in tiles]
                if masked:
                    mine = [jnp.where(a, s, -1e30) for a, s in zip(allowed, mine)]
                old = top_s[j, h]
                top = old
                for s in mine:
                    top = jnp.maximum(top, jnp.max(s, axis=0, keepdims=True))
                decay = jnp.exp(old - top)
                total = total_s[j, h] * decay
                acc = acc_s[j, h] * decay
                for t, s in zip(tiles, mine):
                    p = jnp.exp(s - top)
                    total = total + jnp.sum(p, axis=0, keepdims=True)
                    acc = acc + dot_dims(k_tiles[h, t], p.astype(bf16), 0, 0)
                state.append((top, total, acc))
            for h in range(3):
                top_s[j, h], total_s[j, h], acc_s[j, h] = state[h]

        def second_pairs():
            pair_copies[2].wait_recv()
            spread(2)
            pass_on(1)
            send_rows()
            other_half.wait_recv()
            spot = ew_out.at[1 - n, y]
            for d in (1, 3, 2):
                bulk.append(push(spot, spot, e_send.at[1, d], e_recv.at[1, d], moved(place, {"y": d})))

        between = {0: second_pairs, 1: lambda: pass_on(3), 3: lambda: pass_on(2), 2: lambda: None}
        for d in (0, 1, 3, 2):
            beside[d].wait_recv()
            onward[d].wait_recv()
            block = lax.rem(y + 4 - d, 4)
            halves = for_chunks(
                block,
                part,
                lambda j, block=block: update(j, block, (0, 1), False),
                lambda j, t, block=block: update(j, block, (t,), True),
            )
            next(halves)
            between[d]()
            next(halves)

        save = pltpu.make_async_copy(kv_v, kv_out, save_sem.at[4])
        save.start()
        saves += [save, keep]
        out_copies = []
        for d in (2, 1, 3, 0):
            j = lax.rem(y + d, 4)
            for h in range(3):
                total = total_s[j, h]
                span = slice(h * HEAD_DIM, (h + 1) * HEAD_DIM)
                out = acc_s[j, h, HEAD_DIM:, :] * (1.0 / total)
                of_ref[j, span, :] = out
                o_now[j, span, :] = out.astype(bf16)
                lse_ref[j, h] = top_s[j, h] + jnp.log(total)
            if d:
                out_copies.append(
                    push(o_now.at[j], at_out.at[y], o_send.at[d], o_recv.at[d], moved(place, {"y": d}))
                )
            else:
                at_out[y] = o_now[y]
        for copy in out_copies + row_copies + bulk:
            copy.wait_recv()
        sent = query_copies + list(pair_copies.values()) + row_copies + out_copies
        for copy in sent + list(across.values()) + list(beside.values()) + list(onward.values()):
            copy.wait_send()
        for k in range(3):
            for copy in stages[k] + later[k] + last[k]:
                copy.wait_send()
        for copy in gather_beside + swaps + bulk + [other_half]:
            copy.wait_send()
        for save in saves:
            save.wait()

    four = pltpu.SemaphoreType.DMA((4,))
    any_place = pl.BlockSpec(memory_space=pl.ANY)
    one = (3, HALF, 256)
    return pl.pallas_call(
        kernel,
        out_shape=swap_shapes(swaps_in)
        + [
            shape_of((EXPERTS * CAP, 2 * TOK), bf16),
            shape_of((2 * TOK, 128), jnp.int32),
            shape_of((D, D), bf16),
            shape_of((TOK, D), bf16),
            shape_of((TOK, 1), f32),
            shape_of((4, 192, TOK), bf16),
            shape_of((4, 3, 128, TOK), bf16),
            shape_of((4, 192, TOK), f32),
            shape_of((4, 3, 1, TOK), f32),
            shape_of((16, 64, HALF), bf16),
            shape_of((3 * D, D), bf16),
            shape_of((4, 192, TOK), f32),
            shape_of((8, TOK, 192), f32),
            shape_of((4, 2, 2, TOK, HALF), bf16),
            shape_of((2, 4) + one, bf16),
        ],
        in_specs=in_vmem(count + 4),
        out_specs=in_vmem(extra + 10) + [any_place] * 5,
        scratch_shapes=[pltpu.VMEM((2, 4, 4, 4, PART, HALF), bf16)] * 3
        + [
            pltpu.VMEM((1, PART, HALF), bf16),
            pltpu.VMEM((1, HALF, 128), bf16),
            pltpu.VMEM(one, bf16),
            pltpu.VMEM((16, 64, HALF), bf16),
            pltpu.VMEM((3 * D, D), f32),
            pltpu.VMEM((D, D), f32),
            pltpu.VMEM((3 * D, D), bf16),
            pltpu.VMEM((4, 192, TOK), f32),
            pltpu.VMEM((8, TOK, 192), f32),
            pltpu.VMEM((4, 2, 2, TOK, HALF), bf16),
            pltpu.VMEM((4, 192, TOK), bf16),
            pltpu.VMEM((4, TOK, HALF), bf16),
            pltpu.VMEM((4, 192, TOK), bf16),
            pltpu.VMEM((4, 192, TOK), bf16),
            pltpu.VMEM((4, 3, 1, TOK), f32),
            pltpu.VMEM((4, 3, 1, TOK), f32),
            pltpu.VMEM((4, 3, 128, TOK), f32),
            pltpu.SemaphoreType.DMA((3, 3, 3)),
            pltpu.SemaphoreType.DMA((3, 3, 3)),
            pltpu.SemaphoreType.DMA((3, 4)),
            pltpu.SemaphoreType.DMA((3, 4)),
            four,
            four,
            pltpu.SemaphoreType.DMA((2, 4)),
            pltpu.SemaphoreType.DMA((2, 4)),
            pltpu.SemaphoreType.DMA((5,)),
            four,
            four,
            four,
            four,
            four,
            four,
            pltpu.SemaphoreType.DMA((2, 4)),
            pltpu.SemaphoreType.DMA((2, 4)),
            four,
            four,
            pltpu.SemaphoreType.DMA((len(route_shifts),)),
            pltpu.SemaphoreType.DMA((len(route_shifts),)),
        ],
        compiler_params=comm_params(1),
        name="front",
    )(*given, block_ids, *experts)


def middle_backward(
    place, ready, send_more, send_heads, rows_ref, hit_ref, g_ref, hidden_ref, normed_ref, table_ref, vec_ref, rc_ref, dots_ref,
    plan_ref, prev_ref, res_ref, wo_ref, hg_ref, og_ref, heads_ref, small_ref, gprev_ref, dn, row, sending, other,
    p_send, p_recv,
):
    n = place["n"]
    rows = rows_ref[...].reshape(EXPERTS * CAP, HALF)
    theirs = hit_ref[:, pl.ds(pl.multiple_of((1 - n) * TOK, 128), TOK)]
    sending[...] = dot_dims(theirs, rows, 0, 0).astype(bf16)
    ready()
    swap = push(sending, other, p_send, p_recv, moved(place, {"n": 1}))
    send_more()
    mine = hit_ref[:, pl.ds(pl.multiple_of(n * TOK, 128), TOK)]
    dn[:, pl.ds(pl.multiple_of(n * HALF, 128), HALF)] = dot_dims(mine, rows, 0, 0)
    own_tokens = pl.ds(pl.multiple_of(n * TOK, 128), TOK)
    for b in range(16):
        row[:, b * 64 : (b + 1) * 64] = dots_ref[b, 0:1, 0:64]
    table = table_ref[...]
    val = {name: column(table, name) for name in SCALARS}
    raw = table_ref[:, RAW : RAW + 16]
    g = jnp.concatenate([g_ref[0], g_ref[1]], axis=1).astype(f32)
    hidden = hidden_ref[...]
    gain = vector_rows(vec_ref, 1, 1)
    const = vector_rows(vec_ref, 2, 2)
    weighted = hidden * gain
    normed = normed_ref[...].astype(f32)
    slot = lax.broadcasted_iota(jnp.int32, (TOK, EXPERTS * CAP), 1)
    e0, e1 = plan_ref[own_tokens, 0:1], plan_ref[own_tokens, 1:2]
    dots = row[...]

    def total(array):
        return jnp.sum(array, axis=1, keepdims=True)

    dot_self = total(g * normed)
    dot_vec = [total(g * const[j : j + 1]) for j in range(2)]
    const_dots = [
        val["a00"] * dot_self + val["a01"] * dot_vec[0],
        val["a10"] * dot_self + val["a11"] * dot_vec[1],
    ]

    def gate_dot(expert, places):
        result = total(jnp.where(slot == places, dots, 0.0))
        result = result + jnp.where(expert == EXPERTS + 1, dot_self, 0.0)
        for j in range(2):
            result = result + jnp.where(expert == EXPERTS + 2 + j, const_dots[j], 0.0)
        return result

    d0, d1 = gate_dot(e0, plan_ref[own_tokens, 2:3]), gate_dot(e1, plan_ref[own_tokens, 3:4])
    mean = val["gate0"] * d0 + val["gate1"] * d1
    route = lax.broadcasted_iota(jnp.int32, (TOK, 16), 1)
    grads = jnp.where(route == e0, val["gate0"] * (d0 - mean), 0.0)
    grads = grads + jnp.where(route == e1, val["gate1"] * (d1 - mean), 0.0)
    logits_grad = grads[:, :ROUTES]
    for j in range(2):
        first, second = val["a%d0" % j], val["a%d1" % j]
        weight = val["cw%d" % j]
        da, db = weight * dot_self, weight * dot_vec[j]
        middle = first * da + second * db
        grads = jnp.where(route == ROUTES + 2 * j, first * (da - middle), grads)
        grads = jnp.where(route == ROUTES + 2 * j + 1, second * (db - middle), grads)
    inv = val["inv"]
    scaled_grads = inv * grads
    weighted_grad = exact_dims(scaled_grads, router_table(rc_ref), 1, 1)
    swap.wait_recv()
    dn[:, pl.ds(pl.multiple_of((1 - n) * HALF, 128), HALF)] = other[...].astype(f32)
    normed_grad = dn[...] + val["self"] * g
    inv_grad = total(normed_grad * weighted) + total(grads * raw)
    hidden_grad = (
        g
        + normed_grad * inv * gain
        + weighted_grad * gain
        - (inv_grad * (inv * inv * inv) / D) * hidden
    )
    hg_ref[...] = hidden_grad
    out_grad = hidden_grad.astype(bf16)
    og_ref[...] = out_grad
    for y in range(4):
        heads_ref[y] = dot_dims(wo_ref[y * 192 : (y + 1) * 192, :], out_grad, 1, 1).astype(bf16)
    send_heads()
    small_ref[...] = jnp.zeros_like(small_ref)
    small_ref[0:16, :D] = exact_dims(scaled_grads, weighted, 0, 0)
    small_ref[16:17, :D] = jnp.sum(val["vec0"] * g, axis=0, keepdims=True)
    small_ref[17:18, :D] = jnp.sum(val["vec1"] * g, axis=0, keepdims=True)
    small_ref[18:19, :D] = jnp.sum(normed_grad * hidden * inv + weighted_grad * hidden, axis=0, keepdims=True)
    small_ref[0:ROUTES, D : D + ROUTES] = exact_dims(prev_ref[:, own_tokens], logits_grad, 1, 0)
    gprev_ref[...] = jnp.zeros_like(gprev_ref)
    gprev_ref[0, 0:ROUTES, :] = exact_dims(res_ref[...].astype(f32), logits_grad, 1, 1)
    return swap


def attend_backward(middle, queries, pairs, attended, logs, block_ids, base, out_rows, weight_grads):
    small = shape_of((24, D + 128), f32)
    swaps_in = [(shape_of((1, 16, TOK), f32), 2), (base, 1)]
    extra = len(swaps_in)
    count = len(middle)
    route_shifts = shifts_of(ROUTE_AXES)
    peers = unique([shifts_of((a,)) for a in ("y", "x", "z", "c")] + [[{"n": 1}], route_shifts])
    turns = ("c", "x", "y", "z")
    order = (1, 3, 2, 0)

    def kernel(*refs):
        q_ref, of_ref, lse_ref, ids_ref, base_ref, kv_hbm, rows_in, dw_ref = refs[count : count + 8]
        hg_ref, og_ref, dq_out, dkv_out, rows_out, small_out, sum_out, sum_other = refs[count + 8 : count + 16]
        swapped = refs[count + 16 : count + 16 + extra]
        (
            heads_s, small_s, gprev_s, dn, row, sending, other, m_send, m_recv, kv_ref, kv_sem, rows_sem,
            g_now, g_pad, delta_s, dq_acc, dq_now, acc, to_sibling, from_sibling, to_other, from_other, kept, ready,
            small_now, small_in_flight, g_send, g_recv, c_send, c_recv, n_send, n_recv, y_send, y_recv,
            q_send, q_recv, r_send, r_recv, s_send, s_recv, p_send, p_recv, dw_own, dw_in, dw_on, own_sem, w_send, w_recv,
        ) = refs[count + 16 + extra :]
        place = coords()
        y, c, n = place["y"], place["c"], place["n"]
        part = 2 * c + n
        partner, sibling = moved(place, {"n": 1}), moved(place, {"c": 1})
        me = rank_of(place, ROUTE_AXES)
        ins = (gprev_s, base_ref)
        greet_start(place, peers)
        kv_load = pltpu.make_async_copy(kv_hbm, kv_ref, kv_sem)
        kv_load.start()
        grad_copies, row_copies = [], []

        def send_rows():
            for j, shift in enumerate(route_shifts):
                to = rank_of(place, ROUTE_AXES, shift)
                row_copies.append(
                    push(rows_in.at[to], rows_out.at[me], r_send.at[j], r_recv.at[j], moved(place, shift))
                )

        own_rows = pltpu.make_async_copy(rows_in.at[me], rows_out.at[me], rows_sem)
        own_rows.start()
        ways = (1, 3)
        two_on = lax.rem(y + 2, 4)
        weight_copies = []

        def send_weights():
            for i, d in enumerate(ways):
                weight_copies.append(
                    push(
                        dw_ref.at[i, two_on], dw_in.at[0, i], w_send.at[0, i], w_recv.at[0, i], moved(place, {"y": d})
                    )
                )

        loads = [
            pltpu.make_async_copy(dw_ref.at[i, lax.rem(y + d * k, 4)], dw_own.at[k, i], own_sem.at[k, i])
            for i, d in enumerate(ways)
            for k in range(2)
        ]
        for load in loads:
            load.start()
        def send_heads():
            for d in (2, 1, 3):
                target = lax.rem(y + d, 4)
                grad_copies.append(
                    push(heads_s.at[target], g_now.at[y], g_send.at[d], g_recv.at[d], moved(place, {"y": d}))
                )

        neighbour_swap = middle_backward(
            place, lambda: greet_end(peers), send_weights, send_heads, *refs[:count], hg_ref, og_ref, heads_s, small_s,
            gprev_s, dn, row, sending, other, m_send, m_recv,
        )
        g_now[y] = heads_s[y]
        small_now[0] = small_s[...]

        def small_start(turn):
            axis = turns[turn]
            return [
                push(
                    small_now.at[turn],
                    small_in_flight.at[turn, d],
                    s_send.at[turn, d],
                    s_recv.at[turn, d],
                    moved(place, {axis: d + 1}),
                )
                for d in range(SIZES[axis] - 1)
            ]

        def small_end(turn, copies):
            total = small_now[turn]
            for d, copy in enumerate(copies):
                copy.wait_recv()
                total = total + small_in_flight[turn, d]
            if turn < 3:
                small_now[turn + 1] = total
            else:
                small_out[...] = total

        small_copies = [small_start(0)]
        swaps = swap_start(place, swaps_in, ins, swapped, p_send, p_recv)
        dq_acc[...] = jnp.zeros_like(dq_acc)
        g_pad[...] = jnp.zeros_like(g_pad)
        for load in loads:
            load.wait()
        for i in range(2):
            weight_copies[i].wait_recv()
            dw_on[i] = (dw_own[1, i].astype(f32) + dw_in[0, i].astype(f32)).astype(bf16)
        kv_load.wait()
        for copy in grad_copies:
            copy.wait_recv()
        weight_copies += [
            push(dw_on.at[i], dw_in.at[2, i], w_send.at[2, i], w_recv.at[2, i], moved(place, {"y": d}))
            for i, d in enumerate(ways)
        ]
        weight_copies += [
            push(
                dw_ref.at[i, lax.rem(y + 4 - d, 4)], dw_in.at[1, i], w_send.at[1, i], w_recv.at[1, i],
                moved(place, {"y": 4 - d}),
            )
            for i, d in enumerate(ways)
        ]
        send_rows()
        own_rows.wait()
        for j in range(4):
            inner = g_now[j].astype(f32) * of_ref[j]
            for h in range(3):
                span = slice(h * HEAD_DIM, (h + 1) * HEAD_DIM)
                g_pad[j, h, HEAD_DIM:, :] = g_now[j, span, :]
                delta_s[j, h] = jnp.sum(inner[span, :], axis=0, keepdims=True)

        def update(j, block, tiles, masked):
            if masked:
                allowed = {t: to_column(key_ids(ids_ref, place, block, t)) <= query_ids(ids_ref, place, j) for t in tiles}
            places = [(t, h) for t in tiles for h in range(3)]
            k_tiles, scores, grads, both, dq = {}, {}, {}, {}, {}
            for t, h in places:
                k = kv_ref[block, t, :, :, h * 128 : (h + 1) * 128].reshape(KT, 128)
                k_tiles[t, h] = k
                scores[t, h] = dot_dims(k, q_ref[j, h], 1, 0)
                grads[t, h] = dot_dims(k, g_pad[j, h], 1, 0)
            for t, h in places:
                p = jnp.exp(scores[t, h] - lse_ref[j, h])
                if masked:
                    p = jnp.where(allowed[t], p, 0.0)
                ds = (p * (grads[t, h] - delta_s[j, h])).astype(bf16)
                both[t, h] = dot_dims(ds, q_ref[j, h], 1, 1) + dot_dims(p.astype(bf16), g_pad[j, h], 1, 1)
                more = dot_dims(k_tiles[t, h], ds, 0, 0)
                dq[h] = dq[h] + more if h in dq else more
            for t, h in places:
                acc[t, :, :, h * 128 : (h + 1) * 128] += both[t, h].reshape(2, TOK, 128)
            for h in range(3):
                dq_acc[j, h] += dq[h]

        beside, across, homeward = {}, {}, []

        def send_beside(d):
            to_sibling[d] = acc[1 - c].astype(bf16)
            beside[d] = push(to_sibling.at[d], from_sibling.at[d], c_send.at[d], c_recv.at[d], sibling)
            kept[d] = acc[c]

        def send_across(d):
            beside[d].wait_recv()
            to_other[d] = (kept[d, 1 - n] + from_sibling[d, 1 - n].astype(f32)).astype(bf16)
            across[d] = push(to_other.at[d], from_other.at[d], n_send.at[d], n_recv.at[d], partner)

        def send_home(d):
            across[d].wait_recv()
            total = kept[d, n] + from_sibling[d, n].astype(f32) + from_other[d].astype(f32)
            if d:
                ready[d] = total.astype(bf16)
                homeward.append(
                    push(ready.at[d], dkv_out.at[y], y_send.at[d], y_recv.at[d], moved(place, {"y": d}))
                )
            else:
                dkv_out[y] = total.astype(bf16)

        for step, d in enumerate(order):
            block = lax.rem(y + d, 4)
            acc[...] = jnp.zeros_like(acc)
            halves = for_chunks(
                block,
                part,
                lambda j, block=block: update(j, block, (0, 1), False),
                lambda j, t, block=block: update(j, block, (t,), True),
            )
            next(halves)
            if step:
                send_across(order[step - 1])
                small_end(step - 1, small_copies[step - 1])
                small_copies.append(small_start(step))
            if step > 1:
                send_home(order[step - 2])
            next(halves)
            send_beside(d)
        query_copies = []
        for d in (2, 1, 3, 0):
            j = lax.rem(y + d, 4)
            grad = jnp.concatenate([dq_acc[j, h, :HEAD_DIM, :] for h in range(3)], axis=0)
            grad = (grad * 0.125).astype(bf16)
            if d:
                dq_now[j] = grad
                query_copies.append(
                    push(dq_now.at[j], dq_out.at[y], q_send.at[d], q_recv.at[d], moved(place, {"y": d}))
                )
            else:
                dq_out[y] = grad
        send_home(order[2])
        send_across(order[3])
        small_end(3, small_copies[3])
        send_home(order[3])
        for copy in weight_copies[2:]:
            copy.wait_recv()
        totals = []
        for i in range(2):
            total = dw_own[0, i].astype(f32) + dw_in[1, i].astype(f32) + dw_in[2, i].astype(f32)
            totals.append(total.astype(bf16))
        sum_out[...] = jnp.where(n == 0, totals[0], totals[1])
        sum_other[...] = jnp.where(n == 0, totals[1], totals[0])
        for copy in homeward + query_copies + row_copies + swaps:
            copy.wait_recv()
        sent = grad_copies + row_copies + swaps + query_copies + homeward + weight_copies + [neighbour_swap]
        for copy in sent + list(beside.values()) + list(across.values()):
            copy.wait_send()
        for copies in small_copies:
            for copy in copies:
                copy.wait_send()

    four = pltpu.SemaphoreType.DMA((4,))
    return pl.pallas_call(
        kernel,
        out_shape=[
            shape_of((TOK, D), f32),
            shape_of((TOK, D), bf16),
            shape_of((4, 192, TOK), bf16),
            shape_of((4, TOK, HALF), bf16),
            shape_of(out_rows.shape, bf16),
            small,
            shape_of(weight_grads.shape[2:], bf16),
            shape_of(weight_grads.shape[2:], bf16),
        ]
        + swap_shapes(swaps_in),
        in_specs=in_vmem(count + 5) + [pl.BlockSpec(memory_space=pl.ANY)] * 3,
        out_specs=in_vmem(8 + extra),
        scratch_shapes=[
            pltpu.VMEM((4, 192, TOK), bf16),
            pltpu.VMEM(small.shape, f32),
            pltpu.VMEM((1, 16, TOK), f32),
            pltpu.VMEM((TOK, D), f32),
            pltpu.VMEM((1, EXPERTS * CAP), f32),
            pltpu.VMEM((TOK, HALF), bf16),
            pltpu.VMEM((TOK, HALF), bf16),
            pltpu.SemaphoreType.DMA,
            pltpu.SemaphoreType.DMA,
            pltpu.VMEM(pairs.shape, bf16),
            pltpu.SemaphoreType.DMA,
            pltpu.SemaphoreType.DMA,
            pltpu.VMEM((4, 192, TOK), bf16),
            pltpu.VMEM((4, 3, 128, TOK), bf16),
            pltpu.VMEM((4, 3, 1, TOK), f32),
            pltpu.VMEM((4, 3, 128, TOK), f32),
            pltpu.VMEM((4, 192, TOK), bf16),
            pltpu.VMEM((2, 2, TOK, HALF), f32),
            pltpu.VMEM((4, 2, TOK, HALF), bf16),
            pltpu.VMEM((4, 2, TOK, HALF), bf16),
            pltpu.VMEM((4, TOK, HALF), bf16),
            pltpu.VMEM((4, TOK, HALF), bf16),
            pltpu.VMEM((4, 2, TOK, HALF), f32),
            pltpu.VMEM((4, TOK, HALF), bf16),
            pltpu.VMEM((4,) + small.shape, f32),
            pltpu.VMEM((4, 3) + small.shape, f32),
        ]
        + [four] * 10
        + [pltpu.SemaphoreType.DMA((len(route_shifts),))] * 2
        + [pltpu.SemaphoreType.DMA((4, 3))] * 2
        + [pltpu.SemaphoreType.DMA((extra,))] * 2
        + [
            pltpu.VMEM((2, 2) + weight_grads.shape[2:], bf16),
            pltpu.VMEM((3, 2) + weight_grads.shape[2:], bf16),
            pltpu.VMEM((2,) + weight_grads.shape[2:], bf16),
            pltpu.SemaphoreType.DMA((2, 2)),
            pltpu.SemaphoreType.DMA((3, 2)),
            pltpu.SemaphoreType.DMA((3, 2)),
        ],
        compiler_params=comm_params(3),
        name="attend_backward",
    )(*middle, queries, attended, logs, block_ids, base, pairs, out_rows, weight_grads)


def project_backward(
    dq_ref, dkv_ref, pq_ref, proj_ref, inv_ref, scaled_ref, wq_ref, x_ref, vec_ref, hg_ref, at_ref, og_ref,
    pa, pb, pc, grad_ref, gain_ref, dw_s, dwo_s,
):
    inv = inv_ref[...]
    scaled = scaled_ref[...]
    dscaled = jnp.zeros((TOK, D), f32)
    dinv = jnp.zeros((TOK, 192), f32)
    dinv_row = jnp.zeros((1, TOK), f32)
    inv_row = to_row(inv)
    for s in range(3):
        for y in range(4):
            first = s * D + y * 192
            if s == 0:
                d = dq_ref[y].astype(f32)
                dinv_row = dinv_row + jnp.sum(d * pq_ref[y], axis=0, keepdims=True)
                dproject = (inv_row * d).astype(bf16)
                dscaled = dscaled + dot_dims(dproject, wq_ref[first : first + 192, :], 0, 0)
                dw_s[first : first + 192, :] = dot_dims(dproject, scaled, 1, 0)
                continue
            d = jnp.concatenate(
                [
                    dkv_ref[y, :, h * 128 + (s - 1) * HEAD_DIM : h * 128 + s * HEAD_DIM]
                    for h in range(3)
                ],
                axis=1,
            ).astype(f32)
            dinv = dinv + d * proj_ref[(s - 1) * 4 + y]
            dproject = (inv * d).astype(bf16)
            dscaled = dscaled + dot_dims(dproject, wq_ref[first : first + 192, :], 1, 0)
            dw_s[first : first + 192, :] = dot_dims(dproject, scaled, 0, 0)
    for y in range(4):
        dwo_s[y * 192 : (y + 1) * 192, :] = dot_dims(at_ref[y], og_ref[...], 1, 0)
    for w, cols, spots in blocks_of_weights():
        pa[spots[0]] = dw_s[w * 36 : w * 36 + 16, cols].astype(bf16)
        pb[spots[1]] = dw_s[w * 36 + 16 : w * 36 + 32, cols].astype(bf16)
        pc[spots[2]] = jnp.concatenate(
            [dw_s[w * 36 + 32 : w * 36 + 36, cols], dwo_s[w * 12 : w * 12 + 12, cols]], axis=0
        ).astype(bf16)
    x = jnp.concatenate([x_ref[0], x_ref[1]], axis=1).astype(f32)
    gain = jnp.concatenate([vec_ref[0, 0:1], vec_ref[1, 0:1]], axis=1).astype(f32)
    gain_ref[0] = jnp.zeros_like(gain_ref[0])
    gain_ref[0, 0:1, :] = jnp.sum(dscaled * x, axis=0, keepdims=True)
    dinv = jnp.sum(dinv, axis=1, keepdims=True) + to_column(dinv_row)
    grad = hg_ref[...] + dscaled * gain - (dinv * (inv * inv * inv) / D) * x
    for half in range(2):
        grad_ref[half] = grad[:, half * HALF : (half + 1) * HALF].astype(bf16)


def scatter_sums(given, weight_sum):
    swaps_in = [(shape_of((2, TOK, HALF), bf16), 1)]
    small = shape_of((8, D), f32)
    extra = len(swaps_in)
    peers = unique([shifts_of((a,)) for a in ("x", "y", "z", "c")])
    turns = ("c", "x", "y", "z")
    count = len(given)
    from_hbm = (2, 3, 6)

    def kernel(*refs):
        weight_ref = refs[count]
        block_out, small_out, weight_out = refs[count + 1 : count + 4]
        swapped = refs[count + 4 : count + 4 + extra]
        rest = refs[count + 4 + extra :]
        parts_in, grad_s, dw_s, dwo_s = rest[:3], rest[3], rest[4], rest[5]
        rest = rest[6:]
        from_sibling, sum_three, sum_two, sum_one = rest[0:3], rest[3:6], rest[6:9], rest[9:12]
        in_three, in_two, in_one = rest[12:15], rest[15:18], rest[18:21]
        (
            small_now,
            small_in_flight,
            c_send,
            c_recv,
            send,
            recv,
            s_send,
            s_recv,
            p_send,
            p_recv,
            w_send,
            w_recv,
            load_sem,
            *held,
        ) = rest[21:]
        place = coords()
        core = place["c"]
        ins = (grad_s,)
        greet_start(place, peers)
        loads = [
            pltpu.make_async_copy(refs[at], held[i], load_sem.at[i]) for i, at in enumerate(from_hbm)
        ]
        for load in loads:
            load.start()
        arrays = list(refs[:count])
        for i, at in enumerate(from_hbm):
            arrays[at] = held[i]
        greet_end(peers)
        for load in loads:
            load.wait()
        weight_copy = push(weight_ref, weight_out, w_send, w_recv, moved(place, {"z": 2}))
        project_backward(*arrays, *parts_in, grad_s, small_now, dw_s, dwo_s)
        beside = []
        for j in range(4):
            for k in range(3):
                third = lax.rem(place[ORDERS[k][2]] + (j + 1), 4)
                beside.append(
                    push(
                        parts_in[k].at[1 - core, third],
                        from_sibling[k].at[third],
                        c_send.at[k, j],
                        c_recv.at[k, j],
                        moved(place, {"c": 1}),
                    )
                )

        def small_start(turn):
            axis = turns[turn]
            return [
                push(
                    small_now.at[turn],
                    small_in_flight.at[turn, d],
                    s_send.at[turn, d],
                    s_recv.at[turn, d],
                    moved(place, {axis: d + 1}),
                )
                for d in range(SIZES[axis] - 1)
            ]

        def small_end(turn, copies):
            total = small_now[turn]
            for d, copy in enumerate(copies):
                copy.wait_recv()
                total = total + small_in_flight[turn, d]
            if turn < 3:
                small_now[turn + 1] = total
            else:
                small_out[...] = total

        small_copies = [small_start(0)]
        threes = [[] for _ in range(3)]
        for j in range(4):
            for k in range(3):
                third = lax.rem(place[ORDERS[k][2]] + (j + 1), 4)
                beside[j * 3 + k].wait_recv()
                sum_three[k][third] = (
                    parts_in[k][core, third].astype(f32) + from_sibling[k][third].astype(f32)
                ).astype(bf16)
                if j < 3:
                    threes[k].append(
                        push(
                            sum_three[k].at[third],
                            in_three[k].at[j],
                            send.at[k, 0, j],
                            recv.at[k, 0, j],
                            moved(place, {ORDERS[k][2]: j + 1}),
                        )
                    )
        swaps = swap_start(place, swaps_in, ins, swapped, p_send, p_recv)
        small_end(0, small_copies[0])
        small_copies.append(small_start(1))
        twos = [[] for _ in range(3)]
        for k in range(3):
            for copy in threes[k]:
                copy.wait_recv()
            third = place[ORDERS[k][2]]
            total = sum_three[k][third].astype(f32)
            for j in range(3):
                total = total + in_three[k][j].astype(f32)
            sum_two[k][...] = total.astype(bf16)
            for j in range(3):
                second = lax.rem(place[ORDERS[k][1]] + (j + 1), 4)
                twos[k].append(
                    push(
                        sum_two[k].at[second],
                        in_two[k].at[j],
                        send.at[k, 1, j],
                        recv.at[k, 1, j],
                        moved(place, {ORDERS[k][1]: j + 1}),
                    )
                )
        small_end(1, small_copies[1])
        small_copies.append(small_start(2))
        ones = [[] for _ in range(3)]
        for k in range(3):
            for copy in twos[k]:
                copy.wait_recv()
            second = place[ORDERS[k][1]]
            total = sum_two[k][second].astype(f32)
            for j in range(3):
                total = total + in_two[k][j].astype(f32)
            sum_one[k][...] = total.astype(bf16)
            for j in range(3):
                first = lax.rem(place[ORDERS[k][0]] + (j + 1), 4)
                ones[k].append(
                    push(
                        sum_one[k].at[first],
                        in_one[k].at[j],
                        send.at[k, 2, j],
                        recv.at[k, 2, j],
                        moved(place, {ORDERS[k][0]: j + 1}),
                    )
                )
        small_end(2, small_copies[2])
        small_copies.append(small_start(3))
        for k in range(3):
            for copy in ones[k]:
                copy.wait_recv()
            first = place[ORDERS[k][0]]
            total = sum_one[k][first].astype(f32)
            for j in range(3):
                total = total + in_one[k][j].astype(f32)
            block_out[k * PART : (k + 1) * PART, :] = total
        small_end(3, small_copies[3])
        for copy in swaps + [weight_copy]:
            copy.wait_recv()
        for copy in beside + swaps + [weight_copy]:
            copy.wait_send()
        for k in range(3):
            for copy in threes[k] + twos[k] + ones[k]:
                copy.wait_send()
        for copies in small_copies:
            for copy in copies:
                copy.wait_send()

    three = pltpu.VMEM((4, 4, 4, PART, HALF), bf16)
    two = pltpu.VMEM((4, 4, PART, HALF), bf16)
    one = pltpu.VMEM((4, PART, HALF), bf16)
    return pl.pallas_call(
        kernel,
        out_shape=[shape_of((3 * PART, HALF), f32), small, shape_of(weight_sum.shape, bf16)] + swap_shapes(swaps_in),
        in_specs=[pl.BlockSpec(memory_space=pl.ANY if i in from_hbm else pltpu.VMEM) for i in range(count + 1)],
        out_specs=in_vmem(3 + extra),
        scratch_shapes=[pltpu.VMEM((2, 4, 4, 4, PART, HALF), bf16)] * 3
        + [pltpu.VMEM((2, TOK, HALF), bf16), pltpu.VMEM((3 * D, D), f32), pltpu.VMEM((D, D), f32)]
        + [three] * 3
        + [three] * 3
        + [two] * 3
        + [one] * 3
        + [pltpu.VMEM((3, 4, 4, PART, HALF), bf16)] * 3
        + [pltpu.VMEM((3, 4, PART, HALF), bf16)] * 3
        + [pltpu.VMEM((3, PART, HALF), bf16)] * 3
        + [
            pltpu.VMEM((4,) + small.shape, f32),
            pltpu.VMEM((4, 3) + small.shape, f32),
            pltpu.SemaphoreType.DMA((3, 4)),
            pltpu.SemaphoreType.DMA((3, 4)),
            pltpu.SemaphoreType.DMA((3, 3, 3)),
            pltpu.SemaphoreType.DMA((3, 3, 3)),
            pltpu.SemaphoreType.DMA((4, 3)),
            pltpu.SemaphoreType.DMA((4, 3)),
            pltpu.SemaphoreType.DMA((extra,)),
            pltpu.SemaphoreType.DMA((extra,)),
            pltpu.SemaphoreType.DMA,
            pltpu.SemaphoreType.DMA,
            pltpu.SemaphoreType.DMA((len(from_hbm),)),
        ]
        + [pltpu.VMEM(given[at].shape, given[at].dtype) for at in from_hbm],
        compiler_params=comm_params(4),
        name="scatter_sums",
    )(*given, weight_sum)


def finish(grad_block, gain_sum, grad_halves, small, grad_prev, expert_sum, expert_other, base, out_slots, hit):
    def kernel(
        block_ref, gain_ref, halves_ref, small_ref, prev_ref, expert_ref, other_ref, base_ref, slots_ref, hit_ref,
        layer_out, g_inputs, g_prev, g_gain_one, g_qkv, g_out, g_gain_two, g_router, g_residual, g_const, g_vec,
        g_gate, g_up, g_down,
    ):
        n = lax.axis_index("n")
        cols = pl.ds(pl.multiple_of(n * HALF, 128), HALF)
        mixture = dot_dims(hit_ref[...], slots_ref[...].reshape(EXPERTS * CAP, HALF), 0, 0)
        for side in range(2):
            span = slice(side * TOK, (side + 1) * TOK)
            layer_out[span, :] = (base_ref[side].astype(f32) + mixture[span, :]).astype(bf16)
            g_inputs[span, :] = halves_ref[side].astype(f32)
            g_prev[:, span] = prev_ref[side, :ROUTES, :]
        g_gain_one[...] = gain_ref[0:1, cols].reshape(HALF)
        block = block_ref[...]
        g_qkv[...] = block[:36, :]
        g_out[...] = block[36:48, :]
        g_router[...] = small_ref[:ROUTES, cols]
        g_const[...] = small_ref[ROUTES:16, cols]
        g_vec[...] = small_ref[16:18, cols]
        g_gain_two[...] = small_ref[18:19, cols].reshape(HALF)
        g_residual[...] = small_ref[0:ROUTES, D : D + ROUTES]
        for i, target in enumerate((g_gate, g_up, g_down)):
            total = expert_ref[i].astype(f32) + other_ref[i].astype(f32)
            target[...] = total if i < 2 else total.T

    shapes = [
        shape_of((2 * TOK, HALF), bf16),
        shape_of((2 * TOK, HALF), f32),
        shape_of((ROUTES, 2 * TOK), f32),
        shape_of((HALF,), f32),
        shape_of((36, HALF), f32),
        shape_of((12, HALF), f32),
        shape_of((HALF,), f32),
        shape_of((ROUTES, HALF), f32),
        shape_of((ROUTES, ROUTES), f32),
        shape_of((4, HALF), f32),
        shape_of((2, HALF), f32),
        shape_of((HALF, 256), f32),
        shape_of((HALF, 256), f32),
        shape_of((256, HALF), f32),
    ]
    return pl.pallas_call(
        kernel,
        out_shape=shapes,
        in_specs=in_vmem(10),
        out_specs=in_vmem(len(shapes)),
        compiler_params=pltpu.CompilerParams(vmem_limit_bytes=VMEM_LIMIT),
        name="finish",
    )(grad_block, gain_sum, grad_halves, small, grad_prev, expert_sum, expert_other, base, out_slots, hit)


def shards(
    inputs,
    block_ids,
    expert_ids,
    prev_scores,
    gain_one,
    w_qkv,
    w_out,
    gain_two,
    w_router,
    w_residual,
    w_const,
    const_vec,
    w_gate,
    w_up,
    w_down,
    cotangent,
):
    blocks = block_ids.reshape(64, 1, 512)
    prev = prev_scores.T
    (
        x_halves, g_halves, vectors, routers, hit, plan, wo, scaled, inv_one, attended, queries, attended_f, logs,
        grad_rows, wq, project_q, project, pairs, weights,
    ) = front(
        w_qkv.T,
        w_out,
        inputs.reshape(2, TOK, HALF),
        cotangent.reshape(2, TOK, HALF),
        [gain_one, gain_two, const_vec],
        [w_router.T, w_const.T],
        expert_ids.T,
        blocks,
        [w_gate, w_up, w_down],
    )
    hidden, normed, base, table, out_rows, slot_grads, dots, expert_grads = experts_step(
        attended, x_halves, wo, vectors, routers, prev, w_residual, plan, hit, grad_rows, weights
    )
    hidden_grad, out_grad, dq, dkv, out_slots, small, expert_sum, expert_other, grad_prev, base = attend_backward(
        [
            slot_grads, hit, g_halves, hidden, normed, table, vectors, routers, dots, plan, prev, w_residual, wo,
        ],
        queries, pairs, attended_f, logs, blocks, base, out_rows, expert_grads,
    )
    grad_block, gain_sum, expert_other, grad_halves = scatter_sums(
        [
            dq, dkv, project_q, project, inv_one, scaled, wq, x_halves, vectors, hidden_grad, attended, out_grad,
        ],
        expert_other,
    )
    outputs = finish(
        grad_block, gain_sum, grad_halves, small, grad_prev, expert_sum, expert_other, base, out_slots, hit
    )
    turned = {2, 4, 7, 9}
    return tuple(out.T if i in turned else out for i, out in enumerate(outputs))


def solution(mesh):
    fine = Mesh(mesh.devices.reshape(2, 2, 4, 4, 2), AXES)
    return jax.shard_map(
        shards,
        mesh=fine,
        in_specs=(
            P(WIDE, "n"),
            P(),
            P(WIDE, None),
            P(WIDE, None),
            P("n"),
            P("n", WIDE),
            P(WIDE, "n"),
            P("n"),
            P("n", None),
            P(),
            P("n", None),
            P(None, "n"),
            P("n", WIDE),
            P("n", WIDE),
            P(WIDE, "n"),
            P(WIDE, "n"),
        ),
        out_specs=(
            P(WIDE, "n"),
            P(WIDE, "n"),
            P(WIDE, None),
            P("n"),
            P("n", WIDE),
            P(WIDE, "n"),
            P("n"),
            P("n", None),
            P(),
            P("n", None),
            P(None, "n"),
            P("n", WIDE),
            P("n", WIDE),
            P(WIDE, "n"),
        ),
        check_vma=False,
    )
```

```python
import functools
import math

import jax
import jax.numpy as jnp
from jax import lax
from jax.experimental import pallas as pl
from jax.experimental.pallas import tpu as pltpu
from jax.sharding import Mesh
from jax.sharding import PartitionSpec as P

HEAD_DIM = 64
EXPERTS = 8
ROUTES = 12
CAP = 128
D = 768
HALF = 384
TOK = 256
SEQ = 4096
KT = 512

MESH = pl.DeviceIdType.MESH
AXES = ("n", "zl", "x", "y", "c")
SIZES = dict(n=2, zl=2, x=4, y=4, c=2, z=4)
WIDE = ("zl", "x", "y", "c")
VMEM_LIMIT = 60 * 1024 * 1024

epsilon = 1e-06
highest = lax.Precision.HIGHEST
f32 = jnp.float32
bf16 = jnp.bfloat16


def exact_dot(left_side, right_side):
    return jnp.dot(left_side, right_side, precision=highest, preferred_element_type=f32)


def dot_dims(left_side, right_side, left_dim, right_dim):
    return lax.dot_general(
        left_side, right_side, (((left_dim,), (right_dim,)), ((), ())), preferred_element_type=f32
    )


def pair_softmax(logit_pairs):
    pair_top = jnp.max(logit_pairs, axis=-1, keepdims=True)
    pair_exp = jnp.exp(logit_pairs - pair_top)
    return pair_exp / jnp.sum(pair_exp, axis=-1, keepdims=True)


def coords():
    place = {axis: lax.axis_index(axis) for axis in AXES}
    place["z"] = place["n"] * 2 + place["zl"]
    return place


def moved(place, shift):
    target = {}
    for axis, steps in shift.items():
        value = lax.rem(place[axis] + steps, SIZES[axis])
        if axis == "z":
            target["n"] = value // 2
            target["zl"] = lax.rem(value, 2)
        else:
            target[axis] = value
    return target


def shifts_of(axes):
    found = [{}]
    for axis in axes:
        found = [dict(one, **{axis: k}) for one in found for k in range(SIZES[axis])]
    return [{a: k for a, k in one.items() if k} for one in found if any(one.values())]


def reverse(shift):
    return {axis: (SIZES[axis] - steps) % SIZES[axis] for axis, steps in shift.items()}


def rank_of(place, axes, shift=None):
    rank = 0
    for axis in axes:
        value = place[axis]
        if shift and axis in shift:
            value = lax.rem(value + shift[axis], SIZES[axis])
        rank = rank * SIZES[axis] + value
    return rank


def greet_start(place, shifts):
    barrier = pltpu.get_barrier_semaphore()
    for shift in shifts:
        pl.semaphore_signal(barrier, inc=1, device_id=moved(place, shift), device_id_type=MESH)


def greet_end(shifts):
    pl.semaphore_wait(pltpu.get_barrier_semaphore(), len(shifts))


def greet(place, shifts):
    greet_start(place, shifts)
    greet_end(shifts)


def push(source, target, send_sem, recv_sem, device):
    copy = pltpu.make_async_remote_copy(
        src_ref=source,
        dst_ref=target,
        send_sem=send_sem,
        recv_sem=recv_sem,
        device_id=device,
        device_id_type=MESH,
    )
    copy.start()
    return copy


def in_vmem(count):
    return [pl.BlockSpec(memory_space=pltpu.VMEM)] * count


def comm_params(collective_id):
    return pltpu.CompilerParams(
        collective_id=collective_id, has_side_effects=True, vmem_limit_bytes=VMEM_LIMIT
    )


def shape_of(shape, dtype):
    return jax.ShapeDtypeStruct(shape, dtype)


def unique(shift_lists):
    seen = []
    for shifts in shift_lists:
        for shift in shifts:
            if shift not in seen:
                seen.append(shift)
    return seen


def diagonal(size):
    rows = lax.broadcasted_iota(jnp.int32, (size, size), 0)
    return rows == lax.broadcasted_iota(jnp.int32, (size, size), 1)


def to_row(value):
    size = value.shape[0]
    return jnp.sum(jnp.where(diagonal(size), value, jnp.zeros_like(value)), axis=0, keepdims=True)


def to_column(value):
    size = min(value.shape[1], 128)
    mask = diagonal(size)
    return jnp.concatenate(
        [
            jnp.sum(
                jnp.where(mask, value[:, k * size : (k + 1) * size], jnp.zeros((), value.dtype)),
                axis=1,
                keepdims=True,
            )
            for k in range(value.shape[1] // size)
        ],
        axis=0,
    )


ORDERS = (("x", "y", "z"), ("y", "z", "x"), ("z", "x", "y"))
PART = 16


def make_plan(ids_ref, cot_ref, hit_ref, table_ref, rows_ref):
    tokens = 2 * TOK
    expert = lax.broadcasted_iota(jnp.int32, (tokens, 128), 1)
    ids = [to_column(ids_ref[k : k + 1, :]) for k in range(2)]
    table_ref[...] = jnp.zeros_like(table_ref)
    named = ((expert == ids[0]) | (expert == ids[1])).astype(bf16)
    before = lax.broadcasted_iota(jnp.int32, (tokens, tokens), 1) < lax.broadcasted_iota(
        jnp.int32, (tokens, tokens), 0
    )
    ranks = dot_dims(before.astype(bf16), named, 1, 0)
    slot = lax.broadcasted_iota(jnp.int32, (CAP * 2, tokens), 0)
    rows = []
    for k in range(2):
        rank = jnp.sum(jnp.where(expert == ids[k], ranks, 0.0), axis=1, keepdims=True)
        place = jnp.where(ids[k] < EXPERTS, ids[k] * CAP + rank.astype(jnp.int32), -1)
        table_ref[:, k : k + 1] = ids[k]
        table_ref[:, 2 + k : 3 + k] = place
        rows.append(to_row(place))
    for j in range(4):
        first = j * 2 * CAP
        hit = ((slot + first == rows[0]) | (slot + first == rows[1])).astype(bf16)
        hit_ref[first : first + 2 * CAP, :] = hit
        held = dot_dims(hit[:, :TOK], cot_ref[0], 1, 0) + dot_dims(hit[:, TOK:], cot_ref[1], 1, 0)
        held = held.astype(bf16)
        for i in range(4):
            rows_ref[j * 4 + i] = held[i * 64 : (i + 1) * 64, :]


def swap_shapes(swaps_in):
    return [shape_of((2,) + a.shape[1:], a.dtype) for a, _ in swaps_in]


def swap_start(place, swaps_in, ins, swapped, send, recv):
    n = place["n"]
    copies = []
    for i, (_, share) in enumerate(swaps_in):
        copies.append(
            push(ins[i].at[(1 - n) // share], swapped[i].at[n], send.at[i], recv.at[i], moved(place, {"z": 2}))
        )
        swapped[i][n] = ins[i][n // share]
    return copies


def blocks_of_weights():
    for zl in range(2):
        for x in range(4):
            for y in range(4):
                for c in range(2):
                    for n in range(2):
                        at = dict(x=x, y=y, z=2 * n + zl)
                        spots = [(c, at[o[2]], at[o[1]], at[o[0]]) for o in ORDERS]
                        yield ((zl * 4 + x) * 4 + y) * 2 + c, slice(n * HALF, (n + 1) * HALF), spots


def project_forward(
    parts, x_ref, vec_ref, wq_ref, wo_ref, q_ref, kv_ref, pq_ref, proj_ref, scaled_ref, inv_ref, wq_s, wo_s, send_pairs
):
    for w, cols, spots in blocks_of_weights():
        blocks = [parts[k][spots[k]].astype(f32) for k in range(3)]
        wq_s[w * 36 : w * 36 + 16, cols] = blocks[0]
        wq_s[w * 36 + 16 : w * 36 + 32, cols] = blocks[1]
        wq_s[w * 36 + 32 : w * 36 + 36, cols] = blocks[2][:4]
        wo_s[w * 12 : w * 12 + 12, cols] = blocks[2][4:]
    for j in range(9):
        wq_ref[j * 256 : (j + 1) * 256, :] = wq_s[j * 256 : (j + 1) * 256, :].astype(bf16)
    for j in range(3):
        wo_ref[j * 256 : (j + 1) * 256, :] = wo_s[j * 256 : (j + 1) * 256, :].astype(bf16)
    x = jnp.concatenate([x_ref[0], x_ref[1]], axis=1).astype(f32)
    gain = jnp.concatenate([vec_ref[0, 0:1], vec_ref[1, 0:1]], axis=1).astype(f32)
    inv = lax.rsqrt(jnp.mean(x * x, axis=1, keepdims=True) + epsilon)
    scaled = (x * gain).astype(bf16)
    scaled_ref[...] = scaled
    inv_ref[...] = inv
    inv_row = to_row(inv)
    for s in (1, 2, 0):
        if s == 0:
            send_pairs()
        for y in range(4):
            first = s * D + y * 192
            if s == 0:
                project = dot_dims(wq_ref[first : first + 192, :], scaled, 1, 1)
                pq_ref[y] = project
                q_ref[y] = (inv_row * project).astype(bf16)
            else:
                project = dot_dims(scaled, wq_ref[first : first + 192, :], 1, 1)
                proj_ref[(s - 1) * 4 + y] = project
                value = (inv * project).astype(bf16)
                for h in range(3):
                    spot = h * 128 + (s - 1) * HEAD_DIM
                    kv_ref[y, :, spot : spot + HEAD_DIM] = value[:, h * HEAD_DIM : (h + 1) * HEAD_DIM]


SCALARS = ("inv", "gate0", "gate1", "a00", "a01", "a10", "a11", "cw0", "cw1", "self", "vec0", "vec1")
RAW = 32


def column(table, name):
    spot = SCALARS.index(name)
    return table[:, spot : spot + 1]


def vector_rows(vec_ref, first, count):
    both = [vec_ref[half, first : first + count].astype(f32) for half in range(2)]
    return jnp.concatenate(both, axis=1)


def exact_dims(left_side, right_side, left_dim, right_dim):
    return lax.dot_general(
        left_side,
        right_side,
        (((left_dim,), (right_dim,)), ((), ())),
        precision=highest,
        preferred_element_type=f32,
    )


def router_table(rc_ref):
    return jnp.concatenate([rc_ref[half, :, :16].astype(f32) for half in range(2)], axis=0)


def middle_forward(
    own_tokens, send_normed, at_ref, x_ref, wo_ref, vec_ref, rc_ref, prev_ref, res_ref, plan_ref,
    hidden_ref, normed_ref, base_ref, table_ref, gates_ref,
):
    hidden = jnp.concatenate([x_ref[0], x_ref[1]], axis=1).astype(f32)
    for y in range(4):
        hidden = hidden + dot_dims(at_ref[y], wo_ref[y * 192 : (y + 1) * 192, :], 0, 0)
    hidden_ref[...] = hidden
    gain = vector_rows(vec_ref, 1, 1)
    inv = lax.rsqrt(jnp.mean(hidden * hidden, axis=1, keepdims=True) + epsilon)
    weighted = hidden * gain
    normed = (hidden * inv * gain).astype(bf16)
    normed_ref[...] = normed
    send_normed()
    raw = exact_dims(weighted, router_table(rc_ref), 1, 0)
    logits = inv * raw[:, :ROUTES] + exact_dims(prev_ref[:, own_tokens], res_ref[...].astype(f32), 0, 0)
    route = lax.broadcasted_iota(jnp.int32, (TOK, ROUTES), 1)
    e0, e1 = plan_ref[own_tokens, 0:1], plan_ref[own_tokens, 1:2]
    l0 = jnp.sum(jnp.where(route == e0, logits, 0.0), axis=1, keepdims=True)
    l1 = jnp.sum(jnp.where(route == e1, logits, 0.0), axis=1, keepdims=True)

    def softmax_two(first, second):
        top = jnp.maximum(first, second)
        a, b = jnp.exp(first - top), jnp.exp(second - top)
        return a / (a + b), b / (a + b)

    gate0, gate1 = softmax_two(l0, l1)
    coeff = [inv * raw[:, ROUTES + i : ROUTES + i + 1] for i in range(4)]
    a00, a01 = softmax_two(coeff[0], coeff[1])
    a10, a11 = softmax_two(coeff[2], coeff[3])

    def chosen(expert):
        return jnp.where(e0 == expert, gate0, 0.0) + jnp.where(e1 == expert, gate1, 0.0)

    cw0, cw1 = chosen(EXPERTS + 2), chosen(EXPERTS + 3)
    own = chosen(EXPERTS + 1) + cw0 * a00 + cw1 * a10
    vec0, vec1 = cw0 * a01, cw1 * a11
    const = vector_rows(vec_ref, 2, 2)
    base = hidden + own * normed.astype(f32) + vec0 * const[0:1] + vec1 * const[1:2]
    for half in range(2):
        base_ref[half] = base[:, half * HALF : (half + 1) * HALF].astype(bf16)
    values = dict(
        inv=inv, gate0=gate0, gate1=gate1, a00=a00, a01=a01, a10=a10, a11=a11, cw0=cw0, cw1=cw1,
        self=own, vec0=vec0, vec1=vec1,
    )
    lane = lax.broadcasted_iota(jnp.int32, (TOK, 128), 1)
    table = jnp.zeros((TOK, 128), f32)
    for i, name in enumerate(SCALARS):
        table = jnp.where(lane == i, values[name], table)
    table_ref[...] = table
    table_ref[:, RAW : RAW + 16] = raw
    slot = lax.broadcasted_iota(jnp.int32, (TOK, EXPERTS * CAP), 1)
    s0, s1 = plan_ref[own_tokens, 2:3], plan_ref[own_tokens, 3:4]
    slot_gates = jnp.where(slot == s0, gate0, 0.0) + jnp.where(slot == s1, gate1, 0.0)
    slot_gates = jnp.sum(slot_gates, axis=0, keepdims=True)
    gates_ref[...] = jnp.zeros_like(gates_ref)
    for b in range(16):
        gates_ref[b, 0:1, 0:64] = slot_gates[:, b * 64 : (b + 1) * 64]


ROUTE_AXES = ("zl", "x", "n")


def experts_step(attended, x_halves, wo, vectors, routers, prev, residual, plan, hit, grad_rows, weights):
    shifts = shifts_of(ROUTE_AXES)
    count = len(shifts)
    rows = 2 * TOK
    one = weights.shape[2:]
    peers = unique([shifts, [{"c": 1}, {"y": 2}]])

    def kernel(
        at_ref, x_ref, wo_ref, vec_ref, rc_ref, prev_ref, res_ref, plan_ref, hit_ref, gr_ref, w_hbm,
        hidden_ref, normed_ref, base_ref, table_ref, out_ref, slots_ref, dots_out, dw_hbm,
        gates_s, sending, half, row_s, arrived, gates_in, w, dw, x, xt, g, gate_col, dy, dyt, acts, acts_in,
        x_in, dy_in, xt_in, dyt_in, dx_acc, out_acc, dx_s, dot_s, p_send, p_recv,
        w_sem, f_send, f_recv, c_send, c_recv, dw_sem, x_send, x_recv, a_send, a_recv, g_send, g_recv, r_send, r_recv, b_send, b_recv, d_send, d_recv,
    ):
        place = coords()
        n, y, c = place["n"], place["y"], place["c"]
        me = rank_of(place, ROUTE_AXES)
        sibling = moved(place, {"c": 1})
        greet_start(place, peers)
        places = [(d, lax.rem(y + d, 4), i) for d in range(4) for i in (n, 1 - n)][:-3]
        places += [(3, lax.rem(y + 3, 4), n), (3, lax.rem(y + 3, 4), 1 - n)]
        loads = [
            pltpu.make_async_copy(w_hbm.at[i, k], w.at[i, 2 * k + c], w_sem.at[j])
            for j, (_, k, i) in enumerate(places)
        ]
        for load in loads:
            load.start()
        greet_end(peers)
        far = push(w_hbm.at[1 - n, y], w.at[1 - n, 2 * y + c], f_send, f_recv, moved(place, {"y": 2}))
        beside = [
            push(w_hbm.at[i, k], w.at[i, 2 * k + c], c_send.at[j], c_recv.at[j], sibling)
            for j, (_, k, i) in enumerate(places)
        ]

        def pass_far():
            far.wait_recv()
            spot = w.at[1 - n, 2 * lax.rem(y + 2, 4) + c]
            beside.append(push(spot, spot, c_send.at[7], c_recv.at[7], sibling))

        own_tokens = pl.ds(pl.multiple_of(n * TOK, 128), TOK)
        swaps = []

        def send_normed():
            sending[...] = normed_ref[:, pl.ds(pl.multiple_of((1 - n) * HALF, 128), HALF)]
            swaps.append(push(sending, half.at[n], p_send, p_recv, moved(place, {"n": 1})))

        middle_forward(
            own_tokens, send_normed, at_ref, x_ref, wo_ref, vec_ref, rc_ref, prev_ref, res_ref, plan_ref,
            hidden_ref, normed_ref, base_ref, table_ref, gates_s,
        )
        swap = swaps[0]
        copies = []
        for j, shift in enumerate(shifts):
            to = rank_of(place, ROUTE_AXES, shift)
            copies.append(push(gates_s.at[to], gates_in.at[me], g_send.at[j], g_recv.at[j], moved(place, shift)))
        half[n] = normed_ref[:, pl.ds(pl.multiple_of(n * HALF, 128), HALF)]
        gates_in[me] = gates_s[me]
        for source in range(8):
            for side in range(2):
                g[source * 64 : (source + 1) * 64, side * HALF : (side + 1) * HALF] = gr_ref[2 * source + side]
        swap.wait_recv()
        for e in range(4):
            span = slice(e * 256, (e + 1) * 256)
            block = dot_dims(hit_ref[span, :TOK], half[0], 1, 0) + dot_dims(hit_ref[span, TOK:], half[1], 1, 0)
            block = block.astype(bf16)
            for i in range(4):
                row_s[e * 4 + i] = block[i * 64 : (i + 1) * 64, :]
        for j, shift in enumerate(shifts):
            to = rank_of(place, ROUTE_AXES, shift)
            copies.append(push(row_s.at[to], arrived.at[me], r_send.at[j], r_recv.at[j], moved(place, shift)))
        arrived[me] = row_s[me]
        pass_far()
        for copy in copies[:count]:
            copy.wait_recv()
        for source in range(8):
            both = gates_in[2 * source, 0:1, 0:64] + gates_in[2 * source + 1, 0:1, 0:64]
            gate_col[source * 64 : (source + 1) * 64, :] = to_column(both)
        dffn = (g[...].astype(f32) * gate_col[...]).astype(bf16)
        dy[...] = dffn
        dyt[...] = dffn.T
        dx_acc[...] = jnp.zeros_like(dx_acc)
        out_acc[...] = jnp.zeros_like(out_acc)
        for copy in copies[count:]:
            copy.wait_recv()
        for source in range(8):
            for side in range(2):
                x[source * 64 : (source + 1) * 64, side * HALF : (side + 1) * HALF] = arrived[2 * source + side]
        row_copies = [
            push(x, x_in, x_send.at[0], x_recv.at[0], sibling),
            push(dy, dy_in, x_send.at[1], x_recv.at[1], sibling),
        ]
        xt[...] = x[...].T
        sides = (slice(0, HALF), slice(HALF, D))

        def act_copy(k):
            return pltpu.make_async_remote_copy(
                src_ref=acts.at[1 - c, k],
                dst_ref=acts_in.at[k],
                send_sem=a_send.at[k],
                recv_sem=a_recv.at[k],
                device_id=sibling,
                device_id_type=MESH,
            )

        def units_step(core, k):
            p = 2 * k + core
            gate = sum(dot_dims(x[:, s], w[i, p, 0], 1, 0) for i, s in enumerate(sides))
            up = sum(dot_dims(x[:, s], w[i, p, 1], 1, 0) for i, s in enumerate(sides))
            dunits = sum(dot_dims(dy[:, s], w[i, p, 2], 1, 0) for i, s in enumerate(sides))
            sig = 1.0 / (1.0 + jnp.exp(-gate))
            active = gate * sig
            units = (active * up).astype(bf16)
            slope = sig * (1.0 + gate * (1.0 - sig))
            dgate = (dunits * up * slope).astype(bf16)
            dup = (dunits * active).astype(bf16)
            acts[core, k, 0], acts[core, k, 1], acts[core, k, 2] = dgate, dup, units
            for i, s in enumerate(sides):
                out_acc[:, s] += dot_dims(units, w[i, p, 2], 1, 1)
                dx_acc[:, s] += dot_dims(dgate, w[i, p, 0], 1, 1) + dot_dims(dup, w[i, p, 1], 1, 1)

        def their_step(k, carry):
            units_step(1 - c, k)
            act_copy(k).start()
            return carry

        def own_step(k, carry):
            units_step(c, k)
            return carry

        for load in loads:
            load.wait()
        for copy in beside:
            copy.wait_recv()
        lax.fori_loop(0, 4, their_step, 0)
        lax.fori_loop(0, 4, own_step, 0)
        dot_s[...] = jnp.zeros_like(dot_s)
        for source in range(8):
            span = slice(source * 64, (source + 1) * 64)
            for side in range(2):
                dx_s[2 * source + side] = dx_acc[span, sides[side]].astype(bf16)
        back = []
        for j, shift in enumerate(shifts):
            to = rank_of(place, ROUTE_AXES, shift)
            back.append(push(dx_s.at[to], slots_ref.at[me], b_send.at[j], b_recv.at[j], moved(place, shift)))
        for source in range(8):
            span = slice(source * 64, (source + 1) * 64)
            dots = jnp.sum(g[span, :].astype(f32) * out_acc[span, :], axis=1, keepdims=True)
            dot_s[source, 0:1, 0:64] = to_row(dots)
        for j, shift in enumerate(shifts):
            to = rank_of(place, ROUTE_AXES, shift)
            back.append(push(dot_s.at[to // 2], dots_out.at[me], d_send.at[j], d_recv.at[j], moved(place, shift)))
        slots_ref[me] = dx_s[me]
        dots_out[me] = dot_s[me // 2]
        for source in range(8):
            span = slice(source * 64, (source + 1) * 64)
            for side in range(2):
                out_ref[2 * source + side] = (out_acc[span, sides[side]] * gate_col[span, :]).astype(bf16)

        for copy in row_copies:
            copy.wait_recv()
        xt_in[...] = x_in[...].T
        dyt_in[...] = dy_in[...].T
        stores = []
        for k in range(4):
            act_copy(k).wait_recv()
            for i, s in enumerate(sides):
                for j, (mine, theirs) in enumerate(((xt, xt_in), (xt, xt_in), (dyt, dyt_in))):
                    total = dot_dims(mine[s, :], acts[c, k, j], 1, 0) + dot_dims(theirs[s, :], acts_in[k, j], 1, 0)
                    dw[i, k, j] = total.astype(bf16)
                store = pltpu.make_async_copy(dw.at[i, k], dw_hbm.at[i, k], dw_sem.at[i, k])
                store.start()
                stores.append(store)
        for copy in back:
            copy.wait_recv()
        for copy in copies + back + beside + row_copies + [far]:
            copy.wait_send()
        for k in range(4):
            act_copy(k).wait_send()
        swap.wait_send()
        for store in stores:
            store.wait()

    route = pltpu.SemaphoreType.DMA((count,))
    return pl.pallas_call(
        kernel,
        out_shape=[
            shape_of((TOK, D), f32),
            shape_of((TOK, D), bf16),
            shape_of((2, TOK, HALF), bf16),
            shape_of((TOK, 128), f32),
            shape_of((16, 64, HALF), bf16),
            shape_of((16, 64, HALF), bf16),
            shape_of((16, 8, 128), f32),
            shape_of((2, 4) + one, bf16),
        ],
        in_specs=in_vmem(10) + [pl.BlockSpec(memory_space=pl.ANY)],
        out_specs=in_vmem(7) + [pl.BlockSpec(memory_space=pl.ANY)],
        scratch_shapes=[
            pltpu.VMEM((16, 8, 128), f32),
            pltpu.VMEM((TOK, HALF), bf16),
            pltpu.VMEM((2, TOK, HALF), bf16),
            pltpu.VMEM((16, 64, HALF), bf16),
            pltpu.VMEM((16, 64, HALF), bf16),
            pltpu.VMEM((16, 8, 128), f32),
            pltpu.VMEM((2, 8) + one, bf16),
            pltpu.VMEM((2, 4) + one, bf16),
            pltpu.VMEM((rows, D), bf16),
            pltpu.VMEM((D, rows), bf16),
            pltpu.VMEM((rows, D), bf16),
            pltpu.VMEM((rows, 1), f32),
            pltpu.VMEM((rows, D), bf16),
            pltpu.VMEM((D, rows), bf16),
            pltpu.VMEM((2, 4, 3, rows, 256), bf16),
            pltpu.VMEM((4, 3, rows, 256), bf16),
            pltpu.VMEM((rows, D), bf16),
            pltpu.VMEM((rows, D), bf16),
            pltpu.VMEM((D, rows), bf16),
            pltpu.VMEM((D, rows), bf16),
            pltpu.VMEM((rows, D), f32),
            pltpu.VMEM((rows, D), f32),
            pltpu.VMEM((16, 64, HALF), bf16),
            pltpu.VMEM((8, 8, 128), f32),
            pltpu.SemaphoreType.DMA,
            pltpu.SemaphoreType.DMA,
            pltpu.SemaphoreType.DMA((8,)),
            pltpu.SemaphoreType.DMA,
            pltpu.SemaphoreType.DMA,
            pltpu.SemaphoreType.DMA((8,)),
            pltpu.SemaphoreType.DMA((8,)),
            pltpu.SemaphoreType.DMA((2, 4)),
            pltpu.SemaphoreType.DMA((2,)),
            pltpu.SemaphoreType.DMA((2,)),
            pltpu.SemaphoreType.DMA((4,)),
            pltpu.SemaphoreType.DMA((4,)),
        ]
        + [route] * 8,
        compiler_params=comm_params(6),
        name="experts_step",
    )(attended, x_halves, wo, vectors, routers, prev, residual, plan, hit, grad_rows, weights)


def key_ids(ids_ref, place, block, tile):
    return ids_ref[(place["zl"] * 4 + place["x"]) * 8 + 2 * block + tile]


def query_ids(ids_ref, place, chunk):
    row = (place["zl"] * 4 + place["x"]) * 8 + 2 * chunk + place["c"]
    return ids_ref[row, :, pl.ds(pl.multiple_of(place["n"] * TOK, 128), TOK)]


def for_chunks(block, part, whole_chunks, partial_chunk):
    masked = [
        (block, 0, 1),
        (block, 1, jnp.minimum(part, 1)),
        (block - 1, 0, jnp.where((part == 3) & (block > 0), 1, 0)),
    ]
    for chunk, tile, times in masked:

        def body(_, carry, chunk=chunk, tile=tile):
            partial_chunk(chunk, tile)
            return carry

        if isinstance(times, int):
            partial_chunk(chunk, tile)
        else:
            lax.fori_loop(0, times, body, 0)
    yield
    lax.fori_loop(block + 1, 4, lambda j, carry: (whole_chunks(j), carry)[1], 0)
    yield


def front(w_qkv, w_out, inputs, cotangent, gains, tables, expert_ids, block_ids, experts):
    swaps_in = [
        (inputs, 1),
        (cotangent, 1),
        (shape_of((1, PART, HALF), bf16), 2),
        (shape_of((1, HALF, 128), bf16), 2),
    ]
    extra = len(swaps_in)
    given = [w_qkv, w_out, inputs, cotangent, expert_ids, *gains, *tables]
    count = len(given)
    route_shifts = shifts_of(ROUTE_AXES)
    peers = unique([shifts_of((a,)) for a in ("x", "y", "z", "c")] + [[{"n": 1}], route_shifts])

    def kernel(*refs):
        qkv_ref, out_ref, in_ref, cot_ref, ids_ref = refs[:5]
        small_refs = refs[5:count]
        bid_ref, wg_ref, wu_ref, wd_ref = refs[count : count + 4]
        rest = refs[count + 4 :]
        swapped = rest[:extra]
        x_out, _, vec_out, _ = swapped
        (
            hit_ref, plan_ref, wo_out, scaled_out, inv_out, at_out, q_out, of_ref, lse_ref, rows_done,
            wq_out, pq_out, proj_out, kv_out, ew_out,
        ) = rest[extra : extra + 15]
        parts = rest[extra + 15 : extra + 18]
        (
            gain_s, table_s, block_s, rows_in, wq_s, wo_s, wq_v, pq_v, proj_v, kv_v, q_in, kv_in,
            q_now, o_now, top_s, total_s, acc_s,
            send, recv, sib_send, sib_recv, swap_send, swap_recv, e_send, e_recv, save_sem,
            q_send, q_recv, y_send, y_recv, n_send, n_recv, c_send, c_recv, o_send, o_recv, r_send, r_recv,
        ) = rest[extra + 18 :]
        ins = (in_ref, cot_ref, gain_s, table_s)
        place = coords()
        y, c, n = place["y"], place["c"], place["n"]
        core = c
        part = 2 * c + n
        partner, sibling = moved(place, {"n": 1}), moved(place, {"c": 1})
        me = rank_of(place, ROUTE_AXES)
        greet_start(place, peers)
        block = jnp.concatenate([qkv_ref[...].astype(f32), out_ref[...].astype(f32)], axis=0)
        block = block.astype(bf16)
        for k in range(3):
            first, second, third = (place[a] for a in ORDERS[k])
            parts[k][core, third, second, first] = block[k * PART : (k + 1) * PART, :]
        rows = [ref[...].astype(f32).reshape(-1, HALF) for ref in small_refs[: len(gains)]]
        rows.append(jnp.zeros((PART - sum(row.shape[0] for row in rows), HALF), f32))
        gain_s[0] = jnp.concatenate(rows, axis=0).astype(bf16)
        lanes = [ref[...].astype(f32) for ref in small_refs[len(gains) :]]
        lanes.append(jnp.zeros((128 - sum(lane.shape[0] for lane in lanes), HALF), f32))
        table_s[0] = jnp.concatenate(lanes, axis=0).T.astype(bf16)
        block_s[0], block_s[1], block_s[2] = wg_ref[...], wu_ref[...], wd_ref[...].T
        greet_end(peers)
        bulk = []

        def send_block(d):
            bulk.append(push(block_s, ew_out.at[n, y], e_send.at[0, d], e_recv.at[0, d], moved(place, {"y": d})))

        stages = []
        for k in range(3):
            first, second, third = (place[a] for a in ORDERS[k])
            spot = parts[k].at[core, third, second, first]
            stages.append(
                [
                    push(spot, spot, send.at[k, 0, d], recv.at[k, 0, d], moved(place, {ORDERS[k][0]: d + 1}))
                    for d in range(3)
                ]
            )
        swaps = swap_start(place, swaps_in, ins, swapped, swap_send, swap_recv)
        send_block(1)
        send_block(3)
        later = []
        for k in range(3):
            first, second, third = (place[a] for a in ORDERS[k])
            for copy in stages[k]:
                copy.wait_recv()
            spot = parts[k].at[core, third, second]
            later.append(
                [
                    push(spot, spot, send.at[k, 1, d], recv.at[k, 1, d], moved(place, {ORDERS[k][1]: d + 1}))
                    for d in range(3)
                ]
            )
        last, gather_beside = [], []
        for k in range(3):
            third = place[ORDERS[k][2]]
            for copy in later[k]:
                copy.wait_recv()
            spot = parts[k].at[core, third]
            last.append(
                [
                    push(spot, spot, send.at[k, 2, d], recv.at[k, 2, d], moved(place, {ORDERS[k][2]: d + 1}))
                    for d in range(3)
                ]
            )
            gather_beside.append(push(spot, spot, sib_send.at[k, 0], sib_recv.at[k, 0], sibling))
        other_half = push(block_s, ew_out.at[n, y], e_send.at[0, 0], e_recv.at[0, 0], partner)
        send_block(2)
        keep = pltpu.make_async_copy(block_s, ew_out.at[n, y], save_sem.at[0])
        keep.start()
        make_plan(ids_ref, cot_ref, hit_ref, plan_ref, rows_in)
        for d in range(3):
            for k in range(3):
                third = place[ORDERS[k][2]]
                last[k][d].wait_recv()
                spot = parts[k].at[core, lax.rem(third + 3 - d, 4)]
                gather_beside.append(
                    push(spot, spot, sib_send.at[k, d + 1], sib_recv.at[k, d + 1], sibling)
                )
        for copy in gather_beside + swaps:
            copy.wait_recv()
        query_copies, row_copies = [], []
        pair_copies, across, beside, onward = {}, {}, {}, {}

        def spread(d):
            spot = kv_v.at[lax.rem(y + 4 - d, 4), c, n]
            across[d] = push(spot, spot, n_send.at[d], n_recv.at[d], partner)
            beside[d] = push(spot, spot, c_send.at[0, d], c_recv.at[0, d], sibling)

        def pass_on(d):
            across[d].wait_recv()
            spot = kv_v.at[lax.rem(y + 4 - d, 4), c, 1 - n]
            onward[d] = push(spot, spot, c_send.at[1, d], c_recv.at[1, d], sibling)

        def send_pairs(d):
            target = lax.rem(y + d, 4)
            pair_copies[d] = push(
                kv_in.at[target], kv_v.at[y, c, n], y_send.at[d], y_recv.at[d], moved(place, {"y": d})
            )

        def send_rows():
            for j, shift in enumerate(route_shifts):
                to = rank_of(place, ROUTE_AXES, shift)
                row_copies.append(
                    push(rows_in.at[to], rows_done.at[me], r_send.at[j], r_recv.at[j], moved(place, shift))
                )
            rows_done[me] = rows_in[me]

        def first_pairs():
            kv_v[y, c, n] = kv_in[y]
            send_pairs(1)
            send_pairs(3)
            spread(0)

        project_forward(
            parts, x_out, vec_out, wq_v, wo_out, q_in, kv_in, pq_v, proj_v, scaled_out, inv_out, wq_s, wo_s,
            first_pairs,
        )
        saves = [
            pltpu.make_async_copy(here, there, save_sem.at[i + 1])
            for i, (here, there) in enumerate(((wq_v, wq_out), (pq_v, pq_out), (proj_v, proj_out)))
        ]
        for save in saves:
            save.start()
        q_now[y] = q_in[y]
        for d in (1, 3, 2):
            target = lax.rem(y + d, 4)
            query_copies.append(
                push(q_in.at[target], q_now.at[y], q_send.at[d], q_recv.at[d], moved(place, {"y": d}))
            )
        send_pairs(2)
        top_s[...] = jnp.full_like(top_s, -1e30)
        total_s[...] = jnp.zeros_like(total_s)
        acc_s[...] = jnp.zeros_like(acc_s)
        q_out[...] = jnp.zeros_like(q_out)
        pass_on(0)
        for d in (1, 3):
            pair_copies[d].wait_recv()
            spread(d)
        for copy in query_copies:
            copy.wait_recv()
        for j in range(4):
            for h in range(3):
                q_out[j, h, :HEAD_DIM, :] = q_now[j, h * HEAD_DIM : (h + 1) * HEAD_DIM, :] * 0.125

        def update(j, block, tiles, masked):
            if masked:
                allowed = [to_column(key_ids(bid_ref, place, block, t)) <= query_ids(bid_ref, place, j) for t in tiles]
            k_tiles = {}
            scores = {}
            for h in range(3):
                lanes = slice(h * 128, (h + 1) * 128)
                for t in tiles:
                    k_tiles[h, t] = kv_v[block, t, :, :, lanes].reshape(KT, 128)
                    scores[h, t] = dot_dims(k_tiles[h, t], q_out[j, h], 1, 0)
            state = []
            for h in range(3):
                mine = [scores[h, t] for t in tiles]
                if masked:
                    mine = [jnp.where(a, s, -1e30) for a, s in zip(allowed, mine)]
                old = top_s[j, h]
                top = old
                for s in mine:
                    top = jnp.maximum(top, jnp.max(s, axis=0, keepdims=True))
                decay = jnp.exp(old - top)
                total = total_s[j, h] * decay
                acc = acc_s[j, h] * decay
                for t, s in zip(tiles, mine):
                    p = jnp.exp(s - top)
                    total = total + jnp.sum(p, axis=0, keepdims=True)
                    acc = acc + dot_dims(k_tiles[h, t], p.astype(bf16), 0, 0)
                state.append((top, total, acc))
            for h in range(3):
                top_s[j, h], total_s[j, h], acc_s[j, h] = state[h]

        def second_pairs():
            pair_copies[2].wait_recv()
            spread(2)
            pass_on(1)
            send_rows()
            other_half.wait_recv()
            spot = ew_out.at[1 - n, y]
            for d in (1, 3):
                bulk.append(push(spot, spot, e_send.at[1, d], e_recv.at[1, d], moved(place, {"y": d})))

        between = {0: second_pairs, 1: lambda: pass_on(3), 3: lambda: pass_on(2), 2: lambda: None}
        for d in (0, 1, 3, 2):
            beside[d].wait_recv()
            onward[d].wait_recv()
            block = lax.rem(y + 4 - d, 4)
            halves = for_chunks(
                block,
                part,
                lambda j, block=block: update(j, block, (0, 1), False),
                lambda j, t, block=block: update(j, block, (t,), True),
            )
            next(halves)
            between[d]()
            next(halves)

        save = pltpu.make_async_copy(kv_v, kv_out, save_sem.at[4])
        save.start()
        saves += [save, keep]
        out_copies = []
        for d in (2, 1, 3, 0):
            j = lax.rem(y + d, 4)
            for h in range(3):
                total = total_s[j, h]
                span = slice(h * HEAD_DIM, (h + 1) * HEAD_DIM)
                out = acc_s[j, h, HEAD_DIM:, :] * (1.0 / total)
                of_ref[j, span, :] = out
                o_now[j, span, :] = out.astype(bf16)
                lse_ref[j, h] = top_s[j, h] + jnp.log(total)
            if d:
                out_copies.append(
                    push(o_now.at[j], at_out.at[y], o_send.at[d], o_recv.at[d], moved(place, {"y": d}))
                )
            else:
                at_out[y] = o_now[y]
        for copy in out_copies + row_copies + bulk:
            copy.wait_recv()
        sent = query_copies + list(pair_copies.values()) + row_copies + out_copies
        for copy in sent + list(across.values()) + list(beside.values()) + list(onward.values()):
            copy.wait_send()
        for k in range(3):
            for copy in stages[k] + later[k] + last[k]:
                copy.wait_send()
        for copy in gather_beside + swaps + bulk + [other_half]:
            copy.wait_send()
        for save in saves:
            save.wait()

    four = pltpu.SemaphoreType.DMA((4,))
    any_place = pl.BlockSpec(memory_space=pl.ANY)
    one = (3, HALF, 256)
    return pl.pallas_call(
        kernel,
        out_shape=swap_shapes(swaps_in)
        + [
            shape_of((EXPERTS * CAP, 2 * TOK), bf16),
            shape_of((2 * TOK, 128), jnp.int32),
            shape_of((D, D), bf16),
            shape_of((TOK, D), bf16),
            shape_of((TOK, 1), f32),
            shape_of((4, 192, TOK), bf16),
            shape_of((4, 3, 128, TOK), bf16),
            shape_of((4, 192, TOK), f32),
            shape_of((4, 3, 1, TOK), f32),
            shape_of((16, 64, HALF), bf16),
            shape_of((3 * D, D), bf16),
            shape_of((4, 192, TOK), f32),
            shape_of((8, TOK, 192), f32),
            shape_of((4, 2, 2, TOK, HALF), bf16),
            shape_of((2, 4) + one, bf16),
        ],
        in_specs=in_vmem(count + 4),
        out_specs=in_vmem(extra + 10) + [any_place] * 5,
        scratch_shapes=[pltpu.VMEM((2, 4, 4, 4, PART, HALF), bf16)] * 3
        + [
            pltpu.VMEM((1, PART, HALF), bf16),
            pltpu.VMEM((1, HALF, 128), bf16),
            pltpu.VMEM(one, bf16),
            pltpu.VMEM((16, 64, HALF), bf16),
            pltpu.VMEM((3 * D, D), f32),
            pltpu.VMEM((D, D), f32),
            pltpu.VMEM((3 * D, D), bf16),
            pltpu.VMEM((4, 192, TOK), f32),
            pltpu.VMEM((8, TOK, 192), f32),
            pltpu.VMEM((4, 2, 2, TOK, HALF), bf16),
            pltpu.VMEM((4, 192, TOK), bf16),
            pltpu.VMEM((4, TOK, HALF), bf16),
            pltpu.VMEM((4, 192, TOK), bf16),
            pltpu.VMEM((4, 192, TOK), bf16),
            pltpu.VMEM((4, 3, 1, TOK), f32),
            pltpu.VMEM((4, 3, 1, TOK), f32),
            pltpu.VMEM((4, 3, 128, TOK), f32),
            pltpu.SemaphoreType.DMA((3, 3, 3)),
            pltpu.SemaphoreType.DMA((3, 3, 3)),
            pltpu.SemaphoreType.DMA((3, 4)),
            pltpu.SemaphoreType.DMA((3, 4)),
            four,
            four,
            pltpu.SemaphoreType.DMA((2, 4)),
            pltpu.SemaphoreType.DMA((2, 4)),
            pltpu.SemaphoreType.DMA((5,)),
            four,
            four,
            four,
            four,
            four,
            four,
            pltpu.SemaphoreType.DMA((2, 4)),
            pltpu.SemaphoreType.DMA((2, 4)),
            four,
            four,
            pltpu.SemaphoreType.DMA((len(route_shifts),)),
            pltpu.SemaphoreType.DMA((len(route_shifts),)),
        ],
        compiler_params=comm_params(1),
        name="front",
    )(*given, block_ids, *experts)


def middle_backward(
    place, ready, send_more, send_heads, rows_ref, hit_ref, g_ref, hidden_ref, normed_ref, table_ref, vec_ref, rc_ref, dots_ref,
    plan_ref, prev_ref, res_ref, wo_ref, hg_ref, og_ref, heads_ref, small_ref, gprev_ref, dn, row, sending, other,
    p_send, p_recv,
):
    n = place["n"]
    rows = rows_ref[...].reshape(EXPERTS * CAP, HALF)
    theirs = hit_ref[:, pl.ds(pl.multiple_of((1 - n) * TOK, 128), TOK)]
    sending[...] = dot_dims(theirs, rows, 0, 0).astype(bf16)
    ready()
    swap = push(sending, other, p_send, p_recv, moved(place, {"n": 1}))
    send_more()
    mine = hit_ref[:, pl.ds(pl.multiple_of(n * TOK, 128), TOK)]
    dn[:, pl.ds(pl.multiple_of(n * HALF, 128), HALF)] = dot_dims(mine, rows, 0, 0)
    own_tokens = pl.ds(pl.multiple_of(n * TOK, 128), TOK)
    for b in range(16):
        row[:, b * 64 : (b + 1) * 64] = dots_ref[b, 0:1, 0:64]
    table = table_ref[...]
    val = {name: column(table, name) for name in SCALARS}
    raw = table_ref[:, RAW : RAW + 16]
    g = jnp.concatenate([g_ref[0], g_ref[1]], axis=1).astype(f32)
    hidden = hidden_ref[...]
    gain = vector_rows(vec_ref, 1, 1)
    const = vector_rows(vec_ref, 2, 2)
    weighted = hidden * gain
    normed = normed_ref[...].astype(f32)
    slot = lax.broadcasted_iota(jnp.int32, (TOK, EXPERTS * CAP), 1)
    e0, e1 = plan_ref[own_tokens, 0:1], plan_ref[own_tokens, 1:2]
    dots = row[...]

    def total(array):
        return jnp.sum(array, axis=1, keepdims=True)

    dot_self = total(g * normed)
    dot_vec = [total(g * const[j : j + 1]) for j in range(2)]
    const_dots = [
        val["a00"] * dot_self + val["a01"] * dot_vec[0],
        val["a10"] * dot_self + val["a11"] * dot_vec[1],
    ]

    def gate_dot(expert, places):
        result = total(jnp.where(slot == places, dots, 0.0))
        result = result + jnp.where(expert == EXPERTS + 1, dot_self, 0.0)
        for j in range(2):
            result = result + jnp.where(expert == EXPERTS + 2 + j, const_dots[j], 0.0)
        return result

    d0, d1 = gate_dot(e0, plan_ref[own_tokens, 2:3]), gate_dot(e1, plan_ref[own_tokens, 3:4])
    mean = val["gate0"] * d0 + val["gate1"] * d1
    route = lax.broadcasted_iota(jnp.int32, (TOK, 16), 1)
    grads = jnp.where(route == e0, val["gate0"] * (d0 - mean), 0.0)
    grads = grads + jnp.where(route == e1, val["gate1"] * (d1 - mean), 0.0)
    logits_grad = grads[:, :ROUTES]
    for j in range(2):
        first, second = val["a%d0" % j], val["a%d1" % j]
        weight = val["cw%d" % j]
        da, db = weight * dot_self, weight * dot_vec[j]
        middle = first * da + second * db
        grads = jnp.where(route == ROUTES + 2 * j, first * (da - middle), grads)
        grads = jnp.where(route == ROUTES + 2 * j + 1, second * (db - middle), grads)
    inv = val["inv"]
    scaled_grads = inv * grads
    weighted_grad = exact_dims(scaled_grads, router_table(rc_ref), 1, 1)
    swap.wait_recv()
    dn[:, pl.ds(pl.multiple_of((1 - n) * HALF, 128), HALF)] = other[...].astype(f32)
    normed_grad = dn[...] + val["self"] * g
    inv_grad = total(normed_grad * weighted) + total(grads * raw)
    hidden_grad = (
        g
        + normed_grad * inv * gain
        + weighted_grad * gain
        - (inv_grad * (inv * inv * inv) / D) * hidden
    )
    hg_ref[...] = hidden_grad
    out_grad = hidden_grad.astype(bf16)
    og_ref[...] = out_grad
    for y in range(4):
        heads_ref[y] = dot_dims(wo_ref[y * 192 : (y + 1) * 192, :], out_grad, 1, 1).astype(bf16)
    send_heads()
    small_ref[...] = jnp.zeros_like(small_ref)
    small_ref[0:16, :D] = exact_dims(scaled_grads, weighted, 0, 0)
    small_ref[16:17, :D] = jnp.sum(val["vec0"] * g, axis=0, keepdims=True)
    small_ref[17:18, :D] = jnp.sum(val["vec1"] * g, axis=0, keepdims=True)
    small_ref[18:19, :D] = jnp.sum(normed_grad * hidden * inv + weighted_grad * hidden, axis=0, keepdims=True)
    small_ref[0:ROUTES, D : D + ROUTES] = exact_dims(prev_ref[:, own_tokens], logits_grad, 1, 0)
    gprev_ref[...] = jnp.zeros_like(gprev_ref)
    gprev_ref[0, 0:ROUTES, :] = exact_dims(res_ref[...].astype(f32), logits_grad, 1, 1)
    return swap


def attend_backward(middle, queries, pairs, attended, logs, block_ids, base, out_rows, weight_grads):
    small = shape_of((24, D + 128), f32)
    swaps_in = [(shape_of((1, 16, TOK), f32), 2), (base, 1)]
    extra = len(swaps_in)
    count = len(middle)
    route_shifts = shifts_of(ROUTE_AXES)
    peers = unique([shifts_of((a,)) for a in ("y", "x", "z", "c")] + [[{"n": 1}], route_shifts])
    turns = ("c", "x", "y", "z")
    order = (1, 3, 2, 0)

    def kernel(*refs):
        q_ref, of_ref, lse_ref, ids_ref, base_ref, kv_hbm, rows_in, dw_ref = refs[count : count + 8]
        hg_ref, og_ref, dq_out, dkv_out, rows_out, small_out, sum_out, sum_other = refs[count + 8 : count + 16]
        swapped = refs[count + 16 : count + 16 + extra]
        (
            heads_s, small_s, gprev_s, dn, row, sending, other, m_send, m_recv, kv_ref, kv_sem, rows_sem,
            g_now, g_pad, delta_s, dq_acc, dq_now, acc, to_sibling, from_sibling, to_other, from_other, kept, ready,
            small_now, small_in_flight, g_send, g_recv, c_send, c_recv, n_send, n_recv, y_send, y_recv,
            q_send, q_recv, r_send, r_recv, s_send, s_recv, p_send, p_recv, dw_own, dw_in, dw_on, own_sem, w_send, w_recv,
        ) = refs[count + 16 + extra :]
        place = coords()
        y, c, n = place["y"], place["c"], place["n"]
        part = 2 * c + n
        partner, sibling = moved(place, {"n": 1}), moved(place, {"c": 1})
        me = rank_of(place, ROUTE_AXES)
        ins = (gprev_s, base_ref)
        greet_start(place, peers)
        kv_load = pltpu.make_async_copy(kv_hbm, kv_ref, kv_sem)
        kv_load.start()
        grad_copies, row_copies = [], []

        def send_rows():
            for j, shift in enumerate(route_shifts):
                to = rank_of(place, ROUTE_AXES, shift)
                row_copies.append(
                    push(rows_in.at[to], rows_out.at[me], r_send.at[j], r_recv.at[j], moved(place, shift))
                )

        own_rows = pltpu.make_async_copy(rows_in.at[me], rows_out.at[me], rows_sem)
        own_rows.start()
        ways = (1, 3)
        two_on = lax.rem(y + 2, 4)
        weight_copies = []

        def send_weights():
            for i, d in enumerate(ways):
                weight_copies.append(
                    push(
                        dw_ref.at[i, two_on], dw_in.at[0, i], w_send.at[0, i], w_recv.at[0, i], moved(place, {"y": d})
                    )
                )

        loads = [
            pltpu.make_async_copy(dw_ref.at[i, lax.rem(y + d * k, 4)], dw_own.at[k, i], own_sem.at[k, i])
            for i, d in enumerate(ways)
            for k in range(2)
        ]
        for load in loads:
            load.start()
        def send_heads():
            for d in (2, 1, 3):
                target = lax.rem(y + d, 4)
                grad_copies.append(
                    push(heads_s.at[target], g_now.at[y], g_send.at[d], g_recv.at[d], moved(place, {"y": d}))
                )

        neighbour_swap = middle_backward(
            place, lambda: greet_end(peers), send_weights, send_heads, *refs[:count], hg_ref, og_ref, heads_s, small_s,
            gprev_s, dn, row, sending, other, m_send, m_recv,
        )
        g_now[y] = heads_s[y]
        small_now[0] = small_s[...]

        def small_start(turn):
            axis = turns[turn]
            return [
                push(
                    small_now.at[turn],
                    small_in_flight.at[turn, d],
                    s_send.at[turn, d],
                    s_recv.at[turn, d],
                    moved(place, {axis: d + 1}),
                )
                for d in range(SIZES[axis] - 1)
            ]

        def small_end(turn, copies):
            total = small_now[turn]
            for d, copy in enumerate(copies):
                copy.wait_recv()
                total = total + small_in_flight[turn, d]
            if turn < 3:
                small_now[turn + 1] = total
            else:
                small_out[...] = total

        small_copies = [small_start(0)]
        swaps = swap_start(place, swaps_in, ins, swapped, p_send, p_recv)
        dq_acc[...] = jnp.zeros_like(dq_acc)
        g_pad[...] = jnp.zeros_like(g_pad)
        for load in loads:
            load.wait()
        for i in range(2):
            weight_copies[i].wait_recv()
            dw_on[i] = (dw_own[1, i].astype(f32) + dw_in[0, i].astype(f32)).astype(bf16)
        kv_load.wait()
        for copy in grad_copies:
            copy.wait_recv()
        weight_copies += [
            push(dw_on.at[i], dw_in.at[2, i], w_send.at[2, i], w_recv.at[2, i], moved(place, {"y": d}))
            for i, d in enumerate(ways)
        ]
        weight_copies += [
            push(
                dw_ref.at[i, lax.rem(y + 4 - d, 4)], dw_in.at[1, i], w_send.at[1, i], w_recv.at[1, i],
                moved(place, {"y": 4 - d}),
            )
            for i, d in enumerate(ways)
        ]
        send_rows()
        own_rows.wait()
        for j in range(4):
            inner = g_now[j].astype(f32) * of_ref[j]
            for h in range(3):
                span = slice(h * HEAD_DIM, (h + 1) * HEAD_DIM)
                g_pad[j, h, HEAD_DIM:, :] = g_now[j, span, :]
                delta_s[j, h] = jnp.sum(inner[span, :], axis=0, keepdims=True)

        def update(j, block, tiles, masked):
            if masked:
                allowed = {t: to_column(key_ids(ids_ref, place, block, t)) <= query_ids(ids_ref, place, j) for t in tiles}
            places = [(t, h) for t in tiles for h in range(3)]
            k_tiles, scores, grads, both, dq = {}, {}, {}, {}, {}
            for t, h in places:
                k = kv_ref[block, t, :, :, h * 128 : (h + 1) * 128].reshape(KT, 128)
                k_tiles[t, h] = k
                scores[t, h] = dot_dims(k, q_ref[j, h], 1, 0)
                grads[t, h] = dot_dims(k, g_pad[j, h], 1, 0)
            for t, h in places:
                p = jnp.exp(scores[t, h] - lse_ref[j, h])
                if masked:
                    p = jnp.where(allowed[t], p, 0.0)
                ds = (p * (grads[t, h] - delta_s[j, h])).astype(bf16)
                both[t, h] = dot_dims(ds, q_ref[j, h], 1, 1) + dot_dims(p.astype(bf16), g_pad[j, h], 1, 1)
                more = dot_dims(k_tiles[t, h], ds, 0, 0)
                dq[h] = dq[h] + more if h in dq else more
            for t, h in places:
                acc[t, :, :, h * 128 : (h + 1) * 128] += both[t, h].reshape(2, TOK, 128)
            for h in range(3):
                dq_acc[j, h] += dq[h]

        beside, across, homeward = {}, {}, []

        def send_beside(d):
            to_sibling[d] = acc[1 - c].astype(bf16)
            beside[d] = push(to_sibling.at[d], from_sibling.at[d], c_send.at[d], c_recv.at[d], sibling)
            kept[d] = acc[c]

        def send_across(d):
            beside[d].wait_recv()
            to_other[d] = (kept[d, 1 - n] + from_sibling[d, 1 - n].astype(f32)).astype(bf16)
            across[d] = push(to_other.at[d], from_other.at[d], n_send.at[d], n_recv.at[d], partner)

        def send_home(d):
            across[d].wait_recv()
            total = kept[d, n] + from_sibling[d, n].astype(f32) + from_other[d].astype(f32)
            if d:
                ready[d] = total.astype(bf16)
                homeward.append(
                    push(ready.at[d], dkv_out.at[y], y_send.at[d], y_recv.at[d], moved(place, {"y": d}))
                )
            else:
                dkv_out[y] = total.astype(bf16)

        for step, d in enumerate(order):
            block = lax.rem(y + d, 4)
            acc[...] = jnp.zeros_like(acc)
            halves = for_chunks(
                block,
                part,
                lambda j, block=block: update(j, block, (0, 1), False),
                lambda j, t, block=block: update(j, block, (t,), True),
            )
            next(halves)
            if step:
                send_across(order[step - 1])
                small_end(step - 1, small_copies[step - 1])
                small_copies.append(small_start(step))
            if step > 1:
                send_home(order[step - 2])
            next(halves)
            send_beside(d)
        query_copies = []
        for d in (2, 1, 3, 0):
            j = lax.rem(y + d, 4)
            grad = jnp.concatenate([dq_acc[j, h, :HEAD_DIM, :] for h in range(3)], axis=0)
            grad = (grad * 0.125).astype(bf16)
            if d:
                dq_now[j] = grad
                query_copies.append(
                    push(dq_now.at[j], dq_out.at[y], q_send.at[d], q_recv.at[d], moved(place, {"y": d}))
                )
            else:
                dq_out[y] = grad
        send_home(order[2])
        send_across(order[3])
        small_end(3, small_copies[3])
        send_home(order[3])
        for copy in weight_copies[2:]:
            copy.wait_recv()
        totals = []
        for i in range(2):
            total = dw_own[0, i].astype(f32) + dw_in[1, i].astype(f32) + dw_in[2, i].astype(f32)
            totals.append(total.astype(bf16))
        sum_out[...] = jnp.where(n == 0, totals[0], totals[1])
        sum_other[...] = jnp.where(n == 0, totals[1], totals[0])
        for copy in homeward + query_copies + row_copies + swaps:
            copy.wait_recv()
        sent = grad_copies + row_copies + swaps + query_copies + homeward + weight_copies + [neighbour_swap]
        for copy in sent + list(beside.values()) + list(across.values()):
            copy.wait_send()
        for copies in small_copies:
            for copy in copies:
                copy.wait_send()

    four = pltpu.SemaphoreType.DMA((4,))
    return pl.pallas_call(
        kernel,
        out_shape=[
            shape_of((TOK, D), f32),
            shape_of((TOK, D), bf16),
            shape_of((4, 192, TOK), bf16),
            shape_of((4, TOK, HALF), bf16),
            shape_of(out_rows.shape, bf16),
            small,
            shape_of(weight_grads.shape[2:], bf16),
            shape_of(weight_grads.shape[2:], bf16),
        ]
        + swap_shapes(swaps_in),
        in_specs=in_vmem(count + 5) + [pl.BlockSpec(memory_space=pl.ANY)] * 3,
        out_specs=in_vmem(8 + extra),
        scratch_shapes=[
            pltpu.VMEM((4, 192, TOK), bf16),
            pltpu.VMEM(small.shape, f32),
            pltpu.VMEM((1, 16, TOK), f32),
            pltpu.VMEM((TOK, D), f32),
            pltpu.VMEM((1, EXPERTS * CAP), f32),
            pltpu.VMEM((TOK, HALF), bf16),
            pltpu.VMEM((TOK, HALF), bf16),
            pltpu.SemaphoreType.DMA,
            pltpu.SemaphoreType.DMA,
            pltpu.VMEM(pairs.shape, bf16),
            pltpu.SemaphoreType.DMA,
            pltpu.SemaphoreType.DMA,
            pltpu.VMEM((4, 192, TOK), bf16),
            pltpu.VMEM((4, 3, 128, TOK), bf16),
            pltpu.VMEM((4, 3, 1, TOK), f32),
            pltpu.VMEM((4, 3, 128, TOK), f32),
            pltpu.VMEM((4, 192, TOK), bf16),
            pltpu.VMEM((2, 2, TOK, HALF), f32),
            pltpu.VMEM((4, 2, TOK, HALF), bf16),
            pltpu.VMEM((4, 2, TOK, HALF), bf16),
            pltpu.VMEM((4, TOK, HALF), bf16),
            pltpu.VMEM((4, TOK, HALF), bf16),
            pltpu.VMEM((4, 2, TOK, HALF), f32),
            pltpu.VMEM((4, TOK, HALF), bf16),
            pltpu.VMEM((4,) + small.shape, f32),
            pltpu.VMEM((4, 3) + small.shape, f32),
        ]
        + [four] * 10
        + [pltpu.SemaphoreType.DMA((len(route_shifts),))] * 2
        + [pltpu.SemaphoreType.DMA((4, 3))] * 2
        + [pltpu.SemaphoreType.DMA((extra,))] * 2
        + [
            pltpu.VMEM((2, 2) + weight_grads.shape[2:], bf16),
            pltpu.VMEM((3, 2) + weight_grads.shape[2:], bf16),
            pltpu.VMEM((2,) + weight_grads.shape[2:], bf16),
            pltpu.SemaphoreType.DMA((2, 2)),
            pltpu.SemaphoreType.DMA((3, 2)),
            pltpu.SemaphoreType.DMA((3, 2)),
        ],
        compiler_params=comm_params(3),
        name="attend_backward",
    )(*middle, queries, attended, logs, block_ids, base, pairs, out_rows, weight_grads)


def project_backward(
    dq_ref, dkv_ref, pq_ref, proj_ref, inv_ref, scaled_ref, wq_ref, x_ref, vec_ref, hg_ref, at_ref, og_ref,
    pa, pb, pc, grad_ref, gain_ref, dw_s, dwo_s,
):
    inv = inv_ref[...]
    scaled = scaled_ref[...]
    dscaled = jnp.zeros((TOK, D), f32)
    dinv = jnp.zeros((TOK, 192), f32)
    dinv_row = jnp.zeros((1, TOK), f32)
    inv_row = to_row(inv)
    for s in range(3):
        for y in range(4):
            first = s * D + y * 192
            if s == 0:
                d = dq_ref[y].astype(f32)
                dinv_row = dinv_row + jnp.sum(d * pq_ref[y], axis=0, keepdims=True)
                dproject = (inv_row * d).astype(bf16)
                dscaled = dscaled + dot_dims(dproject, wq_ref[first : first + 192, :], 0, 0)
                dw_s[first : first + 192, :] = dot_dims(dproject, scaled, 1, 0)
                continue
            d = jnp.concatenate(
                [
                    dkv_ref[y, :, h * 128 + (s - 1) * HEAD_DIM : h * 128 + s * HEAD_DIM]
                    for h in range(3)
                ],
                axis=1,
            ).astype(f32)
            dinv = dinv + d * proj_ref[(s - 1) * 4 + y]
            dproject = (inv * d).astype(bf16)
            dscaled = dscaled + dot_dims(dproject, wq_ref[first : first + 192, :], 1, 0)
            dw_s[first : first + 192, :] = dot_dims(dproject, scaled, 0, 0)
    for y in range(4):
        dwo_s[y * 192 : (y + 1) * 192, :] = dot_dims(at_ref[y], og_ref[...], 1, 0)
    for w, cols, spots in blocks_of_weights():
        pa[spots[0]] = dw_s[w * 36 : w * 36 + 16, cols].astype(bf16)
        pb[spots[1]] = dw_s[w * 36 + 16 : w * 36 + 32, cols].astype(bf16)
        pc[spots[2]] = jnp.concatenate(
            [dw_s[w * 36 + 32 : w * 36 + 36, cols], dwo_s[w * 12 : w * 12 + 12, cols]], axis=0
        ).astype(bf16)
    x = jnp.concatenate([x_ref[0], x_ref[1]], axis=1).astype(f32)
    gain = jnp.concatenate([vec_ref[0, 0:1], vec_ref[1, 0:1]], axis=1).astype(f32)
    gain_ref[0] = jnp.zeros_like(gain_ref[0])
    gain_ref[0, 0:1, :] = jnp.sum(dscaled * x, axis=0, keepdims=True)
    dinv = jnp.sum(dinv, axis=1, keepdims=True) + to_column(dinv_row)
    grad = hg_ref[...] + dscaled * gain - (dinv * (inv * inv * inv) / D) * x
    for half in range(2):
        grad_ref[half] = grad[:, half * HALF : (half + 1) * HALF].astype(bf16)


def scatter_sums(given, weight_sum):
    swaps_in = [(shape_of((2, TOK, HALF), bf16), 1)]
    small = shape_of((8, D), f32)
    extra = len(swaps_in)
    peers = unique([shifts_of((a,)) for a in ("x", "y", "z", "c")])
    turns = ("c", "x", "y", "z")
    count = len(given)
    from_hbm = (2, 3, 6)

    def kernel(*refs):
        weight_ref = refs[count]
        block_out, small_out, weight_out = refs[count + 1 : count + 4]
        swapped = refs[count + 4 : count + 4 + extra]
        rest = refs[count + 4 + extra :]
        parts_in, grad_s, dw_s, dwo_s = rest[:3], rest[3], rest[4], rest[5]
        rest = rest[6:]
        from_sibling, sum_three, sum_two, sum_one = rest[0:3], rest[3:6], rest[6:9], rest[9:12]
        in_three, in_two, in_one = rest[12:15], rest[15:18], rest[18:21]
        (
            small_now,
            small_in_flight,
            c_send,
            c_recv,
            send,
            recv,
            s_send,
            s_recv,
            p_send,
            p_recv,
            w_send,
            w_recv,
            load_sem,
            *held,
        ) = rest[21:]
        place = coords()
        core = place["c"]
        ins = (grad_s,)
        greet_start(place, peers)
        loads = [
            pltpu.make_async_copy(refs[at], held[i], load_sem.at[i]) for i, at in enumerate(from_hbm)
        ]
        for load in loads:
            load.start()
        arrays = list(refs[:count])
        for i, at in enumerate(from_hbm):
            arrays[at] = held[i]
        greet_end(peers)
        for load in loads:
            load.wait()
        weight_copy = push(weight_ref, weight_out, w_send, w_recv, moved(place, {"z": 2}))
        project_backward(*arrays, *parts_in, grad_s, small_now, dw_s, dwo_s)
        beside = []
        for j in range(4):
            for k in range(3):
                third = lax.rem(place[ORDERS[k][2]] + (j + 1), 4)
                beside.append(
                    push(
                        parts_in[k].at[1 - core, third],
                        from_sibling[k].at[third],
                        c_send.at[k, j],
                        c_recv.at[k, j],
                        moved(place, {"c": 1}),
                    )
                )

        def small_start(turn):
            axis = turns[turn]
            return [
                push(
                    small_now.at[turn],
                    small_in_flight.at[turn, d],
                    s_send.at[turn, d],
                    s_recv.at[turn, d],
                    moved(place, {axis: d + 1}),
                )
                for d in range(SIZES[axis] - 1)
            ]

        def small_end(turn, copies):
            total = small_now[turn]
            for d, copy in enumerate(copies):
                copy.wait_recv()
                total = total + small_in_flight[turn, d]
            if turn < 3:
                small_now[turn + 1] = total
            else:
                small_out[...] = total

        small_copies = [small_start(0)]
        threes = [[] for _ in range(3)]
        for j in range(4):
            for k in range(3):
                third = lax.rem(place[ORDERS[k][2]] + (j + 1), 4)
                beside[j * 3 + k].wait_recv()
                sum_three[k][third] = (
                    parts_in[k][core, third].astype(f32) + from_sibling[k][third].astype(f32)
                ).astype(bf16)
                if j < 3:
                    threes[k].append(
                        push(
                            sum_three[k].at[third],
                            in_three[k].at[j],
                            send.at[k, 0, j],
                            recv.at[k, 0, j],
                            moved(place, {ORDERS[k][2]: j + 1}),
                        )
                    )
        swaps = swap_start(place, swaps_in, ins, swapped, p_send, p_recv)
        small_end(0, small_copies[0])
        small_copies.append(small_start(1))
        twos = [[] for _ in range(3)]
        for k in range(3):
            for copy in threes[k]:
                copy.wait_recv()
            third = place[ORDERS[k][2]]
            total = sum_three[k][third].astype(f32)
            for j in range(3):
                total = total + in_three[k][j].astype(f32)
            sum_two[k][...] = total.astype(bf16)
            for j in range(3):
                second = lax.rem(place[ORDERS[k][1]] + (j + 1), 4)
                twos[k].append(
                    push(
                        sum_two[k].at[second],
                        in_two[k].at[j],
                        send.at[k, 1, j],
                        recv.at[k, 1, j],
                        moved(place, {ORDERS[k][1]: j + 1}),
                    )
                )
        small_end(1, small_copies[1])
        small_copies.append(small_start(2))
        ones = [[] for _ in range(3)]
        for k in range(3):
            for copy in twos[k]:
                copy.wait_recv()
            second = place[ORDERS[k][1]]
            total = sum_two[k][second].astype(f32)
            for j in range(3):
                total = total + in_two[k][j].astype(f32)
            sum_one[k][...] = total.astype(bf16)
            for j in range(3):
                first = lax.rem(place[ORDERS[k][0]] + (j + 1), 4)
                ones[k].append(
                    push(
                        sum_one[k].at[first],
                        in_one[k].at[j],
                        send.at[k, 2, j],
                        recv.at[k, 2, j],
                        moved(place, {ORDERS[k][0]: j + 1}),
                    )
                )
        small_end(2, small_copies[2])
        small_copies.append(small_start(3))
        for k in range(3):
            for copy in ones[k]:
                copy.wait_recv()
            first = place[ORDERS[k][0]]
            total = sum_one[k][first].astype(f32)
            for j in range(3):
                total = total + in_one[k][j].astype(f32)
            block_out[k * PART : (k + 1) * PART, :] = total
        small_end(3, small_copies[3])
        for copy in swaps + [weight_copy]:
            copy.wait_recv()
        for copy in beside + swaps + [weight_copy]:
            copy.wait_send()
        for k in range(3):
            for copy in threes[k] + twos[k] + ones[k]:
                copy.wait_send()
        for copies in small_copies:
            for copy in copies:
                copy.wait_send()

    three = pltpu.VMEM((4, 4, 4, PART, HALF), bf16)
    two = pltpu.VMEM((4, 4, PART, HALF), bf16)
    one = pltpu.VMEM((4, PART, HALF), bf16)
    return pl.pallas_call(
        kernel,
        out_shape=[shape_of((3 * PART, HALF), f32), small, shape_of(weight_sum.shape, bf16)] + swap_shapes(swaps_in),
        in_specs=[pl.BlockSpec(memory_space=pl.ANY if i in from_hbm else pltpu.VMEM) for i in range(count + 1)],
        out_specs=in_vmem(3 + extra),
        scratch_shapes=[pltpu.VMEM((2, 4, 4, 4, PART, HALF), bf16)] * 3
        + [pltpu.VMEM((2, TOK, HALF), bf16), pltpu.VMEM((3 * D, D), f32), pltpu.VMEM((D, D), f32)]
        + [three] * 3
        + [three] * 3
        + [two] * 3
        + [one] * 3
        + [pltpu.VMEM((3, 4, 4, PART, HALF), bf16)] * 3
        + [pltpu.VMEM((3, 4, PART, HALF), bf16)] * 3
        + [pltpu.VMEM((3, PART, HALF), bf16)] * 3
        + [
            pltpu.VMEM((4,) + small.shape, f32),
            pltpu.VMEM((4, 3) + small.shape, f32),
            pltpu.SemaphoreType.DMA((3, 4)),
            pltpu.SemaphoreType.DMA((3, 4)),
            pltpu.SemaphoreType.DMA((3, 3, 3)),
            pltpu.SemaphoreType.DMA((3, 3, 3)),
            pltpu.SemaphoreType.DMA((4, 3)),
            pltpu.SemaphoreType.DMA((4, 3)),
            pltpu.SemaphoreType.DMA((extra,)),
            pltpu.SemaphoreType.DMA((extra,)),
            pltpu.SemaphoreType.DMA,
            pltpu.SemaphoreType.DMA,
            pltpu.SemaphoreType.DMA((len(from_hbm),)),
        ]
        + [pltpu.VMEM(given[at].shape, given[at].dtype) for at in from_hbm],
        compiler_params=comm_params(4),
        name="scatter_sums",
    )(*given, weight_sum)


def finish(grad_block, gain_sum, grad_halves, small, grad_prev, expert_sum, expert_other, base, out_slots, hit):
    def kernel(
        block_ref, gain_ref, halves_ref, small_ref, prev_ref, expert_ref, other_ref, base_ref, slots_ref, hit_ref,
        layer_out, g_inputs, g_prev, g_gain_one, g_qkv, g_out, g_gain_two, g_router, g_residual, g_const, g_vec,
        g_gate, g_up, g_down,
    ):
        n = lax.axis_index("n")
        cols = pl.ds(pl.multiple_of(n * HALF, 128), HALF)
        mixture = dot_dims(hit_ref[...], slots_ref[...].reshape(EXPERTS * CAP, HALF), 0, 0)
        for side in range(2):
            span = slice(side * TOK, (side + 1) * TOK)
            layer_out[span, :] = (base_ref[side].astype(f32) + mixture[span, :]).astype(bf16)
            g_inputs[span, :] = halves_ref[side].astype(f32)
            g_prev[:, span] = prev_ref[side, :ROUTES, :]
        g_gain_one[...] = gain_ref[0:1, cols].reshape(HALF)
        block = block_ref[...]
        g_qkv[...] = block[:36, :]
        g_out[...] = block[36:48, :]
        g_router[...] = small_ref[:ROUTES, cols]
        g_const[...] = small_ref[ROUTES:16, cols]
        g_vec[...] = small_ref[16:18, cols]
        g_gain_two[...] = small_ref[18:19, cols].reshape(HALF)
        g_residual[...] = small_ref[0:ROUTES, D : D + ROUTES]
        for i, target in enumerate((g_gate, g_up, g_down)):
            total = expert_ref[i].astype(f32) + other_ref[i].astype(f32)
            target[...] = total if i < 2 else total.T

    shapes = [
        shape_of((2 * TOK, HALF), bf16),
        shape_of((2 * TOK, HALF), f32),
        shape_of((ROUTES, 2 * TOK), f32),
        shape_of((HALF,), f32),
        shape_of((36, HALF), f32),
        shape_of((12, HALF), f32),
        shape_of((HALF,), f32),
        shape_of((ROUTES, HALF), f32),
        shape_of((ROUTES, ROUTES), f32),
        shape_of((4, HALF), f32),
        shape_of((2, HALF), f32),
        shape_of((HALF, 256), f32),
        shape_of((HALF, 256), f32),
        shape_of((256, HALF), f32),
    ]
    return pl.pallas_call(
        kernel,
        out_shape=shapes,
        in_specs=in_vmem(10),
        out_specs=in_vmem(len(shapes)),
        compiler_params=pltpu.CompilerParams(vmem_limit_bytes=VMEM_LIMIT),
        name="finish",
    )(grad_block, gain_sum, grad_halves, small, grad_prev, expert_sum, expert_other, base, out_slots, hit)


def shards(
    inputs,
    block_ids,
    expert_ids,
    prev_scores,
    gain_one,
    w_qkv,
    w_out,
    gain_two,
    w_router,
    w_residual,
    w_const,
    const_vec,
    w_gate,
    w_up,
    w_down,
    cotangent,
):
    blocks = block_ids.reshape(64, 1, 512)
    prev = prev_scores.T
    (
        x_halves, g_halves, vectors, routers, hit, plan, wo, scaled, inv_one, attended, queries, attended_f, logs,
        grad_rows, wq, project_q, project, pairs, weights,
    ) = front(
        w_qkv.T,
        w_out,
        inputs.reshape(2, TOK, HALF),
        cotangent.reshape(2, TOK, HALF),
        [gain_one, gain_two, const_vec],
        [w_router.T, w_const.T],
        expert_ids.T,
        blocks,
        [w_gate, w_up, w_down],
    )
    hidden, normed, base, table, out_rows, slot_grads, dots, expert_grads = experts_step(
        attended, x_halves, wo, vectors, routers, prev, w_residual, plan, hit, grad_rows, weights
    )
    hidden_grad, out_grad, dq, dkv, out_slots, small, expert_sum, expert_other, grad_prev, base = attend_backward(
        [
            slot_grads, hit, g_halves, hidden, normed, table, vectors, routers, dots, plan, prev, w_residual, wo,
        ],
        queries, pairs, attended_f, logs, blocks, base, out_rows, expert_grads,
    )
    grad_block, gain_sum, expert_other, grad_halves = scatter_sums(
        [
            dq, dkv, project_q, project, inv_one, scaled, wq, x_halves, vectors, hidden_grad, attended, out_grad,
        ],
        expert_other,
    )
    outputs = finish(
        grad_block, gain_sum, grad_halves, small, grad_prev, expert_sum, expert_other, base, out_slots, hit
    )
    turned = {2, 4, 7, 9}
    return tuple(out.T if i in turned else out for i, out in enumerate(outputs))


def solution(mesh):
    fine = Mesh(mesh.devices.reshape(2, 2, 4, 4, 2), AXES)
    return jax.shard_map(
        shards,
        mesh=fine,
        in_specs=(
            P(WIDE, "n"),
            P(),
            P(WIDE, None),
            P(WIDE, None),
            P("n"),
            P("n", WIDE),
            P(WIDE, "n"),
            P("n"),
            P("n", None),
            P(),
            P("n", None),
            P(None, "n"),
            P("n", WIDE),
            P("n", WIDE),
            P(WIDE, "n"),
            P(WIDE, "n"),
        ),
        out_specs=(
            P(WIDE, "n"),
            P(WIDE, "n"),
            P(WIDE, None),
            P("n"),
            P("n", WIDE),
            P(WIDE, "n"),
            P("n"),
            P("n", None),
            P(),
            P("n", None),
            P(None, "n"),
            P("n", WIDE),
            P("n", WIDE),
            P(WIDE, "n"),
        ),
        check_vma=False,
    )
```
